256 devices in a mesh: grp: 16 (over z_hi, x), seq: 16 (over y, z_lo, core).
Axes of the slice: x: 4, y: 4, z: 8 (z_hi: 4, z_lo: 2; z = z_hi * 2 + z_lo), core: 2. Of those that a mesh axis runs over, the one named last changes fastest.
Arguments:
- t5_context: bfloat16 [16, 512, 4096], P('grp', None, 'seq'), may hold values from -6 to 6
- t5_resid: bfloat16 [16, 512, 4096], P('grp', 'seq'), may hold values from -6 to 6
- t5_out_weight: bfloat16 [4096, 4096], P('seq'), may hold values from -0.09375 to 0.09375
- t5_gain: float32 [4096], replicated, may hold values from 0.1 to 1.9
- text_weight: bfloat16 [4096, 6144], P(None, 'seq'), may hold values from -0.09375 to 0.09375
- prompt_len: int32 [16], P('grp'), may hold values from 1 to 512
- text_order: int32 [16, 32], P('grp'), may hold values from 0 to 31, each once within a row
- img_qkv: bfloat16 [16, 2048, 6144], P('grp', 'seq'), may hold values from -8 to 8
- d_img_out: bfloat16 [16, 2048, 2048], P('grp', 'seq'), may hold values from -6 to 6
- d_txt_out: bfloat16 [16, 512, 2048], P('grp', 'seq'), may hold values from -6 to 6
Outputs:
- img_attn_out: bfloat16 [16, 2048, 2048], P('grp', 'seq')
- text_attn_out: bfloat16 [16, 512, 2048], P('grp', 'seq')
- image_qkv_grad: bfloat16 [16, 2048, 6144], P('grp', 'seq')
- text_weight_grad: float32 [4096, 6144], P('grp', 'seq')
The draws below stay inside these ranges and needn't reach their ends.
Inputs may be any that keep to these rules, and one draw needn't show every extreme that they name: `text_order`: each row holds every block slot 0 to 31 once.
All inputs are finite; a program needn't handle non-finite values.
Results may differ from the reference program's by a relative error of at most 0.02.
Values may be sent and summed in bfloat16 or wider, within the bound.
No kernel may reach another device: no remote copies, remote signals or barrier semaphores. Data moves between devices by JAX's collectives and lax.ppermute only.
A program may use at most 128 MiB of HBM per device.

```python
import jax
import jax.numpy as jnp
from jax import lax

T5_WIDTH = 4096
HEADS = 16
HEAD_DIM = 128
PROMPT = 512
BLOCK_ROWS = 16
REPLICAS = 16
IMAGE_TOKENS = 2048
TEXT_BLOCKS = 32
JOINT_TOKENS = 2560


def draw_img_qkv(key, part):
    key = jax.random.fold_in(key, 7)
    shape = (REPLICAS, IMAGE_TOKENS, HEADS, 3, HEAD_DIM)
    values = jnp.clip(jax.random.normal(key, shape, jnp.float32), -6.0, 6.0)
    return values.reshape(REPLICAS, IMAGE_TOKENS, HEADS * 3 * HEAD_DIM).astype(jnp.bfloat16)


def touch_ends(entries, rng, smallest, high):
    dims = entries.shape
    index_at = [jax.random.randint(jax.random.fold_in(rng, axis), (), 0, dims[axis]) for axis in range(len(dims))]
    entries = entries.at[tuple(index_at)].set(smallest)
    longest = dims.index(max(dims))
    index_at[longest] = (index_at[longest] + 1) % dims[longest]
    return entries.at[tuple(index_at)].set(high)


def shard_levels(own_key, dims, split, low, top_value):
    level = 1.0
    for axis_at, parts in split:
        steps = jax.random.uniform(jax.random.fold_in(jax.random.fold_in(own_key, 6), axis_at), (parts,), jnp.float32, low / len(split), top_value / len(split))
        level = level * jnp.repeat(jnp.exp(steps), dims[axis_at] // parts).reshape((-1,) + (1,) * (len(dims) - 1 - axis_at))
    return level


def noise(rng, dims, scale, most, cuts=(), kind=jnp.bfloat16):
    drawn = scale * jax.random.normal(rng, dims, jnp.float32)
    if cuts:
        drawn = drawn * shard_levels(rng, dims, cuts, -0.22, 0.18)
    return jnp.clip(drawn, -most, most).astype(kind)


def setup_inputs(seed: int = 0) -> dict:
    seeds = jax.random.split(jax.random.key(seed), 11)
    return {
        "t5_context": noise(seeds[0], (REPLICAS, PROMPT, T5_WIDTH), 1.0, 6.0, ((0, 16), (2, 16))),
        "t5_resid": noise(seeds[1], (REPLICAS, PROMPT, T5_WIDTH), 1.0, 6.0, ((0, 16), (1, 16))),
        "t5_out_weight": noise(seeds[2], (T5_WIDTH, T5_WIDTH), T5_WIDTH ** -0.5, 0.09375, ((0, 16),)),
        "t5_gain": jnp.clip(1.0 + 0.18 * jax.random.normal(seeds[3], (T5_WIDTH,), jnp.float32), 0.1, 1.9),
        "text_weight": noise(seeds[4], (T5_WIDTH, HEADS * 3 * HEAD_DIM), T5_WIDTH ** -0.5, 0.09375, ((1, 16),)),
        "prompt_len": touch_ends(jax.random.randint(seeds[5], (REPLICAS,), 1, PROMPT + 1), jax.random.fold_in(seeds[5], 1), 1, PROMPT).astype(jnp.int32),
        "text_order": jax.vmap(lambda own: jax.random.permutation(own, TEXT_BLOCKS))(jax.random.split(seeds[6], REPLICAS)).reshape((REPLICAS, TEXT_BLOCKS)).astype(jnp.int32),
        "img_qkv": draw_img_qkv(jax.random.fold_in(seeds[10], 71), 0),
        "d_img_out": noise(seeds[8], (REPLICAS, IMAGE_TOKENS, HEADS * HEAD_DIM), 1.0, 6.0, ((0, 16), (1, 16))),
        "d_txt_out": noise(seeds[9], (REPLICAS, PROMPT, HEADS * HEAD_DIM), 1.0, 6.0, ((0, 16), (1, 16))),
    }


def encode(context, residual, out_weight, gain):
    mixed_sum = jnp.dot(context, out_weight, preferred_element_type=jnp.float32)
    stream = residual.astype(jnp.float32) + mixed_sum
    inv_norm = lax.rsqrt(lax.optimization_barrier(jnp.mean(stream * stream, axis=-1, keepdims=True)) + 1e-06)
    return (stream * inv_norm * gain).astype(jnp.bfloat16)

def head_pass(queries, key_rows, values, out_grad, key_valid):
    factor = HEAD_DIM ** (-0.5)
    scores = jnp.dot(queries, key_rows.T, preferred_element_type=jnp.float32) * factor
    scores = jnp.where(key_valid[None, :], scores, -1e+30)
    maximum = lax.optimization_barrier(jnp.max(scores, axis=-1, keepdims=True))
    weights = jnp.exp(scores - maximum)
    probability = (weights / lax.optimization_barrier(jnp.sum(weights, axis=-1, keepdims=True))).astype(jnp.bfloat16)
    output = jnp.dot(probability, values, preferred_element_type=jnp.float32)
    row_delta = lax.optimization_barrier(jnp.sum(out_grad.astype(jnp.float32) * output, axis=-1, keepdims=True))
    prob_grad = jnp.dot(out_grad, values.T, preferred_element_type=jnp.float32)
    score_grad = (probability.astype(jnp.float32) * (prob_grad - row_delta) * factor).astype(jnp.bfloat16)
    query_grad = jnp.dot(score_grad, key_rows, preferred_element_type=jnp.float32)
    key_grad = jnp.dot(score_grad.T, queries, preferred_element_type=jnp.float32)
    value_grad = jnp.dot(probability.T, out_grad, preferred_element_type=jnp.float32)
    return (output.astype(jnp.bfloat16), jnp.stack([query_grad, key_grad, value_grad], 1).astype(jnp.bfloat16))

def reference(t5_context, t5_resid, t5_out_weight, t5_gain, text_weight, prompt_len, text_order, img_qkv, d_img_out, d_txt_out):
    positions = jnp.arange(JOINT_TOKENS, dtype=jnp.int32)

    def replica(running, inputs):
        context, residual, length, slot_order, image_rows, image_grad, text_slots = inputs
        encoded = encode(context, residual, t5_out_weight, t5_gain)
        text_rows = jnp.dot(encoded, text_weight, preferred_element_type=jnp.float32).astype(jnp.bfloat16)
        text_grad = jnp.take(text_slots.reshape(TEXT_BLOCKS, BLOCK_ROWS, -1), slot_order, axis=0).reshape(PROMPT, -1)
        joint_rows = jnp.concatenate([text_rows, image_rows], 0).reshape(JOINT_TOKENS, HEADS, 3, HEAD_DIM)
        joint_out_grad = jnp.concatenate([text_grad, image_grad], 0).reshape(JOINT_TOKENS, HEADS, HEAD_DIM)
        key_valid = (positions < length) | (positions >= PROMPT)

        def one_head(pieces):
            head_rows, head_grad = pieces
            return head_pass(head_rows[:, 0], head_rows[:, 1], head_rows[:, 2], head_grad, key_valid)
        outputs, gradients = lax.map(one_head, (jnp.moveaxis(joint_rows, 1, 0), jnp.moveaxis(joint_out_grad, 1, 0)))
        outputs = jnp.moveaxis(outputs, 0, 1).reshape(JOINT_TOKENS, HEADS * HEAD_DIM)
        gradients = jnp.moveaxis(gradients, 0, 1).reshape(JOINT_TOKENS, HEADS * 3 * HEAD_DIM)
        text_blocks = outputs[:PROMPT].reshape(TEXT_BLOCKS, BLOCK_ROWS, HEADS * HEAD_DIM)
        text_out = jnp.zeros_like(text_blocks).at[slot_order].set(text_blocks).reshape(PROMPT, HEADS * HEAD_DIM)
        weight_part = lax.dot_general(encoded, gradients[:PROMPT], (((0,), (0,)), ((), ())), preferred_element_type=jnp.float32)
        return (running + weight_part, (outputs[PROMPT:], text_out, gradients[PROMPT:]))
    start_total = jnp.zeros((T5_WIDTH, HEADS * 3 * HEAD_DIM), jnp.float32)
    weight_total, results = lax.scan(replica, start_total, (t5_context, t5_resid, prompt_len, text_order, img_qkv, d_img_out, d_txt_out))
    img_attn_out, text_attn_out, image_qkv_grad = results
    return (img_attn_out, text_attn_out, image_qkv_grad, weight_total)
```

```python
import jax
import jax.numpy as jnp
from jax import lax
from jax.experimental import pallas as pl
from jax.experimental.pallas import tpu as pltpu
from jax.sharding import Mesh
from jax.sharding import PartitionSpec as P

HEAD_DIM = 128
HEADS = 16
PROMPT = 512
IMAGE = 2048
TOTAL = PROMPT + IMAGE
BLOCK_ROWS = 16
TEXT_BLOCKS = 32
SHARE = IMAGE // HEADS
PACK_ROWS = SHARE + BLOCK_ROWS
PACK_COLS = 4 * HEAD_DIM
QUERY_BLOCK = 256
LOG2_E = 1.4426950408889634

BF16 = jnp.bfloat16
F32 = jnp.float32
SEQ = ("y", "z_lo", "core")
GRP = ("z_hi", "x")
CONTRACT_LAST = (((1,), (1,)), ((), ()))
CONTRACT_FIRST = (((0,), (0,)), ((), ()))
VMEM_LIMIT = 48 * 2**20


def matmul(a, b, dims=(((1,), (0,)), ((), ()))):
    return lax.dot_general(a, b, dims, preferred_element_type=F32)


def pack_kernel(qkv_ref, grad_ref, text_ref, packed_ref):
    packed_ref[0, :SHARE, : 3 * HEAD_DIM] = qkv_ref[...]
    packed_ref[0, :SHARE, 3 * HEAD_DIM :] = grad_ref[...]
    packed_ref[0, SHARE:, :HEAD_DIM] = text_ref[:BLOCK_ROWS, :]
    packed_ref[0, SHARE:, HEAD_DIM : 2 * HEAD_DIM] = text_ref[BLOCK_ROWS:, :]
    packed_ref[0, SHARE:, 2 * HEAD_DIM :] = jnp.zeros((BLOCK_ROWS, 2 * HEAD_DIM), BF16)


def pack(qkv, grad, text):
    return pl.pallas_call(
        pack_kernel,
        grid=(HEADS,),
        out_shape=jax.ShapeDtypeStruct((HEADS, PACK_ROWS, PACK_COLS), BF16),
        in_specs=[
            pl.BlockSpec((SHARE, 3 * HEAD_DIM), lambda h: (0, h)),
            pl.BlockSpec((SHARE, HEAD_DIM), lambda h: (0, h)),
            pl.BlockSpec((2 * BLOCK_ROWS, HEAD_DIM), lambda h: (0, h)),
        ],
        out_specs=pl.BlockSpec((1, PACK_ROWS, PACK_COLS), lambda h: (h, 0, 0)),
    )(qkv, grad, text)


def unpack_kernel(packed_ref, out_ref, text_ref, qkv_ref):
    out_ref[...] = packed_ref[0, :SHARE, :HEAD_DIM]
    qkv_ref[...] = packed_ref[0, :SHARE, HEAD_DIM:]
    text_ref[:BLOCK_ROWS, :] = packed_ref[0, SHARE:, :HEAD_DIM]
    text_ref[BLOCK_ROWS:, :] = packed_ref[0, SHARE:, HEAD_DIM : 2 * HEAD_DIM]


def unpack(packed):
    return pl.pallas_call(
        unpack_kernel,
        grid=(HEADS,),
        out_shape=[
            jax.ShapeDtypeStruct((SHARE, HEADS * HEAD_DIM), BF16),
            jax.ShapeDtypeStruct((2 * BLOCK_ROWS, HEADS * HEAD_DIM), BF16),
            jax.ShapeDtypeStruct((SHARE, HEADS * 3 * HEAD_DIM), BF16),
        ],
        in_specs=[pl.BlockSpec((1, PACK_ROWS, PACK_COLS), lambda h: (h, 0, 0))],
        out_specs=[
            pl.BlockSpec((SHARE, HEAD_DIM), lambda h: (0, h)),
            pl.BlockSpec((2 * BLOCK_ROWS, HEAD_DIM), lambda h: (0, h)),
            pl.BlockSpec((SHARE, 3 * HEAD_DIM), lambda h: (0, h)),
        ],
    )(packed)


def attention_kernel(
    length_ref,
    order_ref,
    text_ref,
    packed_ref,
    sent_ref,
    text_grad_ref,
    q_ref,
    k_ref,
    v_ref,
    do_ref,
    out_ref,
    dq_ref,
    dkt_ref,
    dvt_ref,
):
    length = length_ref[0]
    factor = HEAD_DIM**-0.5
    for role, rows in enumerate((q_ref, k_ref, v_ref)):
        columns = slice(role * HEAD_DIM, (role + 1) * HEAD_DIM)
        rows[:PROMPT, :] = text_ref[:, columns]
        for src in range(HEADS):
            at = PROMPT + src * SHARE
            rows[at : at + SHARE, :] = packed_ref[src, :SHARE, columns]
    for src in range(HEADS):
        at = PROMPT + src * SHARE
        do_ref[at : at + SHARE, :] = packed_ref[src, :SHARE, 3 * HEAD_DIM :]
    for block in range(TEXT_BLOCKS):
        slot = order_ref[block]
        columns = pl.ds(pl.multiple_of((slot % 2) * HEAD_DIM, HEAD_DIM), HEAD_DIM)
        do_ref[block * BLOCK_ROWS : (block + 1) * BLOCK_ROWS, :] = packed_ref[
            slot // 2, SHARE:, columns
        ]
    dkt_ref[...] = jnp.zeros_like(dkt_ref)
    dvt_ref[...] = jnp.zeros_like(dvt_ref)

    def body(step, carry):
        rows = pl.ds(pl.multiple_of(step * QUERY_BLOCK, QUERY_BLOCK), QUERY_BLOCK)
        queries = q_ref[rows, :]
        keys = k_ref[...]
        values = v_ref[...]
        scores = matmul(queries, keys, CONTRACT_LAST)
        position = lax.broadcasted_iota(jnp.int32, (1, TOTAL), 1)
        scores = jnp.where((position < length) | (position >= PROMPT), scores, -1e30)
        maximum = jnp.max(scores, axis=-1, keepdims=True)
        weights = jnp.exp2((scores - maximum) * (factor * LOG2_E)).astype(BF16)
        wide = weights.astype(F32)
        inverse = 1.0 / jnp.sum(wide, axis=-1, keepdims=True)
        output = matmul(weights, values) * inverse
        out_grad = (do_ref[rows, :].astype(F32) * inverse).astype(BF16)
        row_delta = jnp.sum(out_grad.astype(F32) * output, axis=-1, keepdims=True)
        prob_grad = matmul(out_grad, values, CONTRACT_LAST)
        score_grad = (wide * (prob_grad - row_delta)).astype(BF16)
        out_ref[rows, :] = output.astype(BF16)
        dq_ref[rows, :] = (matmul(score_grad, keys) * factor).astype(BF16)
        dkt_ref[...] += matmul(queries, score_grad, CONTRACT_FIRST)
        dvt_ref[...] += matmul(out_grad, weights, CONTRACT_FIRST)
        return carry

    lax.fori_loop(0, TOTAL // QUERY_BLOCK, body, 0)
    q_ref[...] = (dkt_ref[...] * factor).T.astype(BF16)
    k_ref[...] = dvt_ref[...].T.astype(BF16)
    for place, rows in enumerate((out_ref, dq_ref, q_ref, k_ref)):
        columns = slice(place * HEAD_DIM, (place + 1) * HEAD_DIM)
        for dest in range(HEADS):
            at = PROMPT + dest * SHARE
            sent_ref[dest, :SHARE, columns] = rows[at : at + SHARE, :]
        if place:
            text_grad_ref[:, (place - 1) * HEAD_DIM : place * HEAD_DIM] = rows[:PROMPT, :]
    sent_ref[:, SHARE:, 2 * HEAD_DIM :] = jnp.zeros((HEADS, BLOCK_ROWS, 2 * HEAD_DIM), BF16)
    for block in range(TEXT_BLOCKS):
        slot = order_ref[block]
        columns = pl.ds(pl.multiple_of((slot % 2) * HEAD_DIM, HEAD_DIM), HEAD_DIM)
        sent_ref[slot // 2, SHARE:, columns] = out_ref[
            block * BLOCK_ROWS : (block + 1) * BLOCK_ROWS, :
        ]


def attention(length, order, text_rows, packed):
    in_vmem = pl.BlockSpec(memory_space=pltpu.VMEM)
    in_smem = pl.BlockSpec(memory_space=pltpu.SMEM)
    rows = pltpu.VMEM((TOTAL, HEAD_DIM), BF16)
    total = pltpu.VMEM((HEAD_DIM, TOTAL), F32)
    return pl.pallas_call(
        attention_kernel,
        out_shape=[
            jax.ShapeDtypeStruct((HEADS, PACK_ROWS, PACK_COLS), BF16),
            jax.ShapeDtypeStruct((PROMPT, 3 * HEAD_DIM), BF16),
        ],
        in_specs=[in_smem, in_smem, in_vmem, in_vmem],
        out_specs=[in_vmem, in_vmem],
        scratch_shapes=[rows] * 6 + [total] * 2,
        compiler_params=pltpu.CompilerParams(vmem_limit_bytes=VMEM_LIMIT),
        cost_estimate=pl.CostEstimate(
            flops=12 * TOTAL * TOTAL * HEAD_DIM,
            bytes_accessed=6 * 2**20,
            transcendentals=TOTAL * TOTAL,
        ),
    )(length, order, text_rows, packed)


def encode(context, residual, weight, gain):
    core = lax.axis_index("core")
    swap = [(0, 1), (1, 0)]
    blocks = context.reshape(8, 2, 32, context.shape[1])
    own = lax.dynamic_index_in_dim(blocks, core, 1, keepdims=False).reshape(256, -1)
    theirs = lax.dynamic_index_in_dim(blocks, 1 - core, 1, keepdims=False).reshape(256, -1)
    other_weight = lax.ppermute(weight, "core", swap)
    other = lax.ppermute(theirs, "core", swap)
    partial = (matmul(own, weight) + matmul(other, other_weight)).astype(BF16)
    parts = lax.all_to_all(
        partial.reshape(8, 32, -1), ("y", "z_lo"), split_axis=0, concat_axis=0, tiled=True
    )
    stream = residual.astype(F32) + jnp.sum(parts.astype(F32), axis=0)
    inv_norm = lax.rsqrt(jnp.mean(stream * stream, axis=-1, keepdims=True) + 1e-06)
    encoded = (stream * inv_norm * gain).astype(BF16)
    return lax.all_gather(encoded, SEQ, axis=0, tiled=True)


def on_device(
    t5_context,
    t5_resid,
    t5_out_weight,
    t5_gain,
    text_weight,
    prompt_len,
    text_order,
    img_qkv,
    d_img_out,
    d_txt_out,
):
    packed = pack(img_qkv[0], d_img_out[0], d_txt_out[0])
    packed = lax.all_to_all(packed, SEQ, split_axis=0, concat_axis=0, tiled=True)
    encoded = encode(t5_context[0], t5_resid[0], t5_out_weight, t5_gain)
    text_rows = matmul(encoded, text_weight).astype(BF16)
    sent, text_grad = attention(prompt_len, text_order[0], text_rows, packed)
    weight_part = matmul(encoded, text_grad, CONTRACT_FIRST).astype(BF16)
    weight_parts = lax.all_to_all(
        weight_part.reshape(16, -1, weight_part.shape[1]),
        GRP,
        split_axis=0,
        concat_axis=0,
        tiled=True,
    )
    text_weight_grad = jnp.sum(weight_parts.astype(F32), axis=0)
    received = lax.all_to_all(sent, SEQ, split_axis=0, concat_axis=0, tiled=True)
    image_out, text_out, image_qkv_grad = unpack(received)
    return (image_out[None], text_out[None], image_qkv_grad[None], text_weight_grad)


def solution(mesh):
    fine = Mesh(mesh.devices.reshape(4, 4, 4, 2, 2), GRP + SEQ)
    in_specs = (
        P(GRP, None, SEQ),
        P(GRP, SEQ, None),
        P(SEQ, None),
        P(),
        P(None, SEQ),
        P(GRP),
        P(GRP, None),
        P(GRP, SEQ, None),
        P(GRP, SEQ, None),
        P(GRP, SEQ, None),
    )
    out_specs = (
        P(GRP, SEQ, None),
        P(GRP, SEQ, None),
        P(GRP, SEQ, None),
        P(GRP, SEQ),
    )
    return jax.shard_map(
        on_device, mesh=fine, in_specs=in_specs, out_specs=out_specs, check_vma=False
    )
```

```python
import jax
import jax.numpy as jnp
from jax import lax
from jax.experimental import pallas as pl
from jax.experimental.pallas import tpu as pltpu
from jax.sharding import Mesh
from jax.sharding import PartitionSpec as P

HEAD_DIM = 128
HEADS = 16
PROMPT = 512
IMAGE = 2048
TOTAL = PROMPT + IMAGE
BLOCK_ROWS = 16
TEXT_BLOCKS = 32
SHARE = IMAGE // HEADS
PACK_ROWS = SHARE + BLOCK_ROWS
PACK_COLS = 4 * HEAD_DIM
QUERY_BLOCK = 256
LOG2_E = 1.4426950408889634
WIDTH = 4096
FEATURES = WIDTH // HEADS
TEXT_SHARE = PROMPT // HEADS
CHIPS = [(ahead, across) for ahead in range(4) for across in range(2)]

BF16 = jnp.bfloat16
F32 = jnp.float32
SEQ = ("y", "z_lo", "core")
GRP = ("z_hi", "x")
CONTRACT_LAST = (((1,), (1,)), ((), ()))
CONTRACT_FIRST = (((0,), (0,)), ((), ()))
VMEM_LIMIT = 48 * 2**20


def matmul(a, b, dims=(((1,), (0,)), ((), ()))):
    return lax.dot_general(a, b, dims, preferred_element_type=F32)


def pack_kernel(qkv_ref, grad_ref, text_ref, packed_ref):
    for head in range(HEADS):
        columns = slice(head * HEAD_DIM, (head + 1) * HEAD_DIM)
        wide = slice(3 * head * HEAD_DIM, 3 * (head + 1) * HEAD_DIM)
        packed_ref[head, :SHARE, : 3 * HEAD_DIM] = qkv_ref[:, wide]
        packed_ref[head, :SHARE, 3 * HEAD_DIM :] = grad_ref[:, columns]
        packed_ref[head, SHARE:, :HEAD_DIM] = text_ref[:BLOCK_ROWS, columns]
        packed_ref[head, SHARE:, HEAD_DIM : 2 * HEAD_DIM] = text_ref[BLOCK_ROWS:, columns]
        packed_ref[head, SHARE:, 2 * HEAD_DIM :] = jnp.zeros((BLOCK_ROWS, 2 * HEAD_DIM), BF16)


def unpack_kernel(packed_ref, out_ref, text_ref, qkv_ref):
    for head in range(HEADS):
        columns = slice(head * HEAD_DIM, (head + 1) * HEAD_DIM)
        wide = slice(3 * head * HEAD_DIM, 3 * (head + 1) * HEAD_DIM)
        out_ref[:, columns] = packed_ref[head, :SHARE, :HEAD_DIM]
        qkv_ref[:, wide] = packed_ref[head, :SHARE, HEAD_DIM:]
        text_ref[:BLOCK_ROWS, columns] = packed_ref[head, SHARE:, :HEAD_DIM]
        text_ref[BLOCK_ROWS:, columns] = packed_ref[head, SHARE:, HEAD_DIM : 2 * HEAD_DIM]


def whole_call(kernel, out_shape, smem_inputs, vmem_inputs, scratch, flops, moved):
    in_vmem = pl.BlockSpec(memory_space=pltpu.VMEM)
    in_smem = pl.BlockSpec(memory_space=pltpu.SMEM)
    return pl.pallas_call(
        kernel,
        out_shape=out_shape,
        in_specs=[in_smem] * smem_inputs + [in_vmem] * vmem_inputs,
        out_specs=jax.tree.map(lambda _: in_vmem, out_shape),
        scratch_shapes=scratch,
        compiler_params=pltpu.CompilerParams(vmem_limit_bytes=VMEM_LIMIT),
        cost_estimate=pl.CostEstimate(flops=flops, bytes_accessed=moved, transcendentals=0),
    )


def rows_of(*shape):
    return jax.ShapeDtypeStruct(shape, BF16)


def pack(qkv, grad, text):
    shape = rows_of(HEADS, PACK_ROWS, PACK_COLS)
    return whole_call(pack_kernel, shape, 0, 3, [], 0, 2**22)(qkv, grad, text)


def unpack(packed):
    shapes = [
        rows_of(SHARE, HEADS * HEAD_DIM),
        rows_of(2 * BLOCK_ROWS, HEADS * HEAD_DIM),
        rows_of(SHARE, HEADS * 3 * HEAD_DIM),
    ]
    return whole_call(unpack_kernel, shapes, 0, 1, [], 0, 2**22)(packed)


def row_block(place_ref, ahead, across, other_core):
    y = lax.rem(place_ref[0] + ahead, 4)
    z = 1 - place_ref[1] if across else place_ref[1]
    core = 1 - place_ref[2] if other_core else place_ref[2]
    return (y * 2 + z) * 2 + core


def partial_kernel(place_ref, own_ref, other_ref, own_weight_ref, other_weight_ref, *refs):
    chunk_refs, rows_ref = refs[:8], refs[8]
    for index, (ahead, across) in enumerate(CHIPS):
        block = row_block(place_ref, ahead, across, False)
        rows = pl.ds(pl.multiple_of(block * TEXT_SHARE, TEXT_SHARE), TEXT_SHARE)
        to = slice(index * TEXT_SHARE, (index + 1) * TEXT_SHARE)
        rows_ref[to, :FEATURES] = own_ref[rows, :]
        rows_ref[to, FEATURES:] = other_ref[rows, :]

    def body(step, carry):
        columns = pl.ds(pl.multiple_of(step * 512, 512), 512)
        sums = matmul(rows_ref[:, :FEATURES], own_weight_ref[:, columns])
        sums += matmul(rows_ref[:, FEATURES:], other_weight_ref[:, columns])
        for index, chunk_ref in enumerate(chunk_refs):
            rows = slice(index * TEXT_SHARE, (index + 1) * TEXT_SHARE)
            chunk_ref[:, columns] = sums[rows].astype(BF16)
        return carry

    lax.fori_loop(0, WIDTH // 512, body, 0)


def text_kernel(place_ref, *refs):
    block_refs, weight_ref, text_ref, encoded_ref = refs[:16], refs[16], refs[17], refs[18]
    for index, block_ref in enumerate(block_refs):
        ahead, across = CHIPS[index % 8]
        block = row_block(place_ref, ahead, across, index >= 8)
        rows = pl.ds(pl.multiple_of(block * TEXT_SHARE, TEXT_SHARE), TEXT_SHARE)
        encoded_ref[rows, :] = block_ref[...]
    text_ref[...] = matmul(encoded_ref[...], weight_ref[...]).astype(BF16)


def attention_kernel(
    length_ref,
    order_ref,
    text_ref,
    packed_ref,
    sent_ref,
    text_grad_ref,
    q_ref,
    k_ref,
    v_ref,
    do_ref,
    out_ref,
    dq_ref,
    dkt_ref,
    dvt_ref,
):
    length = length_ref[0]
    factor = HEAD_DIM**-0.5
    for role, rows in enumerate((q_ref, k_ref, v_ref)):
        columns = slice(role * HEAD_DIM, (role + 1) * HEAD_DIM)
        rows[:PROMPT, :] = text_ref[:, columns]
        for src in range(HEADS):
            at = PROMPT + src * SHARE
            rows[at : at + SHARE, :] = packed_ref[src, :SHARE, columns]
    for src in range(HEADS):
        at = PROMPT + src * SHARE
        do_ref[at : at + SHARE, :] = packed_ref[src, :SHARE, 3 * HEAD_DIM :]
    for block in range(TEXT_BLOCKS):
        slot = order_ref[block]
        columns = pl.ds(pl.multiple_of((slot % 2) * HEAD_DIM, HEAD_DIM), HEAD_DIM)
        do_ref[block * BLOCK_ROWS : (block + 1) * BLOCK_ROWS, :] = packed_ref[
            slot // 2, SHARE:, columns
        ]
    dkt_ref[...] = jnp.zeros_like(dkt_ref)
    dvt_ref[...] = jnp.zeros_like(dvt_ref)

    def body(step, carry):
        rows = pl.ds(pl.multiple_of(step * QUERY_BLOCK, QUERY_BLOCK), QUERY_BLOCK)
        queries = q_ref[rows, :]
        keys = k_ref[...]
        values = v_ref[...]
        scores = matmul(queries, keys, CONTRACT_LAST)
        position = lax.broadcasted_iota(jnp.int32, (1, TOTAL), 1)
        scores = jnp.where((position < length) | (position >= PROMPT), scores, -1e30)
        maximum = jnp.max(scores, axis=-1, keepdims=True)
        weights = jnp.exp2((scores - maximum) * (factor * LOG2_E)).astype(BF16)
        wide = weights.astype(F32)
        inverse = 1.0 / jnp.sum(wide, axis=-1, keepdims=True)
        output = matmul(weights, values) * inverse
        out_grad = (do_ref[rows, :].astype(F32) * inverse).astype(BF16)
        row_delta = jnp.sum(out_grad.astype(F32) * output, axis=-1, keepdims=True)
        prob_grad = matmul(out_grad, values, CONTRACT_LAST)
        score_grad = (wide * (prob_grad - row_delta)).astype(BF16)
        out_ref[rows, :] = output.astype(BF16)
        dq_ref[rows, :] = (matmul(score_grad, keys) * factor).astype(BF16)
        dkt_ref[...] += matmul(queries, score_grad, CONTRACT_FIRST)
        dvt_ref[...] += matmul(out_grad, weights, CONTRACT_FIRST)
        return carry

    lax.fori_loop(0, TOTAL // QUERY_BLOCK, body, 0)
    q_ref[...] = (dkt_ref[...] * factor).T.astype(BF16)
    k_ref[...] = dvt_ref[...].T.astype(BF16)
    for place, rows in enumerate((out_ref, dq_ref, q_ref, k_ref)):
        columns = slice(place * HEAD_DIM, (place + 1) * HEAD_DIM)
        for dest in range(HEADS):
            at = PROMPT + dest * SHARE
            sent_ref[dest, :SHARE, columns] = rows[at : at + SHARE, :]
        if place:
            text_grad_ref[:, (place - 1) * HEAD_DIM : place * HEAD_DIM] = rows[:PROMPT, :]
    sent_ref[:, SHARE:, 2 * HEAD_DIM :] = jnp.zeros((HEADS, BLOCK_ROWS, 2 * HEAD_DIM), BF16)
    for block in range(TEXT_BLOCKS):
        slot = order_ref[block]
        columns = pl.ds(pl.multiple_of((slot % 2) * HEAD_DIM, HEAD_DIM), HEAD_DIM)
        sent_ref[slot // 2, SHARE:, columns] = out_ref[
            block * BLOCK_ROWS : (block + 1) * BLOCK_ROWS, :
        ]


def attention(length, order, text_rows, packed):
    in_vmem = pl.BlockSpec(memory_space=pltpu.VMEM)
    in_smem = pl.BlockSpec(memory_space=pltpu.SMEM)
    rows = pltpu.VMEM((TOTAL, HEAD_DIM), BF16)
    total = pltpu.VMEM((HEAD_DIM, TOTAL), F32)
    return pl.pallas_call(
        attention_kernel,
        out_shape=[
            jax.ShapeDtypeStruct((HEADS, PACK_ROWS, PACK_COLS), BF16),
            jax.ShapeDtypeStruct((PROMPT, 3 * HEAD_DIM), BF16),
        ],
        in_specs=[in_smem, in_smem, in_vmem, in_vmem],
        out_specs=[in_vmem, in_vmem],
        scratch_shapes=[rows] * 6 + [total] * 2,
        compiler_params=pltpu.CompilerParams(vmem_limit_bytes=VMEM_LIMIT),
        cost_estimate=pl.CostEstimate(
            flops=12 * TOTAL * TOTAL * HEAD_DIM,
            bytes_accessed=6 * 2**20,
            transcendentals=TOTAL * TOTAL,
        ),
    )(length, order, text_rows, packed)


def shift(rows, axis, step):
    size = 2 if axis in ("z_lo", "core") else 4
    return lax.ppermute(rows, axis, [(i, (i + step) % size) for i in range(size)])


def add(*rows):
    return sum(part.astype(F32) for part in rows)


def encode(place, context, residual, weight, gain):
    other_weight = shift(weight, "core", 1)
    other = shift(context, "core", 1)
    chunks = whole_call(
        partial_kernel,
        [rows_of(TEXT_SHARE, WIDTH)] * 8,
        1,
        4,
        [pltpu.VMEM((8 * TEXT_SHARE, 2 * FEATURES), BF16)],
        2 * 8 * TEXT_SHARE * 2 * FEATURES * WIDTH,
        2**23,
    )(place, context, other, weight, other_weight)
    part = dict(zip(CHIPS, chunks))
    from_across = shift(part[2, 1], "z_lo", 1)
    from_below = shift(part[1, 1], "y", 1)
    from_above = shift(part[3, 1], "y", -1)
    below = shift(part[1, 0], "y", 1)
    above = shift(part[3, 0], "y", -1)
    opposite = shift(add(part[2, 0], from_across).astype(BF16), "y", 2)
    across = shift(add(part[0, 1], from_below, from_above).astype(BF16), "z_lo", 1)
    stream = add(residual, part[0, 0], below, above, opposite, across)
    inv_norm = lax.rsqrt(jnp.mean(stream * stream, axis=-1, keepdims=True) + 1e-06)
    encoded = (stream * inv_norm * gain).astype(BF16)
    held = {(0, 0): encoded}
    held[0, 1] = shift(encoded, "z_lo", 1)
    held[3, 0] = shift(encoded, "y", 1)
    held[1, 0] = shift(encoded, "y", -1)
    held[2, 0] = shift(encoded, "y", 2)
    held[3, 1] = shift(held[0, 1], "y", 1)
    held[1, 1] = shift(held[0, 1], "y", -1)
    held[2, 1] = shift(held[2, 0], "z_lo", 1)
    own = [held[chip] for chip in CHIPS]
    return own + [shift(rows, "core", 1) for rows in own]


def project(place, blocks, weight):
    columns = weight.shape[1]
    return whole_call(
        text_kernel,
        [rows_of(PROMPT, columns), rows_of(PROMPT, WIDTH)],
        1,
        17,
        [],
        2 * PROMPT * WIDTH * columns,
        2**23,
    )(place, *blocks, weight)


def on_device(
    t5_context,
    t5_resid,
    t5_out_weight,
    t5_gain,
    text_weight,
    prompt_len,
    text_order,
    img_qkv,
    d_img_out,
    d_txt_out,
):
    packed = pack(img_qkv[0], d_img_out[0], d_txt_out[0])
    packed = lax.all_to_all(packed, SEQ, split_axis=0, concat_axis=0, tiled=True)
    place = jnp.stack([lax.axis_index(axis) for axis in SEQ])
    blocks = encode(place, t5_context[0], t5_resid[0], t5_out_weight, t5_gain)
    text_rows, encoded = project(place, blocks, text_weight)
    sent, text_grad = attention(prompt_len, text_order[0], text_rows, packed)
    weight_part = matmul(encoded, text_grad, CONTRACT_FIRST).astype(BF16)
    weight_parts = lax.all_to_all(
        weight_part.reshape(16, -1, weight_part.shape[1]),
        GRP,
        split_axis=0,
        concat_axis=0,
        tiled=True,
    )
    text_weight_grad = jnp.sum(weight_parts.astype(F32), axis=0)
    received = lax.all_to_all(sent, SEQ, split_axis=0, concat_axis=0, tiled=True)
    image_out, text_out, image_qkv_grad = unpack(received)
    return (image_out[None], text_out[None], image_qkv_grad[None], text_weight_grad)


def solution(mesh):
    fine = Mesh(mesh.devices.reshape(4, 4, 4, 2, 2), GRP + SEQ)
    in_specs = (
        P(GRP, None, SEQ),
        P(GRP, SEQ, None),
        P(SEQ, None),
        P(),
        P(None, SEQ),
        P(GRP),
        P(GRP, None),
        P(GRP, SEQ, None),
        P(GRP, SEQ, None),
        P(GRP, SEQ, None),
    )
    out_specs = (
        P(GRP, SEQ, None),
        P(GRP, SEQ, None),
        P(GRP, SEQ, None),
        P(GRP, SEQ),
    )
    return jax.shard_map(
        on_device, mesh=fine, in_specs=in_specs, out_specs=out_specs, check_vma=False
    )
```

```python
import jax
import jax.numpy as jnp
from jax import lax
from jax.experimental import pallas as pl
from jax.experimental.pallas import tpu as pltpu
from jax.sharding import Mesh
from jax.sharding import PartitionSpec as P

HEAD_DIM = 128
HEADS = 16
PROMPT = 512
IMAGE = 2048
TOTAL = PROMPT + IMAGE
BLOCK_ROWS = 16
TEXT_BLOCKS = 32
SHARE = IMAGE // HEADS
PACK_ROWS = SHARE + BLOCK_ROWS
PACK_COLS = 4 * HEAD_DIM
QUERY_BLOCK = 256
LOG2_E = 1.4426950408889634
WIDTH = 4096
FEATURES = WIDTH // HEADS
TEXT_SHARE = PROMPT // HEADS
HALF_PROMPT = PROMPT // 2
CHIPS = [(ahead, across) for ahead in range(4) for across in range(2)]

BF16 = jnp.bfloat16
F32 = jnp.float32
SEQ = ("y", "z_lo", "core")
GRP = ("z_hi", "x")
CONTRACT_LAST = (((1,), (1,)), ((), ()))
CONTRACT_FIRST = (((0,), (0,)), ((), ()))
VMEM_LIMIT = 48 * 2**20


def matmul(a, b, dims=(((1,), (0,)), ((), ()))):
    return lax.dot_general(a, b, dims, preferred_element_type=F32)


def pack_kernel(qkv_ref, grad_ref, text_ref, packed_ref):
    for head in range(HEADS):
        columns = slice(head * HEAD_DIM, (head + 1) * HEAD_DIM)
        wide = slice(3 * head * HEAD_DIM, 3 * (head + 1) * HEAD_DIM)
        packed_ref[head, :SHARE, : 3 * HEAD_DIM] = qkv_ref[:, wide]
        packed_ref[head, :SHARE, 3 * HEAD_DIM :] = grad_ref[:, columns]
        packed_ref[head, SHARE:, :HEAD_DIM] = text_ref[:BLOCK_ROWS, columns]
        packed_ref[head, SHARE:, HEAD_DIM : 2 * HEAD_DIM] = text_ref[BLOCK_ROWS:, columns]
        packed_ref[head, SHARE:, 2 * HEAD_DIM :] = jnp.zeros((BLOCK_ROWS, 2 * HEAD_DIM), BF16)


def unpack_kernel(packed_ref, out_ref, text_ref, qkv_ref):
    for head in range(HEADS):
        columns = slice(head * HEAD_DIM, (head + 1) * HEAD_DIM)
        wide = slice(3 * head * HEAD_DIM, 3 * (head + 1) * HEAD_DIM)
        out_ref[:, columns] = packed_ref[head, :SHARE, :HEAD_DIM]
        qkv_ref[:, wide] = packed_ref[head, :SHARE, HEAD_DIM:]
        text_ref[:BLOCK_ROWS, columns] = packed_ref[head, SHARE:, :HEAD_DIM]
        text_ref[BLOCK_ROWS:, columns] = packed_ref[head, SHARE:, HEAD_DIM : 2 * HEAD_DIM]


def whole_call(kernel, out_shape, smem_inputs, vmem_inputs, scratch, flops, moved):
    in_vmem = pl.BlockSpec(memory_space=pltpu.VMEM)
    in_smem = pl.BlockSpec(memory_space=pltpu.SMEM)
    return pl.pallas_call(
        kernel,
        out_shape=out_shape,
        in_specs=[in_smem] * smem_inputs + [in_vmem] * vmem_inputs,
        out_specs=jax.tree.map(lambda _: in_vmem, out_shape),
        scratch_shapes=scratch,
        compiler_params=pltpu.CompilerParams(vmem_limit_bytes=VMEM_LIMIT),
        cost_estimate=pl.CostEstimate(flops=flops, bytes_accessed=moved, transcendentals=0),
    )


def rows_of(*shape):
    return jax.ShapeDtypeStruct(shape, BF16)


def pack(qkv, grad, text):
    shape = rows_of(HEADS, PACK_ROWS, PACK_COLS)
    return whole_call(pack_kernel, shape, 0, 3, [], 0, 2**22)(qkv, grad, text)


def unpack(packed):
    shapes = [
        rows_of(SHARE, HEADS * HEAD_DIM),
        rows_of(2 * BLOCK_ROWS, HEADS * HEAD_DIM),
        rows_of(SHARE, HEADS * 3 * HEAD_DIM),
    ]
    return whole_call(unpack_kernel, shapes, 0, 1, [], 0, 2**22)(packed)


def row_block(place_ref, ahead, across, other_core):
    y = lax.rem(place_ref[0] + ahead, 4)
    z = 1 - place_ref[1] if across else place_ref[1]
    core = 1 - place_ref[2] if other_core else place_ref[2]
    return (y * 2 + z) * 2 + core


def partial_kernel(place_ref, own_ref, other_ref, own_weight_ref, other_weight_ref, *refs):
    chunk_refs, rows_ref = refs[:8], refs[8]
    for index, (ahead, across) in enumerate(CHIPS):
        block = row_block(place_ref, ahead, across, False)
        rows = pl.ds(pl.multiple_of(block * TEXT_SHARE, TEXT_SHARE), TEXT_SHARE)
        to = slice(index * TEXT_SHARE, (index + 1) * TEXT_SHARE)
        rows_ref[to, :FEATURES] = own_ref[rows, :]
        rows_ref[to, FEATURES:] = other_ref[rows, :]

    def body(step, carry):
        columns = pl.ds(pl.multiple_of(step * 512, 512), 512)
        sums = matmul(rows_ref[:, :FEATURES], own_weight_ref[:, columns])
        sums += matmul(rows_ref[:, FEATURES:], other_weight_ref[:, columns])
        for index, chunk_ref in enumerate(chunk_refs):
            rows = slice(index * TEXT_SHARE, (index + 1) * TEXT_SHARE)
            chunk_ref[:, columns] = sums[rows].astype(BF16)
        return carry

    lax.fori_loop(0, WIDTH // 512, body, 0)


def text_kernel(place_ref, *refs):
    block_refs, weight_ref, text_ref = refs[:16], refs[16], refs[17]
    kept_ref, sent_refs, encoded_ref = refs[18], refs[19:22], refs[22]
    for index, block_ref in enumerate(block_refs):
        ahead, across = CHIPS[index % 8]
        block = row_block(place_ref, ahead, across, index >= 8)
        rows = pl.ds(pl.multiple_of(block * TEXT_SHARE, TEXT_SHARE), TEXT_SHARE)
        encoded_ref[rows, :] = block_ref[...]
    half = pl.ds(pl.multiple_of(place_ref[2] * HALF_PROMPT, HALF_PROMPT), HALF_PROMPT)
    for ahead in range(4):
        x = lax.rem(place_ref[4] + ahead, 4)
        for z_hi in range(4):
            at = pl.ds(pl.multiple_of((z_hi * 4 + x) * FEATURES, FEATURES), FEATURES)
            to = slice(z_hi * FEATURES, (z_hi + 1) * FEATURES)
            if ahead:
                sent_refs[ahead - 1][:, to] = encoded_ref[half, at]
            else:
                kept_ref[:, to] = encoded_ref[:, at]
    text_ref[...] = matmul(encoded_ref[...], weight_ref[...]).astype(BF16)


def weight_kernel(place_ref, kept_ref, *refs):
    near_refs, far_refs, grad_refs = refs[:3], refs[3:6], refs[6:10]
    kept_sum_ref, sent_refs = refs[10], refs[11:14]
    near = pl.ds(pl.multiple_of(place_ref[2] * HALF_PROMPT, HALF_PROMPT), HALF_PROMPT)
    far = pl.ds(pl.multiple_of((1 - place_ref[2]) * HALF_PROMPT, HALF_PROMPT), HALF_PROMPT)
    for ahead in range(4):
        z_hi = lax.rem(place_ref[3] + ahead, 4)
        at = pl.ds(pl.multiple_of(z_hi * FEATURES, FEATURES), FEATURES)
        total = matmul(grad_refs[0][...], kept_ref[:, at], CONTRACT_FIRST)
        for grad_ref, near_ref, far_ref in zip(grad_refs[1:], near_refs, far_refs):
            total += matmul(grad_ref[near, :], near_ref[:, at], CONTRACT_FIRST)
            total += matmul(grad_ref[far, :], far_ref[:, at], CONTRACT_FIRST)
        if ahead:
            sent_refs[ahead - 1][...] = total.astype(BF16)
        else:
            kept_sum_ref[...] = total


def total_kernel(kept_ref, *refs):
    total = kept_ref[...]
    for part_ref in refs[:3]:
        total += part_ref[...].astype(F32)
    refs[3][...] = total.T


def attention_kernel(
    length_ref,
    order_ref,
    text_ref,
    packed_ref,
    sent_ref,
    text_grad_ref,
    q_ref,
    k_ref,
    v_ref,
    do_ref,
    out_ref,
    dq_ref,
    dkt_ref,
    dvt_ref,
):
    length = length_ref[0]
    factor = HEAD_DIM**-0.5
    for role, rows in enumerate((q_ref, k_ref, v_ref)):
        columns = slice(role * HEAD_DIM, (role + 1) * HEAD_DIM)
        rows[:PROMPT, :] = text_ref[:, columns]
        for src in range(HEADS):
            at = PROMPT + src * SHARE
            rows[at : at + SHARE, :] = packed_ref[src, :SHARE, columns]
    for src in range(HEADS):
        at = PROMPT + src * SHARE
        do_ref[at : at + SHARE, :] = packed_ref[src, :SHARE, 3 * HEAD_DIM :]
    for block in range(TEXT_BLOCKS):
        slot = order_ref[block]
        columns = pl.ds(pl.multiple_of((slot % 2) * HEAD_DIM, HEAD_DIM), HEAD_DIM)
        do_ref[block * BLOCK_ROWS : (block + 1) * BLOCK_ROWS, :] = packed_ref[
            slot // 2, SHARE:, columns
        ]
    dkt_ref[...] = jnp.zeros_like(dkt_ref)
    dvt_ref[...] = jnp.zeros_like(dvt_ref)

    def body(step, carry):
        rows = pl.ds(pl.multiple_of(step * QUERY_BLOCK, QUERY_BLOCK), QUERY_BLOCK)
        queries = q_ref[rows, :]
        keys = k_ref[...]
        values = v_ref[...]
        scores = matmul(queries, keys, CONTRACT_LAST)
        position = lax.broadcasted_iota(jnp.int32, (1, TOTAL), 1)
        scores = jnp.where((position < length) | (position >= PROMPT), scores, -1e30)
        maximum = jnp.max(scores, axis=-1, keepdims=True)
        weights = jnp.exp2((scores - maximum) * (factor * LOG2_E)).astype(BF16)
        wide = weights.astype(F32)
        inverse = 1.0 / jnp.sum(wide, axis=-1, keepdims=True)
        output = matmul(weights, values) * inverse
        out_grad = (do_ref[rows, :].astype(F32) * inverse).astype(BF16)
        row_delta = jnp.sum(out_grad.astype(F32) * output, axis=-1, keepdims=True)
        prob_grad = matmul(out_grad, values, CONTRACT_LAST)
        score_grad = (wide * (prob_grad - row_delta)).astype(BF16)
        out_ref[rows, :] = output.astype(BF16)
        dq_ref[rows, :] = (matmul(score_grad, keys) * factor).astype(BF16)
        dkt_ref[...] += matmul(queries, score_grad, CONTRACT_FIRST)
        dvt_ref[...] += matmul(out_grad, weights, CONTRACT_FIRST)
        return carry

    lax.fori_loop(0, TOTAL // QUERY_BLOCK, body, 0)
    q_ref[...] = (dkt_ref[...] * factor).T.astype(BF16)
    k_ref[...] = dvt_ref[...].T.astype(BF16)
    for place, rows in enumerate((out_ref, dq_ref, q_ref, k_ref)):
        columns = slice(place * HEAD_DIM, (place + 1) * HEAD_DIM)
        for dest in range(HEADS):
            at = PROMPT + dest * SHARE
            sent_ref[dest, :SHARE, columns] = rows[at : at + SHARE, :]
        if place:
            text_grad_ref[:, (place - 1) * HEAD_DIM : place * HEAD_DIM] = rows[:PROMPT, :]
    sent_ref[:, SHARE:, 2 * HEAD_DIM :] = jnp.zeros((HEADS, BLOCK_ROWS, 2 * HEAD_DIM), BF16)
    for block in range(TEXT_BLOCKS):
        slot = order_ref[block]
        columns = pl.ds(pl.multiple_of((slot % 2) * HEAD_DIM, HEAD_DIM), HEAD_DIM)
        sent_ref[slot // 2, SHARE:, columns] = out_ref[
            block * BLOCK_ROWS : (block + 1) * BLOCK_ROWS, :
        ]


def attention(length, order, text_rows, packed):
    in_vmem = pl.BlockSpec(memory_space=pltpu.VMEM)
    in_smem = pl.BlockSpec(memory_space=pltpu.SMEM)
    rows = pltpu.VMEM((TOTAL, HEAD_DIM), BF16)
    total = pltpu.VMEM((HEAD_DIM, TOTAL), F32)
    return pl.pallas_call(
        attention_kernel,
        out_shape=[
            jax.ShapeDtypeStruct((HEADS, PACK_ROWS, PACK_COLS), BF16),
            jax.ShapeDtypeStruct((PROMPT, 3 * HEAD_DIM), BF16),
        ],
        in_specs=[in_smem, in_smem, in_vmem, in_vmem],
        out_specs=[in_vmem, in_vmem],
        scratch_shapes=[rows] * 6 + [total] * 2,
        compiler_params=pltpu.CompilerParams(vmem_limit_bytes=VMEM_LIMIT),
        cost_estimate=pl.CostEstimate(
            flops=360 * TOTAL * TOTAL * HEAD_DIM,
            bytes_accessed=2**29,
            transcendentals=TOTAL * TOTAL,
        ),
    )(length, order, text_rows, packed)


def shift(rows, axis, step):
    size = 2 if axis in ("z_lo", "core") else 4
    return lax.ppermute(rows, axis, [(i, (i + step) % size) for i in range(size)])


def add(*rows):
    return sum(part.astype(F32) for part in rows)


def encode(place, context, residual, weight, gain, packed):
    other_weight = shift(weight, "core", 1)
    other = shift(context, "core", 1)
    other_weight, packed = lax.optimization_barrier((other_weight, packed))
    packed = lax.all_to_all(packed, SEQ, split_axis=0, concat_axis=0, tiled=True)
    chunks = whole_call(
        partial_kernel,
        [rows_of(TEXT_SHARE, WIDTH)] * 8,
        1,
        4,
        [pltpu.VMEM((8 * TEXT_SHARE, 2 * FEATURES), BF16)],
        2 * 8 * TEXT_SHARE * 2 * FEATURES * WIDTH,
        2**23,
    )(place, context, other, weight, other_weight)
    part = dict(zip(CHIPS, chunks))
    from_across = shift(part[2, 1], "z_lo", 1)
    from_below = shift(part[1, 1], "y", 1)
    from_above = shift(part[3, 1], "y", -1)
    below = shift(part[1, 0], "y", 1)
    above = shift(part[3, 0], "y", -1)
    opposite = shift(add(part[2, 0], from_across).astype(BF16), "y", 2)
    across = shift(add(part[0, 1], from_below, from_above).astype(BF16), "z_lo", 1)
    stream = add(residual, part[0, 0], below, above, opposite, across)
    inv_norm = lax.rsqrt(jnp.mean(stream * stream, axis=-1, keepdims=True) + 1e-06)
    encoded = (stream * inv_norm * gain).astype(BF16)
    packed, encoded = lax.optimization_barrier((packed, encoded))
    held = {(0, 0): encoded}
    held[0, 1] = shift(encoded, "z_lo", 1)
    held[3, 0] = shift(encoded, "y", 1)
    held[1, 0] = shift(encoded, "y", -1)
    held[2, 0] = shift(encoded, "y", 2)
    held[3, 1] = shift(held[0, 1], "y", 1)
    held[1, 1] = shift(held[0, 1], "y", -1)
    held[2, 1] = shift(held[2, 0], "z_lo", 1)
    own = [held[chip] for chip in CHIPS]
    return own + [shift(rows, "core", 1) for rows in own], packed


def project(place, blocks, weight):
    columns = weight.shape[1]
    quarter = 4 * FEATURES
    return whole_call(
        text_kernel,
        [rows_of(PROMPT, columns), rows_of(PROMPT, quarter)] + [rows_of(HALF_PROMPT, quarter)] * 3,
        1,
        17,
        [pltpu.VMEM((PROMPT, WIDTH), BF16)],
        2 * PROMPT * WIDTH * columns,
        2**23,
    )(place, *blocks, weight)


def weight_gradient(place, kept, near, far, grads):
    columns = grads[0].shape[1]
    total = jax.ShapeDtypeStruct((columns, FEATURES), F32)
    kept_sum, *sent = whole_call(
        weight_kernel,
        [total] + [rows_of(columns, FEATURES)] * 3,
        1,
        11,
        [],
        2 * 4 * PROMPT * 4 * FEATURES * columns,
        2**23,
    )(place, kept, *near, *far, *grads)
    parts = [shift(rows, "z_hi", step + 1) for step, rows in enumerate(sent)]
    shape = jax.ShapeDtypeStruct((FEATURES, columns), F32)
    return whole_call(total_kernel, shape, 0, 4, [], 0, 2**20)(kept_sum, *parts)


def on_device(
    t5_context,
    t5_resid,
    t5_out_weight,
    t5_gain,
    text_weight,
    prompt_len,
    text_order,
    img_qkv,
    d_img_out,
    d_txt_out,
):
    packed = pack(img_qkv[0], d_img_out[0], d_txt_out[0])
    place = jnp.stack([lax.axis_index(axis) for axis in SEQ + GRP])
    blocks, packed = encode(
        place, t5_context[0], t5_resid[0], t5_out_weight, t5_gain, packed
    )
    text_rows, kept, *slices = project(place, blocks, text_weight)
    near = [shift(rows, "x", step + 1) for step, rows in enumerate(slices)]
    sent, text_grad = attention(prompt_len, text_order[0], text_rows, packed)
    *near, sent = lax.optimization_barrier((*near, sent))
    far = [shift(rows, "core", 1) for rows in near]
    grads = [text_grad] + [shift(text_grad, "x", step) for step in (1, 2, 3)]
    text_weight_grad = weight_gradient(place, kept, near, far, grads)
    received = lax.all_to_all(sent, SEQ, split_axis=0, concat_axis=0, tiled=True)
    image_out, text_out, image_qkv_grad = unpack(received)
    return (image_out[None], text_out[None], image_qkv_grad[None], text_weight_grad)


def solution(mesh):
    fine = Mesh(mesh.devices.reshape(4, 4, 4, 2, 2), GRP + SEQ)
    in_specs = (
        P(GRP, None, SEQ),
        P(GRP, SEQ, None),
        P(SEQ, None),
        P(),
        P(None, SEQ),
        P(GRP),
        P(GRP, None),
        P(GRP, SEQ, None),
        P(GRP, SEQ, None),
        P(GRP, SEQ, None),
    )
    out_specs = (
        P(GRP, SEQ, None),
        P(GRP, SEQ, None),
        P(GRP, SEQ, None),
        P(GRP, SEQ),
    )
    return jax.shard_map(
        on_device, mesh=fine, in_specs=in_specs, out_specs=out_specs, check_vma=False
    )
```

```python
import jax
import jax.numpy as jnp
from jax import lax
from jax.experimental import pallas as pl
from jax.experimental.pallas import tpu as pltpu
from jax.sharding import Mesh
from jax.sharding import PartitionSpec as P

HEAD_DIM = 128
HEADS = 16
PROMPT = 512
IMAGE = 2048
TOTAL = PROMPT + IMAGE
BLOCK_ROWS = 16
TEXT_BLOCKS = 32
SHARE = IMAGE // HEADS
PACK_ROWS = SHARE + BLOCK_ROWS
PACK_COLS = 4 * HEAD_DIM
QUERY_BLOCK = 256
LOG2_E = 1.4426950408889634
PACK_HEADS = 4
CHAINS = 2
WIDTH = 4096
FEATURES = WIDTH // HEADS
TEXT_SHARE = PROMPT // HEADS
HALF_PROMPT = PROMPT // 2
CHIPS = [(ahead, across) for ahead in range(4) for across in range(2)]

BF16 = jnp.bfloat16
F32 = jnp.float32
SEQ = ("y", "z_lo", "core")
GRP = ("z_hi", "x")
CONTRACT_LAST = (((1,), (1,)), ((), ()))
CONTRACT_FIRST = (((0,), (0,)), ((), ()))
VMEM_LIMIT = 48 * 2**20
WHOLE_VMEM = 60 * 2**20


def matmul(a, b, dims=(((1,), (0,)), ((), ()))):
    return lax.dot_general(a, b, dims, preferred_element_type=F32)


def pack_kernel(qkv_hbm, grad_hbm, text_hbm, packed_hbm, *refs):
    qkv_ref, grad_ref, text_ref, packed_ref, loaded, stored = refs
    loads = []
    for source, target in ((grad_hbm, grad_ref), (text_hbm, text_ref)):
        loads.append(pltpu.make_async_copy(source, target, loaded.at[len(loads)]))
    width = 3 * HEAD_DIM * PACK_HEADS
    for group in range(HEADS // PACK_HEADS):
        columns = slice(group * width, (group + 1) * width)
        source, target = qkv_hbm.at[:, columns], qkv_ref.at[:, columns]
        loads.append(pltpu.make_async_copy(source, target, loaded.at[len(loads)]))
    for load in loads:
        load.start()
    loads[0].wait()
    loads[1].wait()
    stores = []
    for group in range(HEADS // PACK_HEADS):
        loads[2 + group].wait()
        heads = slice(group * PACK_HEADS, (group + 1) * PACK_HEADS)
        for head in range(heads.start, heads.stop):
            columns = slice(head * HEAD_DIM, (head + 1) * HEAD_DIM)
            wide = slice(3 * head * HEAD_DIM, 3 * (head + 1) * HEAD_DIM)
            packed_ref[head, :SHARE, : 3 * HEAD_DIM] = qkv_ref[:, wide]
            packed_ref[head, :SHARE, 3 * HEAD_DIM :] = grad_ref[:, columns]
            packed_ref[head, SHARE:, :HEAD_DIM] = text_ref[:BLOCK_ROWS, columns]
            packed_ref[head, SHARE:, HEAD_DIM : 2 * HEAD_DIM] = text_ref[BLOCK_ROWS:, columns]
            packed_ref[head, SHARE:, 2 * HEAD_DIM :] = jnp.zeros(
                (BLOCK_ROWS, 2 * HEAD_DIM), BF16
            )
        store = pltpu.make_async_copy(
            packed_ref.at[heads], packed_hbm.at[heads], stored.at[group]
        )
        store.start()
        stores.append(store)
    for store in stores:
        store.wait()


def unpack_kernel(packed_ref, out_ref, text_ref, qkv_ref):
    for head in range(HEADS):
        columns = slice(head * HEAD_DIM, (head + 1) * HEAD_DIM)
        wide = slice(3 * head * HEAD_DIM, 3 * (head + 1) * HEAD_DIM)
        out_ref[:, columns] = packed_ref[head, :SHARE, :HEAD_DIM]
        qkv_ref[:, wide] = packed_ref[head, :SHARE, HEAD_DIM:]
        text_ref[:BLOCK_ROWS, columns] = packed_ref[head, SHARE:, :HEAD_DIM]
        text_ref[BLOCK_ROWS:, columns] = packed_ref[head, SHARE:, HEAD_DIM : 2 * HEAD_DIM]


def whole_call(kernel, out_shape, smem_inputs, vmem_inputs, scratch, flops, moved):
    in_vmem = pl.BlockSpec(memory_space=pltpu.VMEM)
    in_smem = pl.BlockSpec(memory_space=pltpu.SMEM)
    return pl.pallas_call(
        kernel,
        out_shape=out_shape,
        in_specs=[in_smem] * smem_inputs + [in_vmem] * vmem_inputs,
        out_specs=jax.tree.map(lambda _: in_vmem, out_shape),
        scratch_shapes=scratch,
        compiler_params=pltpu.CompilerParams(vmem_limit_bytes=VMEM_LIMIT),
        cost_estimate=pl.CostEstimate(flops=flops, bytes_accessed=moved, transcendentals=0),
    )


def rows_of(*shape):
    return jax.ShapeDtypeStruct(shape, BF16)


def pack(qkv, grad, text):
    anywhere = pl.BlockSpec(memory_space=pltpu.HBM)
    groups = HEADS // PACK_HEADS
    return pl.pallas_call(
        pack_kernel,
        out_shape=rows_of(HEADS, PACK_ROWS, PACK_COLS),
        in_specs=[anywhere] * 3,
        out_specs=anywhere,
        scratch_shapes=[
            pltpu.VMEM(qkv.shape, BF16),
            pltpu.VMEM(grad.shape, BF16),
            pltpu.VMEM(text.shape, BF16),
            pltpu.VMEM((HEADS, PACK_ROWS, PACK_COLS), BF16),
            pltpu.SemaphoreType.DMA((2 + groups,)),
            pltpu.SemaphoreType.DMA((groups,)),
        ],
        compiler_params=pltpu.CompilerParams(vmem_limit_bytes=WHOLE_VMEM),
        cost_estimate=pl.CostEstimate(flops=0, bytes_accessed=2**22, transcendentals=0),
    )(qkv, grad, text)


def unpack(packed):
    shapes = [
        rows_of(SHARE, HEADS * HEAD_DIM),
        rows_of(2 * BLOCK_ROWS, HEADS * HEAD_DIM),
        rows_of(SHARE, HEADS * 3 * HEAD_DIM),
    ]
    return whole_call(unpack_kernel, shapes, 0, 1, [], 0, 2**22)(packed)


def row_block(place_ref, ahead, across, other_core):
    y = lax.rem(place_ref[0] + ahead, 4)
    z = 1 - place_ref[1] if across else place_ref[1]
    core = 1 - place_ref[2] if other_core else place_ref[2]
    return (y * 2 + z) * 2 + core


def partial_kernel(place_ref, own_ref, other_ref, own_weight_ref, other_weight_ref, *refs):
    chunk_refs, rows_ref = refs[:8], refs[8]
    for index, (ahead, across) in enumerate(CHIPS):
        block = row_block(place_ref, ahead, across, False)
        rows = pl.ds(pl.multiple_of(block * TEXT_SHARE, TEXT_SHARE), TEXT_SHARE)
        to = slice(index * TEXT_SHARE, (index + 1) * TEXT_SHARE)
        rows_ref[to, :FEATURES] = own_ref[rows, :]
        rows_ref[to, FEATURES:] = other_ref[rows, :]

    def body(step, carry):
        columns = pl.ds(pl.multiple_of(step * 512, 512), 512)
        sums = matmul(rows_ref[:, :FEATURES], own_weight_ref[:, columns])
        sums += matmul(rows_ref[:, FEATURES:], other_weight_ref[:, columns])
        for index, chunk_ref in enumerate(chunk_refs):
            rows = slice(index * TEXT_SHARE, (index + 1) * TEXT_SHARE)
            chunk_ref[:, columns] = sums[rows].astype(BF16)
        return carry

    lax.fori_loop(0, WIDTH // 512, body, 0)


def text_kernel(place_ref, *refs):
    block_refs, weight_ref, text_ref = refs[:16], refs[16], refs[17]
    kept_ref, sent_refs, encoded_ref = refs[18], refs[19:22], refs[22]
    for index, block_ref in enumerate(block_refs):
        ahead, across = CHIPS[index % 8]
        block = row_block(place_ref, ahead, across, index >= 8)
        rows = pl.ds(pl.multiple_of(block * TEXT_SHARE, TEXT_SHARE), TEXT_SHARE)
        encoded_ref[rows, :] = block_ref[...]
    half = pl.ds(pl.multiple_of(place_ref[2] * HALF_PROMPT, HALF_PROMPT), HALF_PROMPT)
    for ahead in range(4):
        x = lax.rem(place_ref[4] + ahead, 4)
        for z_hi in range(4):
            at = pl.ds(pl.multiple_of((z_hi * 4 + x) * FEATURES, FEATURES), FEATURES)
            to = slice(z_hi * FEATURES, (z_hi + 1) * FEATURES)
            if ahead:
                sent_refs[ahead - 1][:, to] = encoded_ref[half, at]
            else:
                kept_ref[:, to] = encoded_ref[:, at]
    text_ref[...] = matmul(encoded_ref[...], weight_ref[...]).astype(BF16)


def weight_kernel(place_ref, kept_ref, *refs):
    near_refs, far_refs, grad_refs = refs[:3], refs[3:6], refs[6:10]
    kept_sum_ref, sent_refs = refs[10], refs[11:14]
    near = pl.ds(pl.multiple_of(place_ref[2] * HALF_PROMPT, HALF_PROMPT), HALF_PROMPT)
    far = pl.ds(pl.multiple_of((1 - place_ref[2]) * HALF_PROMPT, HALF_PROMPT), HALF_PROMPT)
    for ahead in range(4):
        z_hi = lax.rem(place_ref[3] + ahead, 4)
        at = pl.ds(pl.multiple_of(z_hi * FEATURES, FEATURES), FEATURES)
        total = matmul(grad_refs[0][...], kept_ref[:, at], CONTRACT_FIRST)
        for grad_ref, near_ref, far_ref in zip(grad_refs[1:], near_refs, far_refs):
            total += matmul(grad_ref[near, :], near_ref[:, at], CONTRACT_FIRST)
            total += matmul(grad_ref[far, :], far_ref[:, at], CONTRACT_FIRST)
        if ahead:
            sent_refs[ahead - 1][...] = total.astype(BF16)
        else:
            kept_sum_ref[...] = total


def total_kernel(kept_ref, *refs):
    total = kept_ref[...]
    for part_ref in refs[:3]:
        total += part_ref[...].astype(F32)
    refs[3][...] = total.T


def attention_kernel(
    length_ref,
    order_ref,
    text_ref,
    packed_ref,
    sent_hbm,
    text_grad_ref,
    q_ref,
    k_ref,
    v_ref,
    do_ref,
    out_ref,
    dq_ref,
    dkt_ref,
    dvt_ref,
    sent_ref,
    stored,
):
    length = length_ref[0]
    factor = HEAD_DIM**-0.5
    for role, rows in enumerate((q_ref, k_ref, v_ref)):
        columns = slice(role * HEAD_DIM, (role + 1) * HEAD_DIM)
        rows[:PROMPT, :] = text_ref[:, columns]
        for src in range(HEADS):
            at = PROMPT + src * SHARE
            rows[at : at + SHARE, :] = packed_ref[src, :SHARE, columns]
    for src in range(HEADS):
        at = PROMPT + src * SHARE
        do_ref[at : at + SHARE, :] = packed_ref[src, :SHARE, 3 * HEAD_DIM :]
    for block in range(TEXT_BLOCKS):
        slot = order_ref[block]
        columns = pl.ds(pl.multiple_of((slot % 2) * HEAD_DIM, HEAD_DIM), HEAD_DIM)
        do_ref[block * BLOCK_ROWS : (block + 1) * BLOCK_ROWS, :] = packed_ref[
            slot // 2, SHARE:, columns
        ]
    dkt_ref[...] = jnp.zeros_like(dkt_ref)
    dvt_ref[...] = jnp.zeros_like(dvt_ref)

    def block_rows(step, chain):
        start = (step * CHAINS + chain) * QUERY_BLOCK
        return pl.ds(pl.multiple_of(start, QUERY_BLOCK), QUERY_BLOCK)

    position = lax.broadcasted_iota(jnp.int32, (1, TOTAL), 1)
    live = (position < length) | (position >= PROMPT)

    def body(step, carry):
        places = [block_rows(step, chain) for chain in range(CHAINS)]
        scores = [matmul(q_ref[rows, :], k_ref[...], CONTRACT_LAST) for rows in places]
        weights = []
        for part in scores:
            part = jnp.where(live, part, -1e30)
            maximum = jnp.max(part, axis=-1, keepdims=True)
            weights.append(jnp.exp2((part - maximum) * (factor * LOG2_E)).astype(BF16))
        middle = []
        for rows, part in zip(places, weights):
            inverse = 1.0 / jnp.sum(part.astype(F32), axis=-1, keepdims=True)
            output = matmul(part, v_ref[...]) * inverse
            out_grad = (do_ref[rows, :].astype(F32) * inverse).astype(BF16)
            row_delta = jnp.sum(out_grad.astype(F32) * output, axis=-1, keepdims=True)
            out_ref[rows, :] = output.astype(BF16)
            middle.append((out_grad, row_delta, matmul(out_grad, v_ref[...], CONTRACT_LAST)))
        for rows, part, (out_grad, row_delta, prob_grad) in zip(places, weights, middle):
            score_grad = (part.astype(F32) * (prob_grad - row_delta)).astype(BF16)
            dq_ref[rows, :] = (matmul(score_grad, k_ref[...]) * factor).astype(BF16)
            dkt_ref[...] += matmul(q_ref[rows, :], score_grad, CONTRACT_FIRST)
            dvt_ref[...] += matmul(out_grad, part, CONTRACT_FIRST)
        return carry

    lax.fori_loop(0, TOTAL // (CHAINS * QUERY_BLOCK), body, 0)
    q_ref[...] = (dkt_ref[...] * factor).T.astype(BF16)
    k_ref[...] = dvt_ref[...].T.astype(BF16)
    for place, rows in enumerate((out_ref, dq_ref, q_ref, k_ref)):
        if place:
            text_grad_ref[:, (place - 1) * HEAD_DIM : place * HEAD_DIM] = rows[:PROMPT, :]
    for block in range(TEXT_BLOCKS):
        slot = order_ref[block]
        columns = pl.ds(pl.multiple_of((slot % 2) * HEAD_DIM, HEAD_DIM), HEAD_DIM)
        sent_ref[slot // 2, SHARE:, columns] = out_ref[
            block * BLOCK_ROWS : (block + 1) * BLOCK_ROWS, :
        ]
    stores = []
    for dest in range(HEADS):
        at = PROMPT + dest * SHARE
        for place, rows in enumerate((out_ref, dq_ref, q_ref, k_ref)):
            columns = slice(place * HEAD_DIM, (place + 1) * HEAD_DIM)
            sent_ref[dest, :SHARE, columns] = rows[at : at + SHARE, :]
        sent_ref[dest, SHARE:, 2 * HEAD_DIM :] = jnp.zeros((BLOCK_ROWS, 2 * HEAD_DIM), BF16)
        if dest % 4 == 3:
            group = slice(dest - 3, dest + 1)
            store = pltpu.make_async_copy(
                sent_ref.at[group], sent_hbm.at[group], stored.at[dest // 4]
            )
            store.start()
            stores.append(store)
    for store in stores:
        store.wait()


def attention(length, order, text_rows, packed):
    in_vmem = pl.BlockSpec(memory_space=pltpu.VMEM)
    in_smem = pl.BlockSpec(memory_space=pltpu.SMEM)
    rows = pltpu.VMEM((TOTAL, HEAD_DIM), BF16)
    total = pltpu.VMEM((HEAD_DIM, TOTAL), F32)
    return pl.pallas_call(
        attention_kernel,
        out_shape=[
            jax.ShapeDtypeStruct((HEADS, PACK_ROWS, PACK_COLS), BF16),
            jax.ShapeDtypeStruct((PROMPT, 3 * HEAD_DIM), BF16),
        ],
        in_specs=[in_smem, in_smem, in_vmem, in_vmem],
        out_specs=[pl.BlockSpec(memory_space=pltpu.HBM), in_vmem],
        scratch_shapes=[rows] * 6
        + [total] * 2
        + [pltpu.VMEM((HEADS, PACK_ROWS, PACK_COLS), BF16), pltpu.SemaphoreType.DMA((4,))],
        compiler_params=pltpu.CompilerParams(vmem_limit_bytes=WHOLE_VMEM),
        cost_estimate=pl.CostEstimate(
            flops=360 * TOTAL * TOTAL * HEAD_DIM,
            bytes_accessed=2**29,
            transcendentals=TOTAL * TOTAL,
        ),
    )(length, order, text_rows, packed)


def shift(rows, axis, step):
    size = 2 if axis in ("z_lo", "core") else 4
    return lax.ppermute(rows, axis, [(i, (i + step) % size) for i in range(size)])


def add(*rows):
    return sum(part.astype(F32) for part in rows)


def encode(place, context, residual, weight, gain, packed):
    other_weight = shift(weight, "core", 1)
    other = shift(context, "core", 1)
    other_weight, packed = lax.optimization_barrier((other_weight, packed))
    packed = lax.all_to_all(packed, SEQ, split_axis=0, concat_axis=0, tiled=True)
    chunks = whole_call(
        partial_kernel,
        [rows_of(TEXT_SHARE, WIDTH)] * 8,
        1,
        4,
        [pltpu.VMEM((8 * TEXT_SHARE, 2 * FEATURES), BF16)],
        2 * 8 * TEXT_SHARE * 2 * FEATURES * WIDTH,
        2**23,
    )(place, context, other, weight, other_weight)
    part = dict(zip(CHIPS, chunks))
    from_across = shift(part[2, 1], "z_lo", 1)
    from_below = shift(part[1, 1], "y", 1)
    from_above = shift(part[3, 1], "y", -1)
    below = shift(part[1, 0], "y", 1)
    above = shift(part[3, 0], "y", -1)
    opposite = shift(add(part[2, 0], from_across).astype(BF16), "y", 2)
    across = shift(add(part[0, 1], from_below, from_above).astype(BF16), "z_lo", 1)
    stream = add(residual, part[0, 0], below, above, opposite, across)
    inv_norm = lax.rsqrt(jnp.mean(stream * stream, axis=-1, keepdims=True) + 1e-06)
    encoded = (stream * inv_norm * gain).astype(BF16)
    packed, encoded = lax.optimization_barrier((packed, encoded))
    held = {(0, 0): encoded}
    held[0, 1] = shift(encoded, "z_lo", 1)
    held[3, 0] = shift(encoded, "y", 1)
    held[1, 0] = shift(encoded, "y", -1)
    held[2, 0] = shift(encoded, "y", 2)
    held[3, 1] = shift(held[0, 1], "y", 1)
    held[1, 1] = shift(held[0, 1], "y", -1)
    held[2, 1] = shift(held[2, 0], "z_lo", 1)
    own = [held[chip] for chip in CHIPS]
    return own + [shift(rows, "core", 1) for rows in own], packed


def project(place, blocks, weight):
    columns = weight.shape[1]
    quarter = 4 * FEATURES
    return whole_call(
        text_kernel,
        [rows_of(PROMPT, columns), rows_of(PROMPT, quarter)] + [rows_of(HALF_PROMPT, quarter)] * 3,
        1,
        17,
        [pltpu.VMEM((PROMPT, WIDTH), BF16)],
        2 * PROMPT * WIDTH * columns,
        2**23,
    )(place, *blocks, weight)


def weight_gradient(place, kept, near, far, grads):
    columns = grads[0].shape[1]
    total = jax.ShapeDtypeStruct((columns, FEATURES), F32)
    kept_sum, *sent = whole_call(
        weight_kernel,
        [total] + [rows_of(columns, FEATURES)] * 3,
        1,
        11,
        [],
        2 * 4 * PROMPT * 4 * FEATURES * columns,
        2**23,
    )(place, kept, *near, *far, *grads)
    parts = [shift(rows, "z_hi", step + 1) for step, rows in enumerate(sent)]
    shape = jax.ShapeDtypeStruct((FEATURES, columns), F32)
    return whole_call(total_kernel, shape, 0, 4, [], 0, 2**20)(kept_sum, *parts)


def on_device(
    t5_context,
    t5_resid,
    t5_out_weight,
    t5_gain,
    text_weight,
    prompt_len,
    text_order,
    img_qkv,
    d_img_out,
    d_txt_out,
):
    packed = pack(img_qkv[0], d_img_out[0], d_txt_out[0])
    place = jnp.stack([lax.axis_index(axis) for axis in SEQ + GRP])
    blocks, packed = encode(
        place, t5_context[0], t5_resid[0], t5_out_weight, t5_gain, packed
    )
    text_rows, kept, *slices = project(place, blocks, text_weight)
    near = [shift(rows, "x", step + 1) for step, rows in enumerate(slices)]
    sent, text_grad = attention(prompt_len, text_order[0], text_rows, packed)
    *near, sent = lax.optimization_barrier((*near, sent))
    grads = [text_grad] + [shift(text_grad, "x", step) for step in (1, 2, 3)]
    near, grads = lax.optimization_barrier((near, grads))
    far = [shift(rows, "core", 1) for rows in near]
    text_weight_grad = weight_gradient(place, kept, near, far, grads)
    received = lax.all_to_all(sent, SEQ, split_axis=0, concat_axis=0, tiled=True)
    image_out, text_out, image_qkv_grad = unpack(received)
    return (image_out[None], text_out[None], image_qkv_grad[None], text_weight_grad)


def solution(mesh):
    fine = Mesh(mesh.devices.reshape(4, 4, 4, 2, 2), GRP + SEQ)
    in_specs = (
        P(GRP, None, SEQ),
        P(GRP, SEQ, None),
        P(SEQ, None),
        P(),
        P(None, SEQ),
        P(GRP),
        P(GRP, None),
        P(GRP, SEQ, None),
        P(GRP, SEQ, None),
        P(GRP, SEQ, None),
    )
    out_specs = (
        P(GRP, SEQ, None),
        P(GRP, SEQ, None),
        P(GRP, SEQ, None),
        P(GRP, SEQ),
    )
    return jax.shard_map(
        on_device, mesh=fine, in_specs=in_specs, out_specs=out_specs, check_vma=False
    )
```

```python
import jax
import jax.numpy as jnp
from jax import lax
from jax.experimental import pallas as pl
from jax.experimental.pallas import tpu as pltpu
from jax.sharding import Mesh
from jax.sharding import PartitionSpec as P

HEAD_DIM = 128
HEADS = 16
PROMPT = 512
IMAGE = 2048
TOTAL = PROMPT + IMAGE
BLOCK_ROWS = 16
TEXT_BLOCKS = 32
SHARE = IMAGE // HEADS
PACK_ROWS = SHARE + BLOCK_ROWS
PACK_COLS = 4 * HEAD_DIM
QUERY_BLOCK = 256
EXPONENT = HEAD_DIM**-0.5 * 1.4426950408889634
FORWARD_ROWS = 512
PACK_HEADS = 4
CHAINS = 2
WIDTH = 4096
FEATURES = WIDTH // HEADS
TEXT_SHARE = PROMPT // HEADS
HALF_PROMPT = PROMPT // 2
CHIPS = [(ahead, across) for ahead in range(4) for across in range(2)]

BF16 = jnp.bfloat16
F32 = jnp.float32
SEQ = ("y", "z_lo", "core")
GRP = ("z_hi", "x")
CONTRACT_LAST = (((1,), (1,)), ((), ()))
CONTRACT_FIRST = (((0,), (0,)), ((), ()))
VMEM_LIMIT = 48 * 2**20
WHOLE_VMEM = 60 * 2**20


def matmul(a, b, dims=(((1,), (0,)), ((), ()))):
    return lax.dot_general(a, b, dims, preferred_element_type=F32)


def pack_kernel(qkv_hbm, grad_hbm, text_hbm, packed_hbm, *refs):
    qkv_ref, grad_ref, text_ref, packed_ref, loaded, stored = refs
    loads = []
    for source, target in ((grad_hbm, grad_ref), (text_hbm, text_ref)):
        loads.append(pltpu.make_async_copy(source, target, loaded.at[len(loads)]))
    width = 3 * HEAD_DIM * PACK_HEADS
    for group in range(HEADS // PACK_HEADS):
        columns = slice(group * width, (group + 1) * width)
        source, target = qkv_hbm.at[:, columns], qkv_ref.at[:, columns]
        loads.append(pltpu.make_async_copy(source, target, loaded.at[len(loads)]))
    for load in loads:
        load.start()
    loads[0].wait()
    loads[1].wait()
    stores = []
    for group in range(HEADS // PACK_HEADS):
        loads[2 + group].wait()
        heads = slice(group * PACK_HEADS, (group + 1) * PACK_HEADS)
        for head in range(heads.start, heads.stop):
            columns = slice(head * HEAD_DIM, (head + 1) * HEAD_DIM)
            wide = slice(3 * head * HEAD_DIM, 3 * (head + 1) * HEAD_DIM)
            packed_ref[head, :SHARE, : 3 * HEAD_DIM] = qkv_ref[:, wide]
            packed_ref[head, :SHARE, 3 * HEAD_DIM :] = grad_ref[:, columns]
            packed_ref[head, SHARE:, :HEAD_DIM] = text_ref[:BLOCK_ROWS, columns]
            packed_ref[head, SHARE:, HEAD_DIM : 2 * HEAD_DIM] = text_ref[BLOCK_ROWS:, columns]
            packed_ref[head, SHARE:, 2 * HEAD_DIM :] = jnp.zeros(
                (BLOCK_ROWS, 2 * HEAD_DIM), BF16
            )
        store = pltpu.make_async_copy(
            packed_ref.at[heads], packed_hbm.at[heads], stored.at[group]
        )
        store.start()
        stores.append(store)
    for store in stores:
        store.wait()


def unpack_kernel(packed_ref, out_ref, text_ref, qkv_ref):
    for head in range(HEADS):
        columns = slice(head * HEAD_DIM, (head + 1) * HEAD_DIM)
        wide = slice(3 * head * HEAD_DIM, 3 * (head + 1) * HEAD_DIM)
        out_ref[:, columns] = packed_ref[head, :SHARE, :HEAD_DIM]
        qkv_ref[:, wide] = packed_ref[head, :SHARE, HEAD_DIM:]
        text_ref[:BLOCK_ROWS, columns] = packed_ref[head, SHARE:, :HEAD_DIM]
        text_ref[BLOCK_ROWS:, columns] = packed_ref[head, SHARE:, HEAD_DIM : 2 * HEAD_DIM]


def whole_call(kernel, out_shape, smem_inputs, vmem_inputs, scratch, flops, moved):
    in_vmem = pl.BlockSpec(memory_space=pltpu.VMEM)
    in_smem = pl.BlockSpec(memory_space=pltpu.SMEM)
    return pl.pallas_call(
        kernel,
        out_shape=out_shape,
        in_specs=[in_smem] * smem_inputs + [in_vmem] * vmem_inputs,
        out_specs=jax.tree.map(lambda _: in_vmem, out_shape),
        scratch_shapes=scratch,
        compiler_params=pltpu.CompilerParams(vmem_limit_bytes=VMEM_LIMIT),
        cost_estimate=pl.CostEstimate(flops=flops, bytes_accessed=moved, transcendentals=0),
    )


def rows_of(*shape):
    return jax.ShapeDtypeStruct(shape, BF16)


def pack(qkv, grad, text):
    anywhere = pl.BlockSpec(memory_space=pltpu.HBM)
    groups = HEADS // PACK_HEADS
    return pl.pallas_call(
        pack_kernel,
        out_shape=rows_of(HEADS, PACK_ROWS, PACK_COLS),
        in_specs=[anywhere] * 3,
        out_specs=anywhere,
        scratch_shapes=[
            pltpu.VMEM(qkv.shape, BF16),
            pltpu.VMEM(grad.shape, BF16),
            pltpu.VMEM(text.shape, BF16),
            pltpu.VMEM((HEADS, PACK_ROWS, PACK_COLS), BF16),
            pltpu.SemaphoreType.DMA((2 + groups,)),
            pltpu.SemaphoreType.DMA((groups,)),
        ],
        compiler_params=pltpu.CompilerParams(vmem_limit_bytes=WHOLE_VMEM),
        cost_estimate=pl.CostEstimate(flops=0, bytes_accessed=2**22, transcendentals=0),
    )(qkv, grad, text)


def unpack(packed):
    shapes = [
        rows_of(SHARE, HEADS * HEAD_DIM),
        rows_of(2 * BLOCK_ROWS, HEADS * HEAD_DIM),
        rows_of(SHARE, HEADS * 3 * HEAD_DIM),
    ]
    return whole_call(unpack_kernel, shapes, 0, 1, [], 0, 2**22)(packed)


def row_block(place_ref, ahead, across, other_core):
    y = lax.rem(place_ref[0] + ahead, 4)
    z = 1 - place_ref[1] if across else place_ref[1]
    core = 1 - place_ref[2] if other_core else place_ref[2]
    return (y * 2 + z) * 2 + core


def partial_kernel(place_ref, own_ref, other_ref, own_weight_ref, other_weight_ref, *refs):
    chunk_refs, rows_ref = refs[:8], refs[8]
    for index, (ahead, across) in enumerate(CHIPS):
        block = row_block(place_ref, ahead, across, False)
        rows = pl.ds(pl.multiple_of(block * TEXT_SHARE, TEXT_SHARE), TEXT_SHARE)
        to = slice(index * TEXT_SHARE, (index + 1) * TEXT_SHARE)
        rows_ref[to, :FEATURES] = own_ref[rows, :]
        rows_ref[to, FEATURES:] = other_ref[rows, :]

    def body(step, carry):
        columns = pl.ds(pl.multiple_of(step * 512, 512), 512)
        sums = matmul(rows_ref[:, :FEATURES], own_weight_ref[:, columns])
        sums += matmul(rows_ref[:, FEATURES:], other_weight_ref[:, columns])
        for index, chunk_ref in enumerate(chunk_refs):
            rows = slice(index * TEXT_SHARE, (index + 1) * TEXT_SHARE)
            chunk_ref[:, columns] = sums[rows].astype(BF16)
        return carry

    lax.fori_loop(0, WIDTH // 512, body, 0)


def text_kernel(place_ref, *refs):
    block_refs, weight_ref, text_ref = refs[:16], refs[16], refs[17]
    kept_ref, sent_refs, encoded_ref = refs[18], refs[19:22], refs[22]
    for index, block_ref in enumerate(block_refs):
        ahead, across = CHIPS[index % 8]
        block = row_block(place_ref, ahead, across, index >= 8)
        rows = pl.ds(pl.multiple_of(block * TEXT_SHARE, TEXT_SHARE), TEXT_SHARE)
        encoded_ref[rows, :] = block_ref[...]
    half = pl.ds(pl.multiple_of(place_ref[2] * HALF_PROMPT, HALF_PROMPT), HALF_PROMPT)
    for ahead in range(4):
        x = lax.rem(place_ref[4] + ahead, 4)
        for z_hi in range(4):
            at = pl.ds(pl.multiple_of((z_hi * 4 + x) * FEATURES, FEATURES), FEATURES)
            to = slice(z_hi * FEATURES, (z_hi + 1) * FEATURES)
            if ahead:
                sent_refs[ahead - 1][:, to] = encoded_ref[half, at]
            else:
                kept_ref[:, to] = encoded_ref[:, at]
    text_ref[...] = matmul(encoded_ref[...], weight_ref[...]).astype(BF16)


def weight_kernel(place_ref, kept_ref, *refs):
    near_refs, far_refs, grad_refs = refs[:3], refs[3:6], refs[6:10]
    kept_sum_ref, sent_refs = refs[10], refs[11:14]
    near = pl.ds(pl.multiple_of(place_ref[2] * HALF_PROMPT, HALF_PROMPT), HALF_PROMPT)
    far = pl.ds(pl.multiple_of((1 - place_ref[2]) * HALF_PROMPT, HALF_PROMPT), HALF_PROMPT)
    for ahead in range(4):
        z_hi = lax.rem(place_ref[3] + ahead, 4)
        at = pl.ds(pl.multiple_of(z_hi * FEATURES, FEATURES), FEATURES)
        total = matmul(grad_refs[0][...], kept_ref[:, at], CONTRACT_FIRST)
        for grad_ref, near_ref, far_ref in zip(grad_refs[1:], near_refs, far_refs):
            total += matmul(grad_ref[near, :], near_ref[:, at], CONTRACT_FIRST)
            total += matmul(grad_ref[far, :], far_ref[:, at], CONTRACT_FIRST)
        if ahead:
            sent_refs[ahead - 1][...] = total.astype(BF16)
        else:
            kept_sum_ref[...] = total


def total_kernel(kept_ref, *refs):
    total = kept_ref[...]
    for part_ref in refs[:3]:
        total += part_ref[...].astype(F32)
    refs[3][...] = total.T


def exp_rows(scores, maximum):
    return jnp.exp2((scores - maximum) * EXPONENT).astype(BF16)


def spread(rows, columns):
    return jnp.concatenate([rows] * (columns // HEAD_DIM), axis=1)


def row_sums(out_grad, output):
    total = jnp.sum(out_grad.astype(F32) * output, axis=-1, keepdims=True)
    return jnp.broadcast_to(total, output.shape)


def score_gradient(weights, prob_grad, row_delta):
    wide = spread(row_delta, weights.shape[1])
    return (weights.astype(F32) * (prob_grad - wide)).astype(BF16)


def chains(count, first, then):
    ahead = first(0)
    for chain in range(count):
        current = ahead
        if chain + 1 < count:
            ahead = first(chain + 1)
        then(chain, current)


def chain_rows(chain):
    return slice(chain * QUERY_BLOCK, (chain + 1) * QUERY_BLOCK)


def image_forward_kernel(
    order_ref,
    packed_ref,
    weights_ref,
    rows_ref,
    output_ref,
    maximum_ref,
    total_ref,
    text_do_ref,
    k_ref,
    v_ref,
):
    step = pl.program_id(0)

    @pl.when(step == 0)
    def _():
        v_ref[:, HEAD_DIM:] = jnp.ones((IMAGE, HEAD_DIM), BF16)
        for src in range(HEADS):
            at = slice(src * SHARE, (src + 1) * SHARE)
            k_ref[at, :] = packed_ref[src, :SHARE, HEAD_DIM : 2 * HEAD_DIM]
            v_ref[at, :HEAD_DIM] = packed_ref[src, :SHARE, 2 * HEAD_DIM : 3 * HEAD_DIM]
        for block in range(TEXT_BLOCKS):
            slot = order_ref[block]
            columns = pl.ds(pl.multiple_of((slot % 2) * HEAD_DIM, HEAD_DIM), HEAD_DIM)
            text_do_ref[block * BLOCK_ROWS : (block + 1) * BLOCK_ROWS, :] = packed_ref[
                slot // 2, SHARE:, columns
            ]

    parts = FORWARD_ROWS // SHARE
    for part in range(parts):
        at = slice(part * SHARE, (part + 1) * SHARE)
        rows_ref[at, :] = packed_ref[step * parts + part, :SHARE, :]

    def first(chain):
        return matmul(rows_ref[chain_rows(chain), :HEAD_DIM], k_ref[...], CONTRACT_LAST)

    def then(chain, scores):
        at = chain_rows(chain)
        maximum = jnp.max(scores, axis=-1, keepdims=True)
        weights = exp_rows(scores, maximum)
        weights_ref[at, :] = weights
        both = matmul(weights, v_ref[...])
        output_ref[at, :] = both[:, :HEAD_DIM]
        total_ref[at, :] = both[:, HEAD_DIM:]
        maximum_ref[at, :] = jnp.broadcast_to(maximum, (QUERY_BLOCK, HEAD_DIM))

    chains(FORWARD_ROWS // QUERY_BLOCK, first, then)


def attention_kernel(
    length_ref,
    order_ref,
    text_ref,
    text_do_ref,
    rows_ref,
    weights_ref,
    output_ref,
    maximum_ref,
    total_ref,
    sent_hbm,
    text_grad_ref,
    sent_ref,
    dkt_ref,
    dvt_ref,
    image_dkt_ref,
    image_dvt_ref,
    tv_ref,
    stored,
):
    step = pl.program_id(0)
    factor = HEAD_DIM**-0.5
    text_keys = text_ref[:, HEAD_DIM : 2 * HEAD_DIM]
    text_values = text_ref[:, 2 * HEAD_DIM :]
    keys = rows_ref[:, HEAD_DIM : 2 * HEAD_DIM]
    values = rows_ref[:, 2 * HEAD_DIM : 3 * HEAD_DIM]
    live = lax.broadcasted_iota(jnp.int32, (1, PROMPT), 1) < length_ref[0]
    sums = (dkt_ref, dvt_ref, image_dkt_ref, image_dvt_ref)

    def text_scores(queries):
        return jnp.where(live, matmul(queries, text_keys, CONTRACT_LAST), -1e30)

    @pl.when(step == 0)
    def _():
        tv_ref[:, :HEAD_DIM] = text_values
        tv_ref[:, HEAD_DIM:] = jnp.ones((PROMPT, HEAD_DIM), BF16)
        sent_ref[:, SHARE:, 2 * HEAD_DIM :] = jnp.zeros((HEADS, BLOCK_ROWS, 2 * HEAD_DIM), BF16)
        places = [chain_rows(chain) for chain in range(CHAINS)]
        scores = []
        for rows in places:
            queries = text_ref[rows, :HEAD_DIM]
            scores.append((text_scores(queries), matmul(queries, keys, CONTRACT_LAST)))
        weights = []
        for to_text, to_image in scores:
            maximum = jnp.maximum(
                jnp.max(to_text, axis=-1, keepdims=True), jnp.max(to_image, axis=-1, keepdims=True)
            )
            weights.append((exp_rows(to_text, maximum), exp_rows(to_image, maximum)))
        middle = []
        for rows, (text_weights, image_weights) in zip(places, weights):
            total = jnp.sum(image_weights.astype(F32), axis=-1, keepdims=True)
            both = matmul(text_weights, tv_ref[...])
            inverse = 1.0 / (both[:, HEAD_DIM:] + total)
            output = (both[:, :HEAD_DIM] + matmul(image_weights, values)) * inverse
            out_grad = (text_do_ref[rows, :].astype(F32) * inverse).astype(BF16)
            prob_grads = [matmul(out_grad, part, CONTRACT_LAST) for part in (text_values, values)]
            middle.append((output, out_grad, row_sums(out_grad, output), prob_grads))
        for chain, rows in enumerate(places):
            text_weights, image_weights = weights[chain]
            output, out_grad, row_delta, prob_grads = middle[chain]
            queries = text_ref[rows, :HEAD_DIM]
            text_scored = score_gradient(text_weights, prob_grads[0], row_delta)
            image_scored = score_gradient(image_weights, prob_grads[1], row_delta)
            query_grad = matmul(text_scored, text_keys) + matmul(image_scored, keys)
            text_grad_ref[rows, :HEAD_DIM] = (query_grad * factor).astype(BF16)
            products = (
                matmul(queries, text_scored, CONTRACT_FIRST),
                matmul(out_grad, text_weights, CONTRACT_FIRST),
                matmul(queries, image_scored, CONTRACT_FIRST),
                matmul(out_grad, image_weights, CONTRACT_FIRST),
            )
            for sum_ref, product in zip(sums, products):
                sum_ref[...] = sum_ref[...] + product if chain else product
            output = output.astype(BF16)
            blocks = QUERY_BLOCK // BLOCK_ROWS
            for block in range(blocks):
                slot = order_ref[chain * blocks + block]
                columns = pl.ds(pl.multiple_of((slot % 2) * HEAD_DIM, HEAD_DIM), HEAD_DIM)
                sent_ref[slot // 2, SHARE:, columns] = output[
                    block * BLOCK_ROWS : (block + 1) * BLOCK_ROWS
                ]

    @pl.when(step > 0)
    def _():
        def place(chain):
            start = (step - 1) * FORWARD_ROWS + chain * QUERY_BLOCK
            return pl.ds(pl.multiple_of(start, QUERY_BLOCK), QUERY_BLOCK)

        places = [chain_rows(chain) for chain in range(CHAINS)]
        scores = [text_scores(rows_ref[place(chain), :HEAD_DIM]) for chain in range(CHAINS)]
        weights = []
        for at, to_text in zip(places, scores):
            image_maximum = maximum_ref[at, :]
            maximum = jnp.maximum(image_maximum, jnp.max(to_text, axis=-1, keepdims=True))
            scale = jnp.exp2((image_maximum - maximum) * EXPONENT)
            weights.append((exp_rows(to_text, spread(maximum, PROMPT)), scale))
        middle = []
        for chain, (at, (text_weights, scale)) in enumerate(zip(places, weights)):
            both = matmul(text_weights, tv_ref[...])
            inverse = 1.0 / (both[:, HEAD_DIM:] + scale * total_ref[at, :])
            output = (scale * output_ref[at, :] + both[:, :HEAD_DIM]) * inverse
            cotangent = rows_ref[place(chain), 3 * HEAD_DIM :].astype(F32)
            out_grad = (cotangent * inverse).astype(BF16)
            image_out_grad = (cotangent * (scale * inverse)).astype(BF16)
            prob_grad = matmul(out_grad, text_values, CONTRACT_LAST)
            image_prob_grad = matmul(image_out_grad, values, CONTRACT_LAST)
            middle.append(
                (
                    (out_grad, row_sums(out_grad, output), prob_grad),
                    (image_out_grad, row_sums(image_out_grad, output), image_prob_grad),
                )
            )
            output = output.astype(BF16)
            for part in range(QUERY_BLOCK // SHARE):
                dest = ((step - 1) * FORWARD_ROWS + chain * QUERY_BLOCK) // SHARE + part
                sent_ref[dest, :SHARE, :HEAD_DIM] = output[part * SHARE : (part + 1) * SHARE]
        for chain, at in enumerate(places):
            queries = rows_ref[place(chain), :HEAD_DIM]
            (out_grad, row_delta, prob_grad), image_parts = middle[chain]
            image_out_grad, image_delta, image_prob_grad = image_parts
            text_weights, image_weights = weights[chain][0], weights_ref[at, :]
            text_scored = score_gradient(text_weights, prob_grad, row_delta)
            image_scored = score_gradient(image_weights, image_prob_grad, image_delta)
            query_grad = matmul(text_scored, text_keys) + matmul(image_scored, keys)
            query_grad = (query_grad * factor).astype(BF16)
            for part in range(QUERY_BLOCK // SHARE):
                dest = ((step - 1) * FORWARD_ROWS + chain * QUERY_BLOCK) // SHARE + part
                sent_ref[dest, :SHARE, HEAD_DIM : 2 * HEAD_DIM] = query_grad[
                    part * SHARE : (part + 1) * SHARE
                ]
            dkt_ref[...] += matmul(queries, text_scored, CONTRACT_FIRST)
            dvt_ref[...] += matmul(out_grad, text_weights, CONTRACT_FIRST)
            image_dkt_ref[...] += matmul(queries, image_scored, CONTRACT_FIRST)
            image_dvt_ref[...] += matmul(image_out_grad, image_weights, CONTRACT_FIRST)

    @pl.when(step == IMAGE // FORWARD_ROWS)
    def _():
        text_grad_ref[:, HEAD_DIM : 2 * HEAD_DIM] = (dkt_ref[...] * factor).T.astype(BF16)
        text_grad_ref[:, 2 * HEAD_DIM :] = dvt_ref[...].T.astype(BF16)
        stores = []
        for dest in range(HEADS):
            at = slice(dest * SHARE, (dest + 1) * SHARE)
            sent_ref[dest, :SHARE, 2 * HEAD_DIM : 3 * HEAD_DIM] = (
                (image_dkt_ref[:, at] * factor).T.astype(BF16)
            )
            sent_ref[dest, :SHARE, 3 * HEAD_DIM :] = image_dvt_ref[:, at].T.astype(BF16)
            if dest % 4 == 3:
                group = slice(dest - 3, dest + 1)
                store = pltpu.make_async_copy(
                    sent_ref.at[group], sent_hbm.at[group], stored.at[dest // 4]
                )
                store.start()
                stores.append(store)
        for store in stores:
            store.wait()


def grid_call(kernel, steps, in_specs, out_shape, out_specs, scratch, products):
    return pl.pallas_call(
        kernel,
        grid=(steps,),
        out_shape=out_shape,
        in_specs=in_specs,
        out_specs=out_specs,
        scratch_shapes=scratch,
        compiler_params=pltpu.CompilerParams(vmem_limit_bytes=WHOLE_VMEM),
        cost_estimate=pl.CostEstimate(
            flops=60 * products * HEAD_DIM, bytes_accessed=2**29, transcendentals=0
        ),
    )


IN_SMEM = pl.BlockSpec(memory_space=pltpu.SMEM)


def fixed(*shape):
    return pl.BlockSpec(shape, lambda step: (0,) * len(shape))


def per_block(rows, columns, skip=0):
    return pl.BlockSpec((rows, columns), lambda step: (jnp.maximum(step - skip, 0), 0))


def image_forward(order, packed):
    floats = jax.ShapeDtypeStruct((IMAGE, HEAD_DIM), F32)
    block = per_block(FORWARD_ROWS, HEAD_DIM)
    return grid_call(
        image_forward_kernel,
        IMAGE // FORWARD_ROWS,
        [IN_SMEM, fixed(HEADS, PACK_ROWS, PACK_COLS)],
        [rows_of(IMAGE, IMAGE), rows_of(IMAGE, PACK_COLS)] + [floats] * 3
        + [rows_of(PROMPT, HEAD_DIM)],
        [per_block(FORWARD_ROWS, IMAGE), per_block(FORWARD_ROWS, PACK_COLS)] + [block] * 3
        + [fixed(PROMPT, HEAD_DIM)],
        [pltpu.VMEM((IMAGE, HEAD_DIM), BF16), pltpu.VMEM((IMAGE, 2 * HEAD_DIM), BF16)],
        2 * IMAGE * IMAGE,
    )(order, packed)


def attention(length, order, text_rows, text_do, rows, weights, output, maximum, total):
    block = per_block(FORWARD_ROWS, HEAD_DIM, 1)
    text_sum = pltpu.VMEM((HEAD_DIM, PROMPT), F32)
    image_sum = pltpu.VMEM((HEAD_DIM, IMAGE), F32)
    return grid_call(
        attention_kernel,
        1 + IMAGE // FORWARD_ROWS,
        [IN_SMEM, IN_SMEM, fixed(PROMPT, 3 * HEAD_DIM), fixed(PROMPT, HEAD_DIM)]
        + [fixed(IMAGE, PACK_COLS), per_block(FORWARD_ROWS, IMAGE, 1)] + [block] * 3,
        [rows_of(HEADS, PACK_ROWS, PACK_COLS), rows_of(PROMPT, 3 * HEAD_DIM)],
        [pl.BlockSpec(memory_space=pltpu.HBM), fixed(PROMPT, 3 * HEAD_DIM)],
        [pltpu.VMEM((HEADS, PACK_ROWS, PACK_COLS), BF16), text_sum, text_sum, image_sum, image_sum]
        + [pltpu.VMEM((PROMPT, 2 * HEAD_DIM), BF16), pltpu.SemaphoreType.DMA((4,))],
        6 * TOTAL * TOTAL - 2 * IMAGE * IMAGE,
    )(length, order, text_rows, text_do, rows, weights, output, maximum, total)


def shift(rows, axis, step):
    size = 2 if axis in ("z_lo", "core") else 4
    return lax.ppermute(rows, axis, [(i, (i + step) % size) for i in range(size)])


def add(*rows):
    return sum(part.astype(F32) for part in rows)


def encode(place, context, residual, weight, gain, packed, order):
    other_weight = shift(weight, "core", 1)
    other = shift(context, "core", 1)
    other_weight, packed = lax.optimization_barrier((other_weight, packed))
    packed = lax.all_to_all(packed, SEQ, split_axis=0, concat_axis=0, tiled=True)
    chunks = whole_call(
        partial_kernel,
        [rows_of(TEXT_SHARE, WIDTH)] * 8,
        1,
        4,
        [pltpu.VMEM((8 * TEXT_SHARE, 2 * FEATURES), BF16)],
        2 * 8 * TEXT_SHARE * 2 * FEATURES * WIDTH,
        2**23,
    )(place, context, other, weight, other_weight)
    part = dict(zip(CHIPS, chunks))
    from_across = shift(part[2, 1], "z_lo", 1)
    from_below = shift(part[1, 1], "y", 1)
    from_above = shift(part[3, 1], "y", -1)
    below = shift(part[1, 0], "y", 1)
    above = shift(part[3, 0], "y", -1)
    opposite = add(part[2, 0], from_across).astype(BF16)
    across = add(part[0, 1], from_below, from_above).astype(BF16)
    packed, opposite, across = lax.optimization_barrier((packed, opposite, across))
    forward = image_forward(order, packed)
    opposite = shift(opposite, "y", 2)
    across = shift(across, "z_lo", 1)
    forward, opposite, across = lax.optimization_barrier((forward, opposite, across))
    stream = add(residual, part[0, 0], below, above, opposite, across)
    inv_norm = lax.rsqrt(jnp.mean(stream * stream, axis=-1, keepdims=True) + 1e-06)
    encoded = (stream * inv_norm * gain).astype(BF16)
    held = {(0, 0): encoded}
    held[0, 1] = shift(encoded, "z_lo", 1)
    held[3, 0] = shift(encoded, "y", 1)
    held[1, 0] = shift(encoded, "y", -1)
    held[2, 0] = shift(encoded, "y", 2)
    held[3, 1] = shift(held[0, 1], "y", 1)
    held[1, 1] = shift(held[0, 1], "y", -1)
    held[2, 1] = shift(held[2, 0], "z_lo", 1)
    own = [held[chip] for chip in CHIPS]
    return own + [shift(rows, "core", 1) for rows in own], forward


def project(place, blocks, weight):
    columns = weight.shape[1]
    quarter = 4 * FEATURES
    return whole_call(
        text_kernel,
        [rows_of(PROMPT, columns), rows_of(PROMPT, quarter)] + [rows_of(HALF_PROMPT, quarter)] * 3,
        1,
        17,
        [pltpu.VMEM((PROMPT, WIDTH), BF16)],
        2 * PROMPT * WIDTH * columns,
        2**23,
    )(place, *blocks, weight)


def weight_gradient(place, kept, near, far, grads):
    columns = grads[0].shape[1]
    total = jax.ShapeDtypeStruct((columns, FEATURES), F32)
    kept_sum, *sent = whole_call(
        weight_kernel,
        [total] + [rows_of(columns, FEATURES)] * 3,
        1,
        11,
        [],
        24 * 2 * 4 * PROMPT * 4 * FEATURES * columns,
        2**23,
    )(place, kept, *near, *far, *grads)
    parts = [shift(rows, "z_hi", step + 1) for step, rows in enumerate(sent)]
    shape = jax.ShapeDtypeStruct((FEATURES, columns), F32)
    return whole_call(total_kernel, shape, 0, 4, [], 0, 2**20)(kept_sum, *parts)


def on_device(
    t5_context,
    t5_resid,
    t5_out_weight,
    t5_gain,
    text_weight,
    prompt_len,
    text_order,
    img_qkv,
    d_img_out,
    d_txt_out,
):
    packed = pack(img_qkv[0], d_img_out[0], d_txt_out[0])
    place = jnp.stack([lax.axis_index(axis) for axis in SEQ + GRP])
    blocks, forward = encode(
        place, t5_context[0], t5_resid[0], t5_out_weight, t5_gain, packed, text_order[0]
    )
    weights, rows, *stats, text_do = forward
    text_rows, kept, *slices = project(place, blocks, text_weight)
    near = [shift(rows, "x", step + 1) for step, rows in enumerate(slices)]
    sent, text_grad = attention(
        prompt_len, text_order[0], text_rows, text_do, rows, weights, *stats
    )
    *near, sent = lax.optimization_barrier((*near, sent))
    grads = [text_grad] + [shift(text_grad, "x", step) for step in (1, 2, 3)]
    near, grads = lax.optimization_barrier((near, grads))
    far = [shift(rows, "core", 1) for rows in near]
    text_weight_grad = weight_gradient(place, kept, near, far, grads)
    received = lax.all_to_all(sent, SEQ, split_axis=0, concat_axis=0, tiled=True)
    image_out, text_out, image_qkv_grad = unpack(received)
    return (image_out[None], text_out[None], image_qkv_grad[None], text_weight_grad)


def solution(mesh):
    fine = Mesh(mesh.devices.reshape(4, 4, 4, 2, 2), GRP + SEQ)
    in_specs = (
        P(GRP, None, SEQ),
        P(GRP, SEQ, None),
        P(SEQ, None),
        P(),
        P(None, SEQ),
        P(GRP),
        P(GRP, None),
        P(GRP, SEQ, None),
        P(GRP, SEQ, None),
        P(GRP, SEQ, None),
    )
    out_specs = (
        P(GRP, SEQ, None),
        P(GRP, SEQ, None),
        P(GRP, SEQ, None),
        P(GRP, SEQ),
    )
    return jax.shard_map(
        on_device, mesh=fine, in_specs=in_specs, out_specs=out_specs, check_vma=False
    )
```

```python
import jax
import jax.numpy as jnp
from jax import lax
from jax.experimental import pallas as pl
from jax.experimental.pallas import tpu as pltpu
from jax.sharding import Mesh
from jax.sharding import PartitionSpec as P

HEAD_DIM = 128
HEADS = 16
PROMPT = 512
IMAGE = 2048
TOTAL = PROMPT + IMAGE
BLOCK_ROWS = 16
TEXT_BLOCKS = 32
SHARE = IMAGE // HEADS
PACK_ROWS = SHARE + BLOCK_ROWS
PACK_COLS = 4 * HEAD_DIM
QUERY_BLOCK = 256
EXPONENT = HEAD_DIM**-0.5 * 1.4426950408889634
FORWARD_ROWS = 512
PACK_HEADS = 4
CHAINS = 2
WIDTH = 4096
FEATURES = WIDTH // HEADS
TEXT_SHARE = PROMPT // HEADS
HALF_PROMPT = PROMPT // 2
CHIPS = [(ahead, across) for ahead in range(4) for across in range(2)]

BF16 = jnp.bfloat16
F32 = jnp.float32
SEQ = ("y", "z_lo", "core")
GRP = ("z_hi", "x")
CONTRACT_LAST = (((1,), (1,)), ((), ()))
CONTRACT_FIRST = (((0,), (0,)), ((), ()))
VMEM_LIMIT = 48 * 2**20
WHOLE_VMEM = 60 * 2**20


def matmul(a, b, dims=(((1,), (0,)), ((), ()))):
    return lax.dot_general(a, b, dims, preferred_element_type=F32)


def pack_kernel(qkv_hbm, grad_hbm, text_hbm, packed_hbm, *refs):
    qkv_ref, grad_ref, text_ref, packed_ref, loaded, stored = refs
    loads = []
    for source, target in ((grad_hbm, grad_ref), (text_hbm, text_ref)):
        loads.append(pltpu.make_async_copy(source, target, loaded.at[len(loads)]))
    width = 3 * HEAD_DIM * PACK_HEADS
    for group in range(HEADS // PACK_HEADS):
        columns = slice(group * width, (group + 1) * width)
        source, target = qkv_hbm.at[:, columns], qkv_ref.at[:, columns]
        loads.append(pltpu.make_async_copy(source, target, loaded.at[len(loads)]))
    for load in loads:
        load.start()
    loads[0].wait()
    loads[1].wait()
    stores = []
    for group in range(HEADS // PACK_HEADS):
        loads[2 + group].wait()
        heads = slice(group * PACK_HEADS, (group + 1) * PACK_HEADS)
        for head in range(heads.start, heads.stop):
            columns = slice(head * HEAD_DIM, (head + 1) * HEAD_DIM)
            wide = slice(3 * head * HEAD_DIM, 3 * (head + 1) * HEAD_DIM)
            packed_ref[head, :SHARE, : 3 * HEAD_DIM] = qkv_ref[:, wide]
            packed_ref[head, :SHARE, 3 * HEAD_DIM :] = grad_ref[:, columns]
            packed_ref[head, SHARE:, :HEAD_DIM] = text_ref[:BLOCK_ROWS, columns]
            packed_ref[head, SHARE:, HEAD_DIM : 2 * HEAD_DIM] = text_ref[BLOCK_ROWS:, columns]
            packed_ref[head, SHARE:, 2 * HEAD_DIM :] = jnp.zeros(
                (BLOCK_ROWS, 2 * HEAD_DIM), BF16
            )
        store = pltpu.make_async_copy(
            packed_ref.at[heads], packed_hbm.at[heads], stored.at[group]
        )
        store.start()
        stores.append(store)
    for store in stores:
        store.wait()


def unpack_kernel(packed_ref, out_ref, text_ref, qkv_ref):
    for head in range(HEADS):
        columns = slice(head * HEAD_DIM, (head + 1) * HEAD_DIM)
        wide = slice(3 * head * HEAD_DIM, 3 * (head + 1) * HEAD_DIM)
        out_ref[:, columns] = packed_ref[head, :SHARE, :HEAD_DIM]
        qkv_ref[:, wide] = packed_ref[head, :SHARE, HEAD_DIM:]
        text_ref[:BLOCK_ROWS, columns] = packed_ref[head, SHARE:, :HEAD_DIM]
        text_ref[BLOCK_ROWS:, columns] = packed_ref[head, SHARE:, HEAD_DIM : 2 * HEAD_DIM]


def whole_call(kernel, out_shape, smem_inputs, vmem_inputs, scratch, flops, moved):
    in_vmem = pl.BlockSpec(memory_space=pltpu.VMEM)
    in_smem = pl.BlockSpec(memory_space=pltpu.SMEM)
    return pl.pallas_call(
        kernel,
        out_shape=out_shape,
        in_specs=[in_smem] * smem_inputs + [in_vmem] * vmem_inputs,
        out_specs=jax.tree.map(lambda _: in_vmem, out_shape),
        scratch_shapes=scratch,
        compiler_params=pltpu.CompilerParams(vmem_limit_bytes=VMEM_LIMIT),
        cost_estimate=pl.CostEstimate(flops=flops, bytes_accessed=moved, transcendentals=0),
    )


def rows_of(*shape):
    return jax.ShapeDtypeStruct(shape, BF16)


def pack(qkv, grad, text):
    anywhere = pl.BlockSpec(memory_space=pltpu.HBM)
    groups = HEADS // PACK_HEADS
    return pl.pallas_call(
        pack_kernel,
        out_shape=rows_of(HEADS, PACK_ROWS, PACK_COLS),
        in_specs=[anywhere] * 3,
        out_specs=anywhere,
        scratch_shapes=[
            pltpu.VMEM(qkv.shape, BF16),
            pltpu.VMEM(grad.shape, BF16),
            pltpu.VMEM(text.shape, BF16),
            pltpu.VMEM((HEADS, PACK_ROWS, PACK_COLS), BF16),
            pltpu.SemaphoreType.DMA((2 + groups,)),
            pltpu.SemaphoreType.DMA((groups,)),
        ],
        compiler_params=pltpu.CompilerParams(vmem_limit_bytes=WHOLE_VMEM),
        cost_estimate=pl.CostEstimate(flops=0, bytes_accessed=2**22, transcendentals=0),
    )(qkv, grad, text)


def unpack(packed):
    shapes = [
        rows_of(SHARE, HEADS * HEAD_DIM),
        rows_of(2 * BLOCK_ROWS, HEADS * HEAD_DIM),
        rows_of(SHARE, HEADS * 3 * HEAD_DIM),
    ]
    return whole_call(unpack_kernel, shapes, 0, 1, [], 0, 2**22)(packed)


def row_block(place_ref, ahead, across, other_core):
    y = lax.rem(place_ref[0] + ahead, 4)
    z = 1 - place_ref[1] if across else place_ref[1]
    core = 1 - place_ref[2] if other_core else place_ref[2]
    return (y * 2 + z) * 2 + core


def partial_kernel(place_ref, own_ref, other_ref, own_weight_ref, other_weight_ref, *refs):
    chunk_refs, rows_ref = refs[:8], refs[8]
    for index, (ahead, across) in enumerate(CHIPS):
        block = row_block(place_ref, ahead, across, False)
        rows = pl.ds(pl.multiple_of(block * TEXT_SHARE, TEXT_SHARE), TEXT_SHARE)
        to = slice(index * TEXT_SHARE, (index + 1) * TEXT_SHARE)
        rows_ref[to, :FEATURES] = own_ref[rows, :]
        rows_ref[to, FEATURES:] = other_ref[rows, :]

    def body(step, carry):
        columns = pl.ds(pl.multiple_of(step * 512, 512), 512)
        sums = matmul(rows_ref[:, :FEATURES], own_weight_ref[:, columns])
        sums += matmul(rows_ref[:, FEATURES:], other_weight_ref[:, columns])
        for index, chunk_ref in enumerate(chunk_refs):
            rows = slice(index * TEXT_SHARE, (index + 1) * TEXT_SHARE)
            chunk_ref[:, columns] = sums[rows].astype(BF16)
        return carry

    lax.fori_loop(0, WIDTH // 512, body, 0)


def text_kernel(place_ref, *refs):
    block_refs, weight_ref, text_ref = refs[:16], refs[16], refs[17]
    kept_hbm, sent_hbms, encoded_ref, stored = refs[18], refs[19:22], refs[22], refs[23]
    for index, block_ref in enumerate(block_refs):
        ahead, across = CHIPS[index % 8]
        block = row_block(place_ref, ahead, across, index >= 8)
        rows = pl.ds(pl.multiple_of(block * TEXT_SHARE, TEXT_SHARE), TEXT_SHARE)
        encoded_ref[rows, :] = block_ref[...]
    half = pl.ds(pl.multiple_of(place_ref[2] * HALF_PROMPT, HALF_PROMPT), HALF_PROMPT)
    stores = []
    for ahead in range(4):
        x = lax.rem(place_ref[4] + ahead, 4)
        for z_hi in range(4):
            at = pl.ds(pl.multiple_of((z_hi * 4 + x) * FEATURES, FEATURES), FEATURES)
            to = slice(z_hi * FEATURES, (z_hi + 1) * FEATURES)
            if ahead:
                source, target = encoded_ref.at[half, at], sent_hbms[ahead - 1].at[:, to]
            else:
                source, target = encoded_ref.at[:, at], kept_hbm.at[:, to]
            store = pltpu.make_async_copy(source, target, stored.at[len(stores)])
            store.start()
            stores.append(store)
    text_ref[...] = matmul(encoded_ref[...], weight_ref[...]).astype(BF16)
    for store in stores:
        store.wait()


def weight_kernel(place_ref, kept_ref, *refs):
    near_refs, far_refs, grad_refs = refs[:3], refs[3:6], refs[6:10]
    kept_sum_ref, sent_refs = refs[10], refs[11:14]
    near = pl.ds(pl.multiple_of(place_ref[2] * HALF_PROMPT, HALF_PROMPT), HALF_PROMPT)
    far = pl.ds(pl.multiple_of((1 - place_ref[2]) * HALF_PROMPT, HALF_PROMPT), HALF_PROMPT)
    for ahead in range(4):
        z_hi = lax.rem(place_ref[3] + ahead, 4)
        at = pl.ds(pl.multiple_of(z_hi * FEATURES, FEATURES), FEATURES)
        total = matmul(grad_refs[0][...], kept_ref[:, at], CONTRACT_FIRST)
        for grad_ref, near_ref, far_ref in zip(grad_refs[1:], near_refs, far_refs):
            total += matmul(grad_ref[near, :], near_ref[:, at], CONTRACT_FIRST)
            total += matmul(grad_ref[far, :], far_ref[:, at], CONTRACT_FIRST)
        if ahead:
            sent_refs[ahead - 1][...] = total.astype(BF16)
        else:
            kept_sum_ref[...] = total


def total_kernel(kept_ref, *refs):
    total = kept_ref[...]
    for part_ref in refs[:3]:
        total += part_ref[...].astype(F32)
    refs[3][...] = total.T


def exp_rows(scores, maximum):
    return jnp.exp2((scores - maximum) * EXPONENT).astype(BF16)


def spread(rows, columns):
    return jnp.concatenate([rows] * (columns // HEAD_DIM), axis=1)


def row_sums(out_grad, output):
    total = jnp.sum(out_grad.astype(F32) * output, axis=-1, keepdims=True)
    return jnp.broadcast_to(total, output.shape)


def score_gradient(weights, prob_grad, row_delta):
    wide = spread(row_delta, weights.shape[1])
    return (weights.astype(F32) * (prob_grad - wide)).astype(BF16)


def chains(count, first, then):
    ahead = first(0)
    for chain in range(count):
        current = ahead
        if chain + 1 < count:
            ahead = first(chain + 1)
        then(chain, current)


def chain_rows(chain):
    return slice(chain * QUERY_BLOCK, (chain + 1) * QUERY_BLOCK)


def image_forward_kernel(
    order_ref,
    packed_ref,
    weights_ref,
    rows_ref,
    output_ref,
    maximum_ref,
    total_ref,
    text_do_ref,
    k_ref,
    v_ref,
):
    step = pl.program_id(0)

    @pl.when(step == 0)
    def _():
        v_ref[:, HEAD_DIM:] = jnp.ones((IMAGE, HEAD_DIM), BF16)
        for src in range(HEADS):
            at = slice(src * SHARE, (src + 1) * SHARE)
            k_ref[at, :] = packed_ref[src, :SHARE, HEAD_DIM : 2 * HEAD_DIM]
            v_ref[at, :HEAD_DIM] = packed_ref[src, :SHARE, 2 * HEAD_DIM : 3 * HEAD_DIM]
        for block in range(TEXT_BLOCKS):
            slot = order_ref[block]
            columns = pl.ds(pl.multiple_of((slot % 2) * HEAD_DIM, HEAD_DIM), HEAD_DIM)
            text_do_ref[block * BLOCK_ROWS : (block + 1) * BLOCK_ROWS, :] = packed_ref[
                slot // 2, SHARE:, columns
            ]

    parts = FORWARD_ROWS // SHARE
    for part in range(parts):
        at = slice(part * SHARE, (part + 1) * SHARE)
        rows_ref[at, :] = packed_ref[step * parts + part, :SHARE, :]

    def first(chain):
        return matmul(rows_ref[chain_rows(chain), :HEAD_DIM], k_ref[...], CONTRACT_LAST)

    def then(chain, scores):
        at = chain_rows(chain)
        maximum = jnp.max(scores, axis=-1, keepdims=True)
        weights = exp_rows(scores, maximum)
        weights_ref[at, :] = weights
        both = matmul(weights, v_ref[...])
        output_ref[at, :] = both[:, :HEAD_DIM]
        total_ref[at, :] = both[:, HEAD_DIM:]
        maximum_ref[at, :] = jnp.broadcast_to(maximum, (QUERY_BLOCK, HEAD_DIM))

    chains(FORWARD_ROWS // QUERY_BLOCK, first, then)


def attention_kernel(
    length_ref,
    order_ref,
    text_ref,
    text_do_ref,
    rows_ref,
    weights_ref,
    output_ref,
    maximum_ref,
    total_ref,
    sent_hbm,
    text_grad_ref,
    sent_ref,
    dkt_ref,
    dvt_ref,
    image_dkt_ref,
    image_dvt_ref,
    tv_ref,
    stored,
):
    step = pl.program_id(0)
    factor = HEAD_DIM**-0.5
    text_keys = text_ref[:, HEAD_DIM : 2 * HEAD_DIM]
    text_values = text_ref[:, 2 * HEAD_DIM :]
    keys = rows_ref[:, HEAD_DIM : 2 * HEAD_DIM]
    values = rows_ref[:, 2 * HEAD_DIM : 3 * HEAD_DIM]
    live = lax.broadcasted_iota(jnp.int32, (1, PROMPT), 1) < length_ref[0]
    sums = (dkt_ref, dvt_ref, image_dkt_ref, image_dvt_ref)

    def text_scores(queries):
        return jnp.where(live, matmul(queries, text_keys, CONTRACT_LAST), -1e30)

    @pl.when(step == 0)
    def _():
        tv_ref[:, :HEAD_DIM] = text_values
        tv_ref[:, HEAD_DIM:] = jnp.ones((PROMPT, HEAD_DIM), BF16)
        sent_ref[:, SHARE:, 2 * HEAD_DIM :] = jnp.zeros((HEADS, BLOCK_ROWS, 2 * HEAD_DIM), BF16)
        places = [chain_rows(chain) for chain in range(CHAINS)]
        scores = []
        for rows in places:
            queries = text_ref[rows, :HEAD_DIM]
            scores.append((text_scores(queries), matmul(queries, keys, CONTRACT_LAST)))
        weights = []
        for to_text, to_image in scores:
            maximum = jnp.maximum(
                jnp.max(to_text, axis=-1, keepdims=True), jnp.max(to_image, axis=-1, keepdims=True)
            )
            weights.append((exp_rows(to_text, maximum), exp_rows(to_image, maximum)))
        middle = []
        for rows, (text_weights, image_weights) in zip(places, weights):
            total = jnp.sum(image_weights.astype(F32), axis=-1, keepdims=True)
            both = matmul(text_weights, tv_ref[...])
            inverse = 1.0 / (both[:, HEAD_DIM:] + total)
            output = (both[:, :HEAD_DIM] + matmul(image_weights, values)) * inverse
            out_grad = (text_do_ref[rows, :].astype(F32) * inverse).astype(BF16)
            prob_grads = [matmul(out_grad, part, CONTRACT_LAST) for part in (text_values, values)]
            middle.append((output, out_grad, row_sums(out_grad, output), prob_grads))
        for chain, rows in enumerate(places):
            text_weights, image_weights = weights[chain]
            output, out_grad, row_delta, prob_grads = middle[chain]
            queries = text_ref[rows, :HEAD_DIM]
            text_scored = score_gradient(text_weights, prob_grads[0], row_delta)
            image_scored = score_gradient(image_weights, prob_grads[1], row_delta)
            query_grad = matmul(text_scored, text_keys) + matmul(image_scored, keys)
            text_grad_ref[rows, :HEAD_DIM] = (query_grad * factor).astype(BF16)
            products = (
                matmul(queries, text_scored, CONTRACT_FIRST),
                matmul(out_grad, text_weights, CONTRACT_FIRST),
                matmul(queries, image_scored, CONTRACT_FIRST),
                matmul(out_grad, image_weights, CONTRACT_FIRST),
            )
            for sum_ref, product in zip(sums, products):
                sum_ref[...] = sum_ref[...] + product if chain else product
            output = output.astype(BF16)
            blocks = QUERY_BLOCK // BLOCK_ROWS
            for block in range(blocks):
                slot = order_ref[chain * blocks + block]
                columns = pl.ds(pl.multiple_of((slot % 2) * HEAD_DIM, HEAD_DIM), HEAD_DIM)
                sent_ref[slot // 2, SHARE:, columns] = output[
                    block * BLOCK_ROWS : (block + 1) * BLOCK_ROWS
                ]

    @pl.when(step > 0)
    def _():
        def place(chain):
            start = (step - 1) * FORWARD_ROWS + chain * QUERY_BLOCK
            return pl.ds(pl.multiple_of(start, QUERY_BLOCK), QUERY_BLOCK)

        places = [chain_rows(chain) for chain in range(CHAINS)]
        scores = [text_scores(rows_ref[place(chain), :HEAD_DIM]) for chain in range(CHAINS)]
        weights = []
        for at, to_text in zip(places, scores):
            image_maximum = maximum_ref[at, :]
            maximum = jnp.maximum(image_maximum, jnp.max(to_text, axis=-1, keepdims=True))
            scale = jnp.exp2((image_maximum - maximum) * EXPONENT)
            weights.append((exp_rows(to_text, spread(maximum, PROMPT)), scale))
        middle = []
        for chain, (at, (text_weights, scale)) in enumerate(zip(places, weights)):
            both = matmul(text_weights, tv_ref[...])
            inverse = 1.0 / (both[:, HEAD_DIM:] + scale * total_ref[at, :])
            output = (scale * output_ref[at, :] + both[:, :HEAD_DIM]) * inverse
            cotangent = rows_ref[place(chain), 3 * HEAD_DIM :].astype(F32)
            out_grad = (cotangent * inverse).astype(BF16)
            image_out_grad = (cotangent * (scale * inverse)).astype(BF16)
            prob_grad = matmul(out_grad, text_values, CONTRACT_LAST)
            image_prob_grad = matmul(image_out_grad, values, CONTRACT_LAST)
            middle.append(
                (
                    (out_grad, row_sums(out_grad, output), prob_grad),
                    (image_out_grad, row_sums(image_out_grad, output), image_prob_grad),
                )
            )
            output = output.astype(BF16)
            for part in range(QUERY_BLOCK // SHARE):
                dest = ((step - 1) * FORWARD_ROWS + chain * QUERY_BLOCK) // SHARE + part
                sent_ref[dest, :SHARE, :HEAD_DIM] = output[part * SHARE : (part + 1) * SHARE]
        for chain, at in enumerate(places):
            queries = rows_ref[place(chain), :HEAD_DIM]
            (out_grad, row_delta, prob_grad), image_parts = middle[chain]
            image_out_grad, image_delta, image_prob_grad = image_parts
            text_weights, image_weights = weights[chain][0], weights_ref[at, :]
            text_scored = score_gradient(text_weights, prob_grad, row_delta)
            image_scored = score_gradient(image_weights, image_prob_grad, image_delta)
            query_grad = matmul(text_scored, text_keys) + matmul(image_scored, keys)
            query_grad = (query_grad * factor).astype(BF16)
            for part in range(QUERY_BLOCK // SHARE):
                dest = ((step - 1) * FORWARD_ROWS + chain * QUERY_BLOCK) // SHARE + part
                sent_ref[dest, :SHARE, HEAD_DIM : 2 * HEAD_DIM] = query_grad[
                    part * SHARE : (part + 1) * SHARE
                ]
            dkt_ref[...] += matmul(queries, text_scored, CONTRACT_FIRST)
            dvt_ref[...] += matmul(out_grad, text_weights, CONTRACT_FIRST)
            image_dkt_ref[...] += matmul(queries, image_scored, CONTRACT_FIRST)
            image_dvt_ref[...] += matmul(image_out_grad, image_weights, CONTRACT_FIRST)

    @pl.when(step == IMAGE // FORWARD_ROWS)
    def _():
        text_grad_ref[:, HEAD_DIM : 2 * HEAD_DIM] = (dkt_ref[...] * factor).T.astype(BF16)
        text_grad_ref[:, 2 * HEAD_DIM :] = dvt_ref[...].T.astype(BF16)
        stores = []
        for dest in range(HEADS):
            at = slice(dest * SHARE, (dest + 1) * SHARE)
            sent_ref[dest, :SHARE, 2 * HEAD_DIM : 3 * HEAD_DIM] = (
                (image_dkt_ref[:, at] * factor).T.astype(BF16)
            )
            sent_ref[dest, :SHARE, 3 * HEAD_DIM :] = image_dvt_ref[:, at].T.astype(BF16)
            if dest % 4 == 3:
                group = slice(dest - 3, dest + 1)
                store = pltpu.make_async_copy(
                    sent_ref.at[group], sent_hbm.at[group], stored.at[dest // 4]
                )
                store.start()
                stores.append(store)
        for store in stores:
            store.wait()


def grid_call(kernel, steps, in_specs, out_shape, out_specs, scratch, products):
    return pl.pallas_call(
        kernel,
        grid=(steps,),
        out_shape=out_shape,
        in_specs=in_specs,
        out_specs=out_specs,
        scratch_shapes=scratch,
        compiler_params=pltpu.CompilerParams(vmem_limit_bytes=WHOLE_VMEM),
        cost_estimate=pl.CostEstimate(
            flops=60 * products * HEAD_DIM, bytes_accessed=2**29, transcendentals=0
        ),
    )


IN_SMEM = pl.BlockSpec(memory_space=pltpu.SMEM)


def fixed(*shape):
    return pl.BlockSpec(shape, lambda step: (0,) * len(shape))


def per_block(rows, columns, skip=0):
    return pl.BlockSpec((rows, columns), lambda step: (jnp.maximum(step - skip, 0), 0))


def image_forward(order, packed):
    floats = jax.ShapeDtypeStruct((IMAGE, HEAD_DIM), F32)
    block = per_block(FORWARD_ROWS, HEAD_DIM)
    return grid_call(
        image_forward_kernel,
        IMAGE // FORWARD_ROWS,
        [IN_SMEM, fixed(HEADS, PACK_ROWS, PACK_COLS)],
        [rows_of(IMAGE, IMAGE), rows_of(IMAGE, PACK_COLS)] + [floats] * 3
        + [rows_of(PROMPT, HEAD_DIM)],
        [per_block(FORWARD_ROWS, IMAGE), per_block(FORWARD_ROWS, PACK_COLS)] + [block] * 3
        + [fixed(PROMPT, HEAD_DIM)],
        [pltpu.VMEM((IMAGE, HEAD_DIM), BF16), pltpu.VMEM((IMAGE, 2 * HEAD_DIM), BF16)],
        2 * IMAGE * IMAGE,
    )(order, packed)


def attention(length, order, text_rows, text_do, rows, weights, output, maximum, total):
    block = per_block(FORWARD_ROWS, HEAD_DIM, 1)
    text_sum = pltpu.VMEM((HEAD_DIM, PROMPT), F32)
    image_sum = pltpu.VMEM((HEAD_DIM, IMAGE), F32)
    return grid_call(
        attention_kernel,
        1 + IMAGE // FORWARD_ROWS,
        [IN_SMEM, IN_SMEM, fixed(PROMPT, 3 * HEAD_DIM), fixed(PROMPT, HEAD_DIM)]
        + [fixed(IMAGE, PACK_COLS), per_block(FORWARD_ROWS, IMAGE, 1)] + [block] * 3,
        [rows_of(HEADS, PACK_ROWS, PACK_COLS), rows_of(PROMPT, 3 * HEAD_DIM)],
        [pl.BlockSpec(memory_space=pltpu.HBM), fixed(PROMPT, 3 * HEAD_DIM)],
        [pltpu.VMEM((HEADS, PACK_ROWS, PACK_COLS), BF16), text_sum, text_sum, image_sum, image_sum]
        + [pltpu.VMEM((PROMPT, 2 * HEAD_DIM), BF16), pltpu.SemaphoreType.DMA((4,))],
        6 * TOTAL * TOTAL - 2 * IMAGE * IMAGE,
    )(length, order, text_rows, text_do, rows, weights, output, maximum, total)


def shift(rows, axis, step):
    size = 2 if axis in ("z_lo", "core") else 4
    return lax.ppermute(rows, axis, [(i, (i + step) % size) for i in range(size)])


def add(*rows):
    return sum(part.astype(F32) for part in rows)


def encode(place, context, residual, weight, gain, packed, order):
    other_weight = shift(weight, "core", 1)
    other = shift(context, "core", 1)
    other_weight, packed = lax.optimization_barrier((other_weight, packed))
    packed = lax.all_to_all(packed, SEQ, split_axis=0, concat_axis=0, tiled=True)
    chunks = whole_call(
        partial_kernel,
        [rows_of(TEXT_SHARE, WIDTH)] * 8,
        1,
        4,
        [pltpu.VMEM((8 * TEXT_SHARE, 2 * FEATURES), BF16)],
        2 * 8 * TEXT_SHARE * 2 * FEATURES * WIDTH,
        2**23,
    )(place, context, other, weight, other_weight)
    part = dict(zip(CHIPS, chunks))
    from_across = shift(part[2, 1], "z_lo", 1)
    from_below = shift(part[1, 1], "y", 1)
    from_above = shift(part[3, 1], "y", -1)
    below = shift(part[1, 0], "y", 1)
    above = shift(part[3, 0], "y", -1)
    opposite = add(part[2, 0], from_across).astype(BF16)
    across = add(part[0, 1], from_below, from_above).astype(BF16)
    packed, opposite, across = lax.optimization_barrier((packed, opposite, across))
    forward = image_forward(order, packed)
    opposite = shift(opposite, "y", 2)
    across = shift(across, "z_lo", 1)
    forward, opposite, across = lax.optimization_barrier((forward, opposite, across))
    stream = add(residual, part[0, 0], below, above, opposite, across)
    inv_norm = lax.rsqrt(jnp.mean(stream * stream, axis=-1, keepdims=True) + 1e-06)
    encoded = (stream * inv_norm * gain).astype(BF16)
    held = {(0, 0): encoded}
    held[0, 1] = shift(encoded, "z_lo", 1)
    held[3, 0] = shift(encoded, "y", 1)
    held[1, 0] = shift(encoded, "y", -1)
    held[2, 0] = shift(encoded, "y", 2)
    held[3, 1] = shift(held[0, 1], "y", 1)
    held[1, 1] = shift(held[0, 1], "y", -1)
    held[2, 1] = shift(held[2, 0], "z_lo", 1)
    early = [held[chip] for chip in CHIPS[:5] + CHIPS[6:7]]
    early = lax.optimization_barrier(early)
    held.update(zip(CHIPS[:5] + CHIPS[6:7], early))
    own = [held[chip] for chip in CHIPS]
    return own + [shift(rows, "core", 1) for rows in own], forward


def project(place, blocks, weight):
    columns = weight.shape[1]
    quarter = 4 * FEATURES
    in_vmem = pl.BlockSpec(memory_space=pltpu.VMEM)
    in_hbm = pl.BlockSpec(memory_space=pltpu.HBM)
    return pl.pallas_call(
        text_kernel,
        out_shape=[rows_of(PROMPT, columns), rows_of(PROMPT, quarter)]
        + [rows_of(HALF_PROMPT, quarter)] * 3,
        in_specs=[IN_SMEM] + [in_vmem] * 17,
        out_specs=[in_vmem] + [in_hbm] * 4,
        scratch_shapes=[pltpu.VMEM((PROMPT, WIDTH), BF16), pltpu.SemaphoreType.DMA((16,))],
        compiler_params=pltpu.CompilerParams(vmem_limit_bytes=VMEM_LIMIT),
        cost_estimate=pl.CostEstimate(
            flops=2 * PROMPT * WIDTH * columns, bytes_accessed=2**23, transcendentals=0
        ),
    )(place, *blocks, weight)


def weight_sums(place, kept, near, far, grads):
    columns = grads[0].shape[1]
    total = jax.ShapeDtypeStruct((columns, FEATURES), F32)
    kept_sum, *sent = whole_call(
        weight_kernel,
        [total] + [rows_of(columns, FEATURES)] * 3,
        1,
        11,
        [],
        28 * 2 * 4 * PROMPT * 4 * FEATURES * columns,
        2**23,
    )(place, kept, *near, *far, *grads)
    return [kept_sum] + [shift(rows, "z_hi", step + 1) for step, rows in enumerate(sent)]


def weight_total(kept_sum, *parts):
    shape = jax.ShapeDtypeStruct(kept_sum.shape[::-1], F32)
    return whole_call(total_kernel, shape, 0, 4, [], 0, 2**20)(kept_sum, *parts)


def on_device(
    t5_context,
    t5_resid,
    t5_out_weight,
    t5_gain,
    text_weight,
    prompt_len,
    text_order,
    img_qkv,
    d_img_out,
    d_txt_out,
):
    packed = pack(img_qkv[0], d_img_out[0], d_txt_out[0])
    place = jnp.stack([lax.axis_index(axis) for axis in SEQ + GRP])
    blocks, forward = encode(
        place, t5_context[0], t5_resid[0], t5_out_weight, t5_gain, packed, text_order[0]
    )
    weights, rows, *stats, text_do = forward
    text_rows, kept, *slices = project(place, blocks, text_weight)
    near = [shift(rows, "x", step + 1) for step, rows in enumerate(slices)]
    sent, text_grad = attention(
        prompt_len, text_order[0], text_rows, text_do, rows, weights, *stats
    )
    *near, sent = lax.optimization_barrier((*near, sent))
    grads = [text_grad] + [shift(text_grad, "x", step) for step in (1, 2, 3)]
    far = [shift(rows, "core", 1) for rows in near]
    far, sent = lax.optimization_barrier((far, sent))
    sums = weight_sums(place, kept, near, far, grads)
    received = lax.all_to_all(sent, SEQ, split_axis=0, concat_axis=0, tiled=True)
    outputs = unpack(received)
    sums, outputs = lax.optimization_barrier((sums, outputs))
    image_out, text_out, image_qkv_grad = outputs
    text_weight_grad = weight_total(*sums)
    return (image_out[None], text_out[None], image_qkv_grad[None], text_weight_grad)


def solution(mesh):
    fine = Mesh(mesh.devices.reshape(4, 4, 4, 2, 2), GRP + SEQ)
    in_specs = (
        P(GRP, None, SEQ),
        P(GRP, SEQ, None),
        P(SEQ, None),
        P(),
        P(None, SEQ),
        P(GRP),
        P(GRP, None),
        P(GRP, SEQ, None),
        P(GRP, SEQ, None),
        P(GRP, SEQ, None),
    )
    out_specs = (
        P(GRP, SEQ, None),
        P(GRP, SEQ, None),
        P(GRP, SEQ, None),
        P(GRP, SEQ),
    )
    return jax.shard_map(
        on_device, mesh=fine, in_specs=in_specs, out_specs=out_specs, check_vma=False
    )
```

```python
import jax
import jax.numpy as jnp
from jax import lax
from jax.experimental import pallas as pl
from jax.experimental.pallas import tpu as pltpu
from jax.sharding import Mesh
from jax.sharding import PartitionSpec as P

HEAD_DIM = 128
HEADS = 16
PROMPT = 512
IMAGE = 2048
TOTAL = PROMPT + IMAGE
BLOCK_ROWS = 16
TEXT_BLOCKS = 32
SHARE = IMAGE // HEADS
PACK_ROWS = SHARE + BLOCK_ROWS
PACK_COLS = 4 * HEAD_DIM
QUERY_BLOCK = 256
EXPONENT = HEAD_DIM**-0.5 * 1.4426950408889634
FORWARD_ROWS = 512
PACK_HEADS = 4
CHAINS = 2
WIDTH = 4096
FEATURES = WIDTH // HEADS
TEXT_SHARE = PROMPT // HEADS
HALF_PROMPT = PROMPT // 2
TEXT_DEPTH = 1024
CHIPS = [(ahead, across) for ahead in range(4) for across in range(2)]

BF16 = jnp.bfloat16
F32 = jnp.float32
SEQ = ("y", "z_lo", "core")
GRP = ("z_hi", "x")
CONTRACT_LAST = (((1,), (1,)), ((), ()))
CONTRACT_FIRST = (((0,), (0,)), ((), ()))
VMEM_LIMIT = 48 * 2**20
WHOLE_VMEM = 60 * 2**20


def matmul(a, b, dims=(((1,), (0,)), ((), ()))):
    return lax.dot_general(a, b, dims, preferred_element_type=F32)


def pack_kernel(qkv_hbm, grad_hbm, text_hbm, packed_hbm, *refs):
    qkv_ref, grad_ref, text_ref, packed_ref, loaded, stored = refs
    loads = []
    for source, target in ((grad_hbm, grad_ref), (text_hbm, text_ref)):
        loads.append(pltpu.make_async_copy(source, target, loaded.at[len(loads)]))
    width = 3 * HEAD_DIM * PACK_HEADS
    for group in range(HEADS // PACK_HEADS):
        columns = slice(group * width, (group + 1) * width)
        source, target = qkv_hbm.at[:, columns], qkv_ref.at[:, columns]
        loads.append(pltpu.make_async_copy(source, target, loaded.at[len(loads)]))
    for load in loads:
        load.start()
    loads[0].wait()
    loads[1].wait()
    stores = []
    for group in range(HEADS // PACK_HEADS):
        loads[2 + group].wait()
        heads = slice(group * PACK_HEADS, (group + 1) * PACK_HEADS)
        for head in range(heads.start, heads.stop):
            columns = slice(head * HEAD_DIM, (head + 1) * HEAD_DIM)
            wide = slice(3 * head * HEAD_DIM, 3 * (head + 1) * HEAD_DIM)
            packed_ref[head, :SHARE, : 3 * HEAD_DIM] = qkv_ref[:, wide]
            packed_ref[head, :SHARE, 3 * HEAD_DIM :] = grad_ref[:, columns]
            packed_ref[head, SHARE:, :HEAD_DIM] = text_ref[:BLOCK_ROWS, columns]
            packed_ref[head, SHARE:, HEAD_DIM : 2 * HEAD_DIM] = text_ref[BLOCK_ROWS:, columns]
            packed_ref[head, SHARE:, 2 * HEAD_DIM :] = jnp.zeros(
                (BLOCK_ROWS, 2 * HEAD_DIM), BF16
            )
        store = pltpu.make_async_copy(
            packed_ref.at[heads], packed_hbm.at[heads], stored.at[group]
        )
        store.start()
        stores.append(store)
    for store in stores:
        store.wait()


def unpack_kernel(packed_ref, out_ref, text_ref, qkv_ref):
    for head in range(HEADS):
        columns = slice(head * HEAD_DIM, (head + 1) * HEAD_DIM)
        wide = slice(3 * head * HEAD_DIM, 3 * (head + 1) * HEAD_DIM)
        out_ref[:, columns] = packed_ref[head, :SHARE, :HEAD_DIM]
        qkv_ref[:, wide] = packed_ref[head, :SHARE, HEAD_DIM:]
        text_ref[:BLOCK_ROWS, columns] = packed_ref[head, SHARE:, :HEAD_DIM]
        text_ref[BLOCK_ROWS:, columns] = packed_ref[head, SHARE:, HEAD_DIM : 2 * HEAD_DIM]


def whole_call(kernel, out_shape, smem_inputs, vmem_inputs, scratch, flops, moved, limit=None):
    in_vmem = pl.BlockSpec(memory_space=pltpu.VMEM)
    in_smem = pl.BlockSpec(memory_space=pltpu.SMEM)
    return pl.pallas_call(
        kernel,
        out_shape=out_shape,
        in_specs=[in_smem] * smem_inputs + [in_vmem] * vmem_inputs,
        out_specs=jax.tree.map(lambda _: in_vmem, out_shape),
        scratch_shapes=scratch,
        compiler_params=pltpu.CompilerParams(vmem_limit_bytes=limit or VMEM_LIMIT),
        cost_estimate=pl.CostEstimate(flops=flops, bytes_accessed=moved, transcendentals=0),
    )


def rows_of(*shape):
    return jax.ShapeDtypeStruct(shape, BF16)


def pack(qkv, grad, text):
    anywhere = pl.BlockSpec(memory_space=pltpu.HBM)
    groups = HEADS // PACK_HEADS
    return pl.pallas_call(
        pack_kernel,
        out_shape=rows_of(HEADS, PACK_ROWS, PACK_COLS),
        in_specs=[anywhere] * 3,
        out_specs=anywhere,
        scratch_shapes=[
            pltpu.VMEM(qkv.shape, BF16),
            pltpu.VMEM(grad.shape, BF16),
            pltpu.VMEM(text.shape, BF16),
            pltpu.VMEM((HEADS, PACK_ROWS, PACK_COLS), BF16),
            pltpu.SemaphoreType.DMA((2 + groups,)),
            pltpu.SemaphoreType.DMA((groups,)),
        ],
        compiler_params=pltpu.CompilerParams(vmem_limit_bytes=WHOLE_VMEM),
        cost_estimate=pl.CostEstimate(flops=0, bytes_accessed=2**22, transcendentals=0),
    )(qkv, grad, text)


def unpack(packed):
    shapes = [
        rows_of(SHARE, HEADS * HEAD_DIM),
        rows_of(2 * BLOCK_ROWS, HEADS * HEAD_DIM),
        rows_of(SHARE, HEADS * 3 * HEAD_DIM),
    ]
    return whole_call(unpack_kernel, shapes, 0, 1, [], 0, 2**22)(packed)


def row_block(place_ref, ahead, across, other_core):
    y = lax.rem(place_ref[0] + ahead, 4)
    z = 1 - place_ref[1] if across else place_ref[1]
    core = 1 - place_ref[2] if other_core else place_ref[2]
    return (y * 2 + z) * 2 + core


def partial_kernel(place_ref, own_ref, other_ref, own_weight_ref, other_weight_ref, *refs):
    chunk_refs, rows_ref = refs[:8], refs[8]
    for index, (ahead, across) in enumerate(CHIPS):
        block = row_block(place_ref, ahead, across, False)
        rows = pl.ds(pl.multiple_of(block * TEXT_SHARE, TEXT_SHARE), TEXT_SHARE)
        to = slice(index * TEXT_SHARE, (index + 1) * TEXT_SHARE)
        rows_ref[to, :FEATURES] = own_ref[rows, :]
        rows_ref[to, FEATURES:] = other_ref[rows, :]

    def body(step, carry):
        columns = pl.ds(pl.multiple_of(step * 512, 512), 512)
        sums = matmul(rows_ref[:, :FEATURES], own_weight_ref[:, columns])
        sums += matmul(rows_ref[:, FEATURES:], other_weight_ref[:, columns])
        for index, chunk_ref in enumerate(chunk_refs):
            rows = slice(index * TEXT_SHARE, (index + 1) * TEXT_SHARE)
            chunk_ref[:, columns] = sums[rows].astype(BF16)
        return carry

    lax.fori_loop(0, WIDTH // 512, body, 0)


def text_kernel(place_ref, *refs):
    block_refs, weight_ref, text_ref = refs[:16], refs[16], refs[17]
    kept_hbm, sent_hbms, encoded_ref, total_ref, stored = refs[18], refs[19:22], *refs[22:]
    for index, block_ref in enumerate(block_refs):
        ahead, across = CHIPS[index % 8]
        block = row_block(place_ref, ahead, across, index >= 8)
        rows = pl.ds(pl.multiple_of(block * TEXT_SHARE, TEXT_SHARE), TEXT_SHARE)
        encoded_ref[rows, :] = block_ref[...]
    half = pl.ds(pl.multiple_of(place_ref[2] * HALF_PROMPT, HALF_PROMPT), HALF_PROMPT)
    stores = []
    for ahead in range(4):
        x = lax.rem(place_ref[4] + ahead, 4)
        for z_hi in range(4):
            at = pl.ds(pl.multiple_of((z_hi * 4 + x) * FEATURES, FEATURES), FEATURES)
            to = slice(z_hi * FEATURES, (z_hi + 1) * FEATURES)
            if ahead:
                source, target = encoded_ref.at[half, at], sent_hbms[ahead - 1].at[:, to]
            else:
                source, target = encoded_ref.at[:, at], kept_hbm.at[:, to]
            store = pltpu.make_async_copy(source, target, stored.at[len(stores)])
            store.start()
            stores.append(store)
    total_ref[...] = jnp.zeros_like(total_ref)

    def body(step, carry):
        depth = pl.ds(pl.multiple_of(step * TEXT_DEPTH, TEXT_DEPTH), TEXT_DEPTH)
        total_ref[...] += matmul(encoded_ref[:, depth], weight_ref[depth, :])
        return carry

    lax.fori_loop(0, WIDTH // TEXT_DEPTH, body, 0)
    text_ref[...] = total_ref[...].astype(BF16)
    for store in stores:
        store.wait()


def weight_kernel(place_ref, kept_ref, *refs):
    near_refs, far_refs, grad_refs = refs[:3], refs[3:6], refs[6:10]
    kept_sum_ref, sent_refs, totals_ref = refs[10], refs[11:14], refs[14]
    near = pl.ds(pl.multiple_of(place_ref[2] * HALF_PROMPT, HALF_PROMPT), HALF_PROMPT)
    far = pl.ds(pl.multiple_of((1 - place_ref[2]) * HALF_PROMPT, HALF_PROMPT), HALF_PROMPT)

    def body(ahead, carry):
        z_hi = lax.rem(place_ref[3] + ahead, 4)
        at = pl.ds(pl.multiple_of(z_hi * FEATURES, FEATURES), FEATURES)
        total = matmul(grad_refs[0][...], kept_ref[:, at], CONTRACT_FIRST)
        for grad_ref, near_ref, far_ref in zip(grad_refs[1:], near_refs, far_refs):
            total += matmul(grad_ref[near, :], near_ref[:, at], CONTRACT_FIRST)
            total += matmul(grad_ref[far, :], far_ref[:, at], CONTRACT_FIRST)
        totals_ref[ahead] = total
        return carry

    lax.fori_loop(0, 4, body, 0)
    kept_sum_ref[...] = totals_ref[0]
    for step, sent_ref in enumerate(sent_refs):
        sent_ref[...] = totals_ref[step + 1].astype(BF16)


def total_kernel(kept_ref, *refs):
    total = kept_ref[...]
    for part_ref in refs[:3]:
        total += part_ref[...].astype(F32)
    refs[3][...] = total.T


def exp_rows(scores, maximum):
    return jnp.exp2((scores - maximum) * EXPONENT).astype(BF16)


def spread(rows, columns):
    return jnp.concatenate([rows] * (columns // HEAD_DIM), axis=1)


def row_sums(out_grad, output):
    total = jnp.sum(out_grad.astype(F32) * output, axis=-1, keepdims=True)
    return jnp.broadcast_to(total, output.shape)


def score_gradient(weights, prob_grad, row_delta):
    wide = spread(row_delta, weights.shape[1])
    return (weights.astype(F32) * (prob_grad - wide)).astype(BF16)


def chains(count, first, then):
    ahead = first(0)
    for chain in range(count):
        current = ahead
        if chain + 1 < count:
            ahead = first(chain + 1)
        then(chain, current)


def chain_rows(chain):
    return slice(chain * QUERY_BLOCK, (chain + 1) * QUERY_BLOCK)


def image_forward_kernel(
    order_ref,
    packed_ref,
    weights_ref,
    rows_ref,
    output_ref,
    maximum_ref,
    total_ref,
    text_do_ref,
    k_ref,
    v_ref,
):
    step = pl.program_id(0)

    @pl.when(step == 0)
    def _():
        v_ref[:, HEAD_DIM:] = jnp.ones((IMAGE, HEAD_DIM), BF16)
        for src in range(HEADS):
            at = slice(src * SHARE, (src + 1) * SHARE)
            k_ref[at, :] = packed_ref[src, :SHARE, HEAD_DIM : 2 * HEAD_DIM]
            v_ref[at, :HEAD_DIM] = packed_ref[src, :SHARE, 2 * HEAD_DIM : 3 * HEAD_DIM]
        for block in range(TEXT_BLOCKS):
            slot = order_ref[block]
            columns = pl.ds(pl.multiple_of((slot % 2) * HEAD_DIM, HEAD_DIM), HEAD_DIM)
            text_do_ref[block * BLOCK_ROWS : (block + 1) * BLOCK_ROWS, :] = packed_ref[
                slot // 2, SHARE:, columns
            ]

    parts = FORWARD_ROWS // SHARE
    for part in range(parts):
        at = slice(part * SHARE, (part + 1) * SHARE)
        rows_ref[at, :] = packed_ref[step * parts + part, :SHARE, :]

    def first(chain):
        return matmul(rows_ref[chain_rows(chain), :HEAD_DIM], k_ref[...], CONTRACT_LAST)

    def then(chain, scores):
        at = chain_rows(chain)
        maximum = jnp.max(scores, axis=-1, keepdims=True)
        weights = exp_rows(scores, maximum)
        weights_ref[at, :] = weights
        both = matmul(weights, v_ref[...])
        output_ref[at, :] = both[:, :HEAD_DIM]
        total_ref[at, :] = both[:, HEAD_DIM:]
        maximum_ref[at, :] = jnp.broadcast_to(maximum, (QUERY_BLOCK, HEAD_DIM))

    chains(FORWARD_ROWS // QUERY_BLOCK, first, then)


def attention_kernel(
    length_ref,
    order_ref,
    text_ref,
    text_do_ref,
    rows_ref,
    weights_ref,
    output_ref,
    maximum_ref,
    total_ref,
    sent_hbm,
    text_grad_ref,
    sent_ref,
    dkt_ref,
    dvt_ref,
    image_dkt_ref,
    image_dvt_ref,
    tv_ref,
    stored,
):
    step = pl.program_id(0)
    factor = HEAD_DIM**-0.5
    text_keys = text_ref[:, HEAD_DIM : 2 * HEAD_DIM]
    text_values = text_ref[:, 2 * HEAD_DIM :]
    keys = rows_ref[:, HEAD_DIM : 2 * HEAD_DIM]
    values = rows_ref[:, 2 * HEAD_DIM : 3 * HEAD_DIM]
    live = lax.broadcasted_iota(jnp.int32, (1, PROMPT), 1) < length_ref[0]
    sums = (dkt_ref, dvt_ref, image_dkt_ref, image_dvt_ref)

    def text_scores(queries):
        return jnp.where(live, matmul(queries, text_keys, CONTRACT_LAST), -1e30)

    @pl.when(step == 0)
    def _():
        tv_ref[:, :HEAD_DIM] = text_values
        tv_ref[:, HEAD_DIM:] = jnp.ones((PROMPT, HEAD_DIM), BF16)
        sent_ref[:, SHARE:, 2 * HEAD_DIM :] = jnp.zeros((HEADS, BLOCK_ROWS, 2 * HEAD_DIM), BF16)
        for sum_ref in sums:
            sum_ref[...] = jnp.zeros_like(sum_ref)

        def body(chain, carry):
            rows = pl.ds(pl.multiple_of(chain * QUERY_BLOCK, QUERY_BLOCK), QUERY_BLOCK)
            queries = text_ref[rows, :HEAD_DIM]
            to_text = text_scores(queries)
            to_image = matmul(queries, keys, CONTRACT_LAST)
            maximum = jnp.maximum(
                jnp.max(to_text, axis=-1, keepdims=True), jnp.max(to_image, axis=-1, keepdims=True)
            )
            text_weights, image_weights = exp_rows(to_text, maximum), exp_rows(to_image, maximum)
            total = jnp.sum(image_weights.astype(F32), axis=-1, keepdims=True)
            both = matmul(text_weights, tv_ref[...])
            inverse = 1.0 / (both[:, HEAD_DIM:] + total)
            output = (both[:, :HEAD_DIM] + matmul(image_weights, values)) * inverse
            out_grad = (text_do_ref[rows, :].astype(F32) * inverse).astype(BF16)
            row_delta = row_sums(out_grad, output)
            prob_grads = [matmul(out_grad, part, CONTRACT_LAST) for part in (text_values, values)]
            text_scored = score_gradient(text_weights, prob_grads[0], row_delta)
            image_scored = score_gradient(image_weights, prob_grads[1], row_delta)
            query_grad = matmul(text_scored, text_keys) + matmul(image_scored, keys)
            text_grad_ref[rows, :HEAD_DIM] = (query_grad * factor).astype(BF16)
            dkt_ref[...] += matmul(queries, text_scored, CONTRACT_FIRST)
            dvt_ref[...] += matmul(out_grad, text_weights, CONTRACT_FIRST)
            image_dkt_ref[...] += matmul(queries, image_scored, CONTRACT_FIRST)
            image_dvt_ref[...] += matmul(out_grad, image_weights, CONTRACT_FIRST)
            output = output.astype(BF16)
            blocks = QUERY_BLOCK // BLOCK_ROWS
            for block in range(blocks):
                slot = order_ref[chain * blocks + block]
                columns = pl.ds(pl.multiple_of((slot % 2) * HEAD_DIM, HEAD_DIM), HEAD_DIM)
                sent_ref[slot // 2, SHARE:, columns] = output[
                    block * BLOCK_ROWS : (block + 1) * BLOCK_ROWS
                ]
            return carry

        lax.fori_loop(0, PROMPT // QUERY_BLOCK, body, 0)

    @pl.when(step > 0)
    def _():
        def place(chain):
            start = (step - 1) * FORWARD_ROWS + chain * QUERY_BLOCK
            return pl.ds(pl.multiple_of(start, QUERY_BLOCK), QUERY_BLOCK)

        places = [chain_rows(chain) for chain in range(CHAINS)]
        scores = [text_scores(rows_ref[place(chain), :HEAD_DIM]) for chain in range(CHAINS)]
        weights = []
        for at, to_text in zip(places, scores):
            image_maximum = maximum_ref[at, :]
            maximum = jnp.maximum(image_maximum, jnp.max(to_text, axis=-1, keepdims=True))
            scale = jnp.exp2((image_maximum - maximum) * EXPONENT)
            weights.append((exp_rows(to_text, spread(maximum, PROMPT)), scale))
        middle = []
        for chain, (at, (text_weights, scale)) in enumerate(zip(places, weights)):
            both = matmul(text_weights, tv_ref[...])
            inverse = 1.0 / (both[:, HEAD_DIM:] + scale * total_ref[at, :])
            output = (scale * output_ref[at, :] + both[:, :HEAD_DIM]) * inverse
            cotangent = rows_ref[place(chain), 3 * HEAD_DIM :].astype(F32)
            out_grad = (cotangent * inverse).astype(BF16)
            image_out_grad = (cotangent * (scale * inverse)).astype(BF16)
            prob_grad = matmul(out_grad, text_values, CONTRACT_LAST)
            image_prob_grad = matmul(image_out_grad, values, CONTRACT_LAST)
            middle.append(
                (
                    (out_grad, row_sums(out_grad, output), prob_grad),
                    (image_out_grad, row_sums(image_out_grad, output), image_prob_grad),
                )
            )
            output = output.astype(BF16)
            for part in range(QUERY_BLOCK // SHARE):
                dest = ((step - 1) * FORWARD_ROWS + chain * QUERY_BLOCK) // SHARE + part
                sent_ref[dest, :SHARE, :HEAD_DIM] = output[part * SHARE : (part + 1) * SHARE]
        for chain, at in enumerate(places):
            queries = rows_ref[place(chain), :HEAD_DIM]
            (out_grad, row_delta, prob_grad), image_parts = middle[chain]
            image_out_grad, image_delta, image_prob_grad = image_parts
            text_weights, image_weights = weights[chain][0], weights_ref[at, :]
            text_scored = score_gradient(text_weights, prob_grad, row_delta)
            image_scored = score_gradient(image_weights, image_prob_grad, image_delta)
            query_grad = matmul(text_scored, text_keys) + matmul(image_scored, keys)
            query_grad = (query_grad * factor).astype(BF16)
            for part in range(QUERY_BLOCK // SHARE):
                dest = ((step - 1) * FORWARD_ROWS + chain * QUERY_BLOCK) // SHARE + part
                sent_ref[dest, :SHARE, HEAD_DIM : 2 * HEAD_DIM] = query_grad[
                    part * SHARE : (part + 1) * SHARE
                ]
            dkt_ref[...] += matmul(queries, text_scored, CONTRACT_FIRST)
            dvt_ref[...] += matmul(out_grad, text_weights, CONTRACT_FIRST)
            image_dkt_ref[...] += matmul(queries, image_scored, CONTRACT_FIRST)
            image_dvt_ref[...] += matmul(image_out_grad, image_weights, CONTRACT_FIRST)

    @pl.when(step == IMAGE // FORWARD_ROWS)
    def _():
        text_grad_ref[:, HEAD_DIM : 2 * HEAD_DIM] = (dkt_ref[...] * factor).T.astype(BF16)
        text_grad_ref[:, 2 * HEAD_DIM :] = dvt_ref[...].T.astype(BF16)
        stores = []
        for dest in range(HEADS):
            at = slice(dest * SHARE, (dest + 1) * SHARE)
            sent_ref[dest, :SHARE, 2 * HEAD_DIM : 3 * HEAD_DIM] = (
                (image_dkt_ref[:, at] * factor).T.astype(BF16)
            )
            sent_ref[dest, :SHARE, 3 * HEAD_DIM :] = image_dvt_ref[:, at].T.astype(BF16)
            if dest % 4 == 3:
                group = slice(dest - 3, dest + 1)
                store = pltpu.make_async_copy(
                    sent_ref.at[group], sent_hbm.at[group], stored.at[dest // 4]
                )
                store.start()
                stores.append(store)
        for store in stores:
            store.wait()


def grid_call(kernel, steps, in_specs, out_shape, out_specs, scratch, products):
    return pl.pallas_call(
        kernel,
        grid=(steps,),
        out_shape=out_shape,
        in_specs=in_specs,
        out_specs=out_specs,
        scratch_shapes=scratch,
        compiler_params=pltpu.CompilerParams(vmem_limit_bytes=WHOLE_VMEM),
        cost_estimate=pl.CostEstimate(
            flops=60 * products * HEAD_DIM, bytes_accessed=2**29, transcendentals=0
        ),
    )


IN_SMEM = pl.BlockSpec(memory_space=pltpu.SMEM)


def fixed(*shape):
    return pl.BlockSpec(shape, lambda step: (0,) * len(shape))


def per_block(rows, columns, skip=0):
    return pl.BlockSpec((rows, columns), lambda step: (jnp.maximum(step - skip, 0), 0))


def image_forward(order, packed):
    floats = jax.ShapeDtypeStruct((IMAGE, HEAD_DIM), F32)
    block = per_block(FORWARD_ROWS, HEAD_DIM)
    return grid_call(
        image_forward_kernel,
        IMAGE // FORWARD_ROWS,
        [IN_SMEM, fixed(HEADS, PACK_ROWS, PACK_COLS)],
        [rows_of(IMAGE, IMAGE), rows_of(IMAGE, PACK_COLS)] + [floats] * 3
        + [rows_of(PROMPT, HEAD_DIM)],
        [per_block(FORWARD_ROWS, IMAGE), per_block(FORWARD_ROWS, PACK_COLS)] + [block] * 3
        + [fixed(PROMPT, HEAD_DIM)],
        [pltpu.VMEM((IMAGE, HEAD_DIM), BF16), pltpu.VMEM((IMAGE, 2 * HEAD_DIM), BF16)],
        2 * IMAGE * IMAGE,
    )(order, packed)


def attention(length, order, text_rows, text_do, rows, weights, output, maximum, total):
    block = per_block(FORWARD_ROWS, HEAD_DIM, 1)
    text_sum = pltpu.VMEM((HEAD_DIM, PROMPT), F32)
    image_sum = pltpu.VMEM((HEAD_DIM, IMAGE), F32)
    return grid_call(
        attention_kernel,
        1 + IMAGE // FORWARD_ROWS,
        [IN_SMEM, IN_SMEM, fixed(PROMPT, 3 * HEAD_DIM), fixed(PROMPT, HEAD_DIM)]
        + [fixed(IMAGE, PACK_COLS), per_block(FORWARD_ROWS, IMAGE, 1)] + [block] * 3,
        [rows_of(HEADS, PACK_ROWS, PACK_COLS), rows_of(PROMPT, 3 * HEAD_DIM)],
        [pl.BlockSpec(memory_space=pltpu.HBM), fixed(PROMPT, 3 * HEAD_DIM)],
        [pltpu.VMEM((HEADS, PACK_ROWS, PACK_COLS), BF16), text_sum, text_sum, image_sum, image_sum]
        + [pltpu.VMEM((PROMPT, 2 * HEAD_DIM), BF16), pltpu.SemaphoreType.DMA((4,))],
        6 * TOTAL * TOTAL - 2 * IMAGE * IMAGE,
    )(length, order, text_rows, text_do, rows, weights, output, maximum, total)


def shift(rows, axis, step):
    size = 2 if axis in ("z_lo", "core") else 4
    return lax.ppermute(rows, axis, [(i, (i + step) % size) for i in range(size)])


def add(*rows):
    return sum(part.astype(F32) for part in rows)


def encode(place, context, residual, weight, gain, packed, order):
    other_weight = shift(weight, "core", 1)
    other = shift(context, "core", 1)
    other_weight, packed = lax.optimization_barrier((other_weight, packed))
    packed = lax.all_to_all(packed, SEQ, split_axis=0, concat_axis=0, tiled=True)
    chunks = whole_call(
        partial_kernel,
        [rows_of(TEXT_SHARE, WIDTH)] * 8,
        1,
        4,
        [pltpu.VMEM((8 * TEXT_SHARE, 2 * FEATURES), BF16)],
        2 * 8 * TEXT_SHARE * 2 * FEATURES * WIDTH,
        2**23,
    )(place, context, other, weight, other_weight)
    part = dict(zip(CHIPS, chunks))
    from_across = shift(part[2, 1], "z_lo", 1)
    from_below = shift(part[1, 1], "y", 1)
    from_above = shift(part[3, 1], "y", -1)
    below = shift(part[1, 0], "y", 1)
    above = shift(part[3, 0], "y", -1)
    opposite = add(part[2, 0], from_across).astype(BF16)
    across = add(part[0, 1], from_below, from_above).astype(BF16)
    packed, opposite, across = lax.optimization_barrier((packed, opposite, across))
    forward = image_forward(order, packed)
    opposite = shift(opposite, "y", 2)
    across = shift(across, "z_lo", 1)
    forward, opposite, across = lax.optimization_barrier((forward, opposite, across))
    stream = add(residual, part[0, 0], below, above, opposite, across)
    inv_norm = lax.rsqrt(jnp.mean(stream * stream, axis=-1, keepdims=True) + 1e-06)
    encoded = (stream * inv_norm * gain).astype(BF16)
    held = {(0, 0): encoded}
    held[0, 1] = shift(encoded, "z_lo", 1)
    held[3, 0] = shift(encoded, "y", 1)
    held[1, 0] = shift(encoded, "y", -1)
    held[2, 0] = shift(encoded, "y", 2)
    held[3, 1] = shift(held[0, 1], "y", 1)
    held[1, 1] = shift(held[0, 1], "y", -1)
    held[2, 1] = shift(held[2, 0], "z_lo", 1)
    early = [held[chip] for chip in CHIPS[:5] + CHIPS[6:7]]
    early = lax.optimization_barrier(early)
    held.update(zip(CHIPS[:5] + CHIPS[6:7], early))
    own = [held[chip] for chip in CHIPS]
    return own + [shift(rows, "core", 1) for rows in own], forward


def project(place, blocks, weight):
    columns = weight.shape[1]
    quarter = 4 * FEATURES
    in_vmem = pl.BlockSpec(memory_space=pltpu.VMEM)
    in_hbm = pl.BlockSpec(memory_space=pltpu.HBM)
    return pl.pallas_call(
        text_kernel,
        out_shape=[rows_of(PROMPT, columns), rows_of(PROMPT, quarter)]
        + [rows_of(HALF_PROMPT, quarter)] * 3,
        in_specs=[IN_SMEM] + [in_vmem] * 17,
        out_specs=[in_vmem] + [in_hbm] * 4,
        scratch_shapes=[
            pltpu.VMEM((PROMPT, WIDTH), BF16),
            pltpu.VMEM((PROMPT, columns), F32),
            pltpu.SemaphoreType.DMA((16,)),
        ],
        compiler_params=pltpu.CompilerParams(vmem_limit_bytes=VMEM_LIMIT),
        cost_estimate=pl.CostEstimate(
            flops=2 * PROMPT * WIDTH * columns, bytes_accessed=2**23, transcendentals=0
        ),
    )(place, *blocks, weight)


def weight_sums(place, kept, near, far, grads):
    columns = grads[0].shape[1]
    total = jax.ShapeDtypeStruct((columns, FEATURES), F32)
    kept_sum, *sent = whole_call(
        weight_kernel,
        [total] + [rows_of(columns, FEATURES)] * 3,
        1,
        11,
        [pltpu.VMEM((4, columns, FEATURES), F32)],
        12 * 2 * 4 * PROMPT * 4 * FEATURES * columns,
        2**23,
        WHOLE_VMEM,
    )(place, kept, *near, *far, *grads)
    return [kept_sum] + [shift(rows, "z_hi", step + 1) for step, rows in enumerate(sent)]


def weight_total(kept_sum, *parts):
    shape = jax.ShapeDtypeStruct(kept_sum.shape[::-1], F32)
    return whole_call(total_kernel, shape, 0, 4, [], 0, 2**20)(kept_sum, *parts)


def on_device(
    t5_context,
    t5_resid,
    t5_out_weight,
    t5_gain,
    text_weight,
    prompt_len,
    text_order,
    img_qkv,
    d_img_out,
    d_txt_out,
):
    packed = pack(img_qkv[0], d_img_out[0], d_txt_out[0])
    place = jnp.stack([lax.axis_index(axis) for axis in SEQ + GRP])
    blocks, forward = encode(
        place, t5_context[0], t5_resid[0], t5_out_weight, t5_gain, packed, text_order[0]
    )
    weights, rows, *stats, text_do = forward
    text_rows, kept, *slices = project(place, blocks, text_weight)
    near = [shift(rows, "x", step + 1) for step, rows in enumerate(slices)]
    sent, text_grad = attention(
        prompt_len, text_order[0], text_rows, text_do, rows, weights, *stats
    )
    *near, sent = lax.optimization_barrier((*near, sent))
    grads = [text_grad] + [shift(text_grad, "x", step) for step in (1, 2)] + [None]
    far = [shift(rows, "core", 1) for rows in near]
    last, far = lax.optimization_barrier((text_grad, far))
    grads[3] = shift(last, "x", 3)
    sums = weight_sums(place, kept, near, far, grads)
    received = lax.all_to_all(sent, SEQ, split_axis=0, concat_axis=0, tiled=True)
    outputs = unpack(received)
    sums, outputs = lax.optimization_barrier((sums, outputs))
    image_out, text_out, image_qkv_grad = outputs
    text_weight_grad = weight_total(*sums)
    return (image_out[None], text_out[None], image_qkv_grad[None], text_weight_grad)


def solution(mesh):
    fine = Mesh(mesh.devices.reshape(4, 4, 4, 2, 2), GRP + SEQ)
    in_specs = (
        P(GRP, None, SEQ),
        P(GRP, SEQ, None),
        P(SEQ, None),
        P(),
        P(None, SEQ),
        P(GRP),
        P(GRP, None),
        P(GRP, SEQ, None),
        P(GRP, SEQ, None),
        P(GRP, SEQ, None),
    )
    out_specs = (
        P(GRP, SEQ, None),
        P(GRP, SEQ, None),
        P(GRP, SEQ, None),
        P(GRP, SEQ),
    )
    return jax.shard_map(
        on_device, mesh=fine, in_specs=in_specs, out_specs=out_specs, check_vma=False
    )
```

```python
import jax
import jax.numpy as jnp
from jax import lax
from jax.experimental import pallas as pl
from jax.experimental.pallas import tpu as pltpu
from jax.sharding import Mesh
from jax.sharding import PartitionSpec as P

HEAD_DIM = 128
HEADS = 16
PROMPT = 512
IMAGE = 2048
TOTAL = PROMPT + IMAGE
BLOCK_ROWS = 16
TEXT_BLOCKS = 32
SHARE = IMAGE // HEADS
PACK_ROWS = SHARE + BLOCK_ROWS
PACK_COLS = 4 * HEAD_DIM
QUERY_BLOCK = 256
EXPONENT = HEAD_DIM**-0.5 * 1.4426950408889634
FORWARD_ROWS = 512
PACK_HEADS = 4
CHAINS = 2
WIDTH = 4096
FEATURES = WIDTH // HEADS
TEXT_SHARE = PROMPT // HEADS
HALF_PROMPT = PROMPT // 2
TEXT_DEPTH = 512
LATE_COST = 12
CHIPS = [(ahead, across) for ahead in range(4) for across in range(2)]

BF16 = jnp.bfloat16
F32 = jnp.float32
SEQ = ("y", "z_lo", "core")
GRP = ("z_hi", "x")
CONTRACT_LAST = (((1,), (1,)), ((), ()))
CONTRACT_FIRST = (((0,), (0,)), ((), ()))
VMEM_LIMIT = 48 * 2**20
WHOLE_VMEM = 60 * 2**20


def matmul(a, b, dims=(((1,), (0,)), ((), ()))):
    return lax.dot_general(a, b, dims, preferred_element_type=F32)


def pack_kernel(qkv_hbm, grad_hbm, text_hbm, packed_hbm, *refs):
    qkv_ref, grad_ref, text_ref, packed_ref, loaded, stored = refs
    loads = []
    for source, target in ((grad_hbm, grad_ref), (text_hbm, text_ref)):
        loads.append(pltpu.make_async_copy(source, target, loaded.at[len(loads)]))
    width = 3 * HEAD_DIM * PACK_HEADS
    for group in range(HEADS // PACK_HEADS):
        columns = slice(group * width, (group + 1) * width)
        source, target = qkv_hbm.at[:, columns], qkv_ref.at[:, columns]
        loads.append(pltpu.make_async_copy(source, target, loaded.at[len(loads)]))
    for load in loads:
        load.start()
    loads[0].wait()
    loads[1].wait()
    stores = []
    for group in range(HEADS // PACK_HEADS):
        loads[2 + group].wait()
        heads = slice(group * PACK_HEADS, (group + 1) * PACK_HEADS)
        for head in range(heads.start, heads.stop):
            columns = slice(head * HEAD_DIM, (head + 1) * HEAD_DIM)
            wide = slice(3 * head * HEAD_DIM, 3 * (head + 1) * HEAD_DIM)
            packed_ref[head, :SHARE, : 3 * HEAD_DIM] = qkv_ref[:, wide]
            packed_ref[head, :SHARE, 3 * HEAD_DIM :] = grad_ref[:, columns]
            packed_ref[head, SHARE:, :HEAD_DIM] = text_ref[:BLOCK_ROWS, columns]
            packed_ref[head, SHARE:, HEAD_DIM : 2 * HEAD_DIM] = text_ref[BLOCK_ROWS:, columns]
            packed_ref[head, SHARE:, 2 * HEAD_DIM :] = jnp.zeros(
                (BLOCK_ROWS, 2 * HEAD_DIM), BF16
            )
        store = pltpu.make_async_copy(
            packed_ref.at[heads], packed_hbm.at[heads], stored.at[group]
        )
        store.start()
        stores.append(store)
    for store in stores:
        store.wait()


def unpack_kernel(packed_ref, out_ref, text_ref, qkv_ref):
    for head in range(HEADS):
        columns = slice(head * HEAD_DIM, (head + 1) * HEAD_DIM)
        wide = slice(3 * head * HEAD_DIM, 3 * (head + 1) * HEAD_DIM)
        out_ref[:, columns] = packed_ref[head, :SHARE, :HEAD_DIM]
        qkv_ref[:, wide] = packed_ref[head, :SHARE, HEAD_DIM:]
        text_ref[:BLOCK_ROWS, columns] = packed_ref[head, SHARE:, :HEAD_DIM]
        text_ref[BLOCK_ROWS:, columns] = packed_ref[head, SHARE:, HEAD_DIM : 2 * HEAD_DIM]


def whole_call(kernel, out_shape, smem_inputs, vmem_inputs, scratch, flops, moved, limit=None):
    in_vmem = pl.BlockSpec(memory_space=pltpu.VMEM)
    in_smem = pl.BlockSpec(memory_space=pltpu.SMEM)
    return pl.pallas_call(
        kernel,
        out_shape=out_shape,
        in_specs=[in_smem] * smem_inputs + [in_vmem] * vmem_inputs,
        out_specs=jax.tree.map(lambda _: in_vmem, out_shape),
        scratch_shapes=scratch,
        compiler_params=pltpu.CompilerParams(vmem_limit_bytes=limit or VMEM_LIMIT),
        cost_estimate=pl.CostEstimate(flops=flops, bytes_accessed=moved, transcendentals=0),
    )


def rows_of(*shape):
    return jax.ShapeDtypeStruct(shape, BF16)


def pack(qkv, grad, text):
    anywhere = pl.BlockSpec(memory_space=pltpu.HBM)
    groups = HEADS // PACK_HEADS
    return pl.pallas_call(
        pack_kernel,
        out_shape=rows_of(HEADS, PACK_ROWS, PACK_COLS),
        in_specs=[anywhere] * 3,
        out_specs=anywhere,
        scratch_shapes=[
            pltpu.VMEM(qkv.shape, BF16),
            pltpu.VMEM(grad.shape, BF16),
            pltpu.VMEM(text.shape, BF16),
            pltpu.VMEM((HEADS, PACK_ROWS, PACK_COLS), BF16),
            pltpu.SemaphoreType.DMA((2 + groups,)),
            pltpu.SemaphoreType.DMA((groups,)),
        ],
        compiler_params=pltpu.CompilerParams(vmem_limit_bytes=WHOLE_VMEM),
        cost_estimate=pl.CostEstimate(flops=0, bytes_accessed=2**22, transcendentals=0),
    )(qkv, grad, text)


def unpack(packed):
    shapes = [
        rows_of(SHARE, HEADS * HEAD_DIM),
        rows_of(2 * BLOCK_ROWS, HEADS * HEAD_DIM),
        rows_of(SHARE, HEADS * 3 * HEAD_DIM),
    ]
    return whole_call(unpack_kernel, shapes, 0, 1, [], 0, 2**22)(packed)


def row_block(place_ref, ahead, across, other_core):
    y = lax.rem(place_ref[0] + ahead, 4)
    z = 1 - place_ref[1] if across else place_ref[1]
    core = 1 - place_ref[2] if other_core else place_ref[2]
    return (y * 2 + z) * 2 + core


def partial_kernel(place_ref, own_ref, other_ref, own_weight_ref, other_weight_ref, *refs):
    chunk_refs, rows_ref = refs[:8], refs[8]
    for index, (ahead, across) in enumerate(CHIPS):
        block = row_block(place_ref, ahead, across, False)
        rows = pl.ds(pl.multiple_of(block * TEXT_SHARE, TEXT_SHARE), TEXT_SHARE)
        to = slice(index * TEXT_SHARE, (index + 1) * TEXT_SHARE)
        rows_ref[to, :FEATURES] = own_ref[rows, :]
        rows_ref[to, FEATURES:] = other_ref[rows, :]

    def body(step, carry):
        columns = pl.ds(pl.multiple_of(step * 512, 512), 512)
        sums = matmul(rows_ref[:, :FEATURES], own_weight_ref[:, columns])
        sums += matmul(rows_ref[:, FEATURES:], other_weight_ref[:, columns])
        for index, chunk_ref in enumerate(chunk_refs):
            rows = slice(index * TEXT_SHARE, (index + 1) * TEXT_SHARE)
            chunk_ref[:, columns] = sums[rows].astype(BF16)
        return carry

    lax.fori_loop(0, WIDTH // 512, body, 0)


def text_kernel(place_ref, *refs):
    block_refs, weight_ref, text_ref = refs[:16], refs[16], refs[17]
    kept_hbm, sent_hbms, encoded_ref, total_ref, stored = refs[18], refs[19:22], *refs[22:]
    for index, block_ref in enumerate(block_refs):
        ahead, across = CHIPS[index % 8]
        block = row_block(place_ref, ahead, across, index >= 8)
        rows = pl.ds(pl.multiple_of(block * TEXT_SHARE, TEXT_SHARE), TEXT_SHARE)
        encoded_ref[rows, :] = block_ref[...]
    half = pl.ds(pl.multiple_of(place_ref[2] * HALF_PROMPT, HALF_PROMPT), HALF_PROMPT)
    stores = []
    for ahead in range(4):
        x = lax.rem(place_ref[4] + ahead, 4)
        for z_hi in range(4):
            at = pl.ds(pl.multiple_of((z_hi * 4 + x) * FEATURES, FEATURES), FEATURES)
            to = slice(z_hi * FEATURES, (z_hi + 1) * FEATURES)
            if ahead:
                source, target = encoded_ref.at[half, at], sent_hbms[ahead - 1].at[:, to]
            else:
                source, target = encoded_ref.at[:, at], kept_hbm.at[:, to]
            store = pltpu.make_async_copy(source, target, stored.at[len(stores)])
            store.start()
            stores.append(store)
    total_ref[...] = jnp.zeros_like(total_ref)

    def body(step, carry):
        depth = pl.ds(pl.multiple_of(step * TEXT_DEPTH, TEXT_DEPTH), TEXT_DEPTH)
        total_ref[...] += matmul(encoded_ref[:, depth], weight_ref[depth, :])
        return carry

    lax.fori_loop(0, WIDTH // TEXT_DEPTH, body, 0)
    text_ref[...] = total_ref[...].astype(BF16)
    for store in stores:
        store.wait()


def half_rows(place_ref):
    near = pl.ds(pl.multiple_of(place_ref[2] * HALF_PROMPT, HALF_PROMPT), HALF_PROMPT)
    far = pl.ds(pl.multiple_of((1 - place_ref[2]) * HALF_PROMPT, HALF_PROMPT), HALF_PROMPT)
    return near, far


def feature_block(place_ref, ahead):
    z_hi = lax.rem(place_ref[3] + ahead, 4)
    return pl.ds(pl.multiple_of(z_hi * FEATURES, FEATURES), FEATURES)


def early_weight_kernel(place_ref, kept_ref, near_ref, far_ref, own_ref, grad_ref, totals_ref):
    near, far = half_rows(place_ref)

    def body(ahead, carry):
        at = feature_block(place_ref, ahead)
        total = matmul(own_ref[...], kept_ref[:, at], CONTRACT_FIRST)
        total += matmul(grad_ref[near, :], near_ref[:, at], CONTRACT_FIRST)
        totals_ref[ahead] = total + matmul(grad_ref[far, :], far_ref[:, at], CONTRACT_FIRST)
        return carry

    lax.fori_loop(0, 4, body, 0)


def late_weight_kernel(place_ref, early_ref, *refs):
    near_refs, far_refs, grad_refs = refs[:2], refs[2:4], refs[4:6]
    kept_sum_ref, sent_refs, totals_ref = refs[6], refs[7:10], refs[10]
    near, far = half_rows(place_ref)

    def body(ahead, carry):
        at = feature_block(place_ref, ahead)
        total = early_ref[ahead]
        for grad_ref, near_ref, far_ref in zip(grad_refs, near_refs, far_refs):
            total += matmul(grad_ref[near, :], near_ref[:, at], CONTRACT_FIRST)
            total += matmul(grad_ref[far, :], far_ref[:, at], CONTRACT_FIRST)
        totals_ref[ahead] = total
        return carry

    lax.fori_loop(0, 4, body, 0)
    kept_sum_ref[...] = totals_ref[0]
    for step, sent_ref in enumerate(sent_refs):
        sent_ref[...] = totals_ref[step + 1].astype(BF16)


def total_kernel(kept_ref, *refs):
    total = kept_ref[...]
    for part_ref in refs[:3]:
        total += part_ref[...].astype(F32)
    refs[3][...] = total.T


def exp_rows(scores, maximum):
    return jnp.exp2((scores - maximum) * EXPONENT).astype(BF16)


def spread(rows, columns):
    return jnp.concatenate([rows] * (columns // HEAD_DIM), axis=1)


def row_sums(out_grad, output):
    total = jnp.sum(out_grad.astype(F32) * output, axis=-1, keepdims=True)
    return jnp.broadcast_to(total, output.shape)


def score_gradient(weights, prob_grad, row_delta):
    wide = spread(row_delta, weights.shape[1])
    return (weights.astype(F32) * (prob_grad - wide)).astype(BF16)


def chains(count, first, then):
    ahead = first(0)
    for chain in range(count):
        current = ahead
        if chain + 1 < count:
            ahead = first(chain + 1)
        then(chain, current)


def chain_rows(chain):
    return slice(chain * QUERY_BLOCK, (chain + 1) * QUERY_BLOCK)


def image_forward_kernel(
    order_ref,
    packed_ref,
    weights_ref,
    rows_ref,
    output_ref,
    maximum_ref,
    total_ref,
    text_do_ref,
    k_ref,
    v_ref,
):
    step = pl.program_id(0)

    @pl.when(step == 0)
    def _():
        v_ref[:, HEAD_DIM:] = jnp.ones((IMAGE, HEAD_DIM), BF16)
        for src in range(HEADS):
            at = slice(src * SHARE, (src + 1) * SHARE)
            k_ref[at, :] = packed_ref[src, :SHARE, HEAD_DIM : 2 * HEAD_DIM]
            v_ref[at, :HEAD_DIM] = packed_ref[src, :SHARE, 2 * HEAD_DIM : 3 * HEAD_DIM]
        for block in range(TEXT_BLOCKS):
            slot = order_ref[block]
            columns = pl.ds(pl.multiple_of((slot % 2) * HEAD_DIM, HEAD_DIM), HEAD_DIM)
            text_do_ref[block * BLOCK_ROWS : (block + 1) * BLOCK_ROWS, :] = packed_ref[
                slot // 2, SHARE:, columns
            ]

    parts = FORWARD_ROWS // SHARE
    for part in range(parts):
        at = slice(part * SHARE, (part + 1) * SHARE)
        rows_ref[at, :] = packed_ref[step * parts + part, :SHARE, :]

    def first(chain):
        return matmul(rows_ref[chain_rows(chain), :HEAD_DIM], k_ref[...], CONTRACT_LAST)

    def then(chain, scores):
        at = chain_rows(chain)
        maximum = jnp.max(scores, axis=-1, keepdims=True)
        weights = exp_rows(scores, maximum)
        weights_ref[at, :] = weights
        both = matmul(weights, v_ref[...])
        output_ref[at, :] = both[:, :HEAD_DIM]
        total_ref[at, :] = both[:, HEAD_DIM:]
        maximum_ref[at, :] = jnp.broadcast_to(maximum, (QUERY_BLOCK, HEAD_DIM))

    chains(FORWARD_ROWS // QUERY_BLOCK, first, then)


def attention_kernel(
    length_ref,
    order_ref,
    text_ref,
    text_do_ref,
    rows_ref,
    weights_ref,
    output_ref,
    maximum_ref,
    total_ref,
    sent_hbm,
    text_grad_ref,
    sent_ref,
    dkt_ref,
    dvt_ref,
    image_dkt_ref,
    image_dvt_ref,
    tv_ref,
    stored,
):
    step = pl.program_id(0)
    factor = HEAD_DIM**-0.5
    text_keys = text_ref[:, HEAD_DIM : 2 * HEAD_DIM]
    text_values = text_ref[:, 2 * HEAD_DIM :]
    keys = rows_ref[:, HEAD_DIM : 2 * HEAD_DIM]
    values = rows_ref[:, 2 * HEAD_DIM : 3 * HEAD_DIM]
    live = lax.broadcasted_iota(jnp.int32, (1, PROMPT), 1) < length_ref[0]
    sums = (dkt_ref, dvt_ref, image_dkt_ref, image_dvt_ref)

    def text_scores(queries):
        return jnp.where(live, matmul(queries, text_keys, CONTRACT_LAST), -1e30)

    @pl.when(step == 0)
    def _():
        tv_ref[:, :HEAD_DIM] = text_values
        tv_ref[:, HEAD_DIM:] = jnp.ones((PROMPT, HEAD_DIM), BF16)
        sent_ref[:, SHARE:, 2 * HEAD_DIM :] = jnp.zeros((HEADS, BLOCK_ROWS, 2 * HEAD_DIM), BF16)
        for sum_ref in sums:
            sum_ref[...] = jnp.zeros_like(sum_ref)

        def body(chain, carry):
            rows = pl.ds(pl.multiple_of(chain * QUERY_BLOCK, QUERY_BLOCK), QUERY_BLOCK)
            queries = text_ref[rows, :HEAD_DIM]
            to_text = text_scores(queries)
            to_image = matmul(queries, keys, CONTRACT_LAST)
            maximum = jnp.maximum(
                jnp.max(to_text, axis=-1, keepdims=True), jnp.max(to_image, axis=-1, keepdims=True)
            )
            text_weights, image_weights = exp_rows(to_text, maximum), exp_rows(to_image, maximum)
            total = jnp.sum(image_weights.astype(F32), axis=-1, keepdims=True)
            both = matmul(text_weights, tv_ref[...])
            inverse = 1.0 / (both[:, HEAD_DIM:] + total)
            output = (both[:, :HEAD_DIM] + matmul(image_weights, values)) * inverse
            out_grad = (text_do_ref[rows, :].astype(F32) * inverse).astype(BF16)
            row_delta = row_sums(out_grad, output)
            prob_grads = [matmul(out_grad, part, CONTRACT_LAST) for part in (text_values, values)]
            text_scored = score_gradient(text_weights, prob_grads[0], row_delta)
            image_scored = score_gradient(image_weights, prob_grads[1], row_delta)
            query_grad = matmul(text_scored, text_keys) + matmul(image_scored, keys)
            text_grad_ref[rows, :HEAD_DIM] = (query_grad * factor).astype(BF16)
            dkt_ref[...] += matmul(queries, text_scored, CONTRACT_FIRST)
            dvt_ref[...] += matmul(out_grad, text_weights, CONTRACT_FIRST)
            image_dkt_ref[...] += matmul(queries, image_scored, CONTRACT_FIRST)
            image_dvt_ref[...] += matmul(out_grad, image_weights, CONTRACT_FIRST)
            output = output.astype(BF16)
            blocks = QUERY_BLOCK // BLOCK_ROWS
            for block in range(blocks):
                slot = order_ref[chain * blocks + block]
                columns = pl.ds(pl.multiple_of((slot % 2) * HEAD_DIM, HEAD_DIM), HEAD_DIM)
                sent_ref[slot // 2, SHARE:, columns] = output[
                    block * BLOCK_ROWS : (block + 1) * BLOCK_ROWS
                ]
            return carry

        lax.fori_loop(0, PROMPT // QUERY_BLOCK, body, 0)

    @pl.when(step > 0)
    def _():
        def place(chain):
            start = (step - 1) * FORWARD_ROWS + chain * QUERY_BLOCK
            return pl.ds(pl.multiple_of(start, QUERY_BLOCK), QUERY_BLOCK)

        places = [chain_rows(chain) for chain in range(CHAINS)]
        scores = [text_scores(rows_ref[place(chain), :HEAD_DIM]) for chain in range(CHAINS)]
        weights = []
        for at, to_text in zip(places, scores):
            image_maximum = maximum_ref[at, :]
            maximum = jnp.maximum(image_maximum, jnp.max(to_text, axis=-1, keepdims=True))
            scale = jnp.exp2((image_maximum - maximum) * EXPONENT)
            weights.append((exp_rows(to_text, spread(maximum, PROMPT)), scale))
        middle = []
        for chain, (at, (text_weights, scale)) in enumerate(zip(places, weights)):
            both = matmul(text_weights, tv_ref[...])
            inverse = 1.0 / (both[:, HEAD_DIM:] + scale * total_ref[at, :])
            output = (scale * output_ref[at, :] + both[:, :HEAD_DIM]) * inverse
            cotangent = rows_ref[place(chain), 3 * HEAD_DIM :].astype(F32)
            out_grad = (cotangent * inverse).astype(BF16)
            image_out_grad = (cotangent * (scale * inverse)).astype(BF16)
            prob_grad = matmul(out_grad, text_values, CONTRACT_LAST)
            image_prob_grad = matmul(image_out_grad, values, CONTRACT_LAST)
            middle.append(
                (
                    (out_grad, row_sums(out_grad, output), prob_grad),
                    (image_out_grad, row_sums(image_out_grad, output), image_prob_grad),
                )
            )
            output = output.astype(BF16)
            for part in range(QUERY_BLOCK // SHARE):
                dest = ((step - 1) * FORWARD_ROWS + chain * QUERY_BLOCK) // SHARE + part
                sent_ref[dest, :SHARE, :HEAD_DIM] = output[part * SHARE : (part + 1) * SHARE]
        for chain, at in enumerate(places):
            queries = rows_ref[place(chain), :HEAD_DIM]
            (out_grad, row_delta, prob_grad), image_parts = middle[chain]
            image_out_grad, image_delta, image_prob_grad = image_parts
            text_weights, image_weights = weights[chain][0], weights_ref[at, :]
            text_scored = score_gradient(text_weights, prob_grad, row_delta)
            image_scored = score_gradient(image_weights, image_prob_grad, image_delta)
            query_grad = matmul(text_scored, text_keys) + matmul(image_scored, keys)
            query_grad = (query_grad * factor).astype(BF16)
            for part in range(QUERY_BLOCK // SHARE):
                dest = ((step - 1) * FORWARD_ROWS + chain * QUERY_BLOCK) // SHARE + part
                sent_ref[dest, :SHARE, HEAD_DIM : 2 * HEAD_DIM] = query_grad[
                    part * SHARE : (part + 1) * SHARE
                ]
            dkt_ref[...] += matmul(queries, text_scored, CONTRACT_FIRST)
            dvt_ref[...] += matmul(out_grad, text_weights, CONTRACT_FIRST)
            image_dkt_ref[...] += matmul(queries, image_scored, CONTRACT_FIRST)
            image_dvt_ref[...] += matmul(image_out_grad, image_weights, CONTRACT_FIRST)

    @pl.when(step == IMAGE // FORWARD_ROWS)
    def _():
        text_grad_ref[:, HEAD_DIM : 2 * HEAD_DIM] = (dkt_ref[...] * factor).T.astype(BF16)
        text_grad_ref[:, 2 * HEAD_DIM :] = dvt_ref[...].T.astype(BF16)
        stores = []
        for dest in range(HEADS):
            at = slice(dest * SHARE, (dest + 1) * SHARE)
            sent_ref[dest, :SHARE, 2 * HEAD_DIM : 3 * HEAD_DIM] = (
                (image_dkt_ref[:, at] * factor).T.astype(BF16)
            )
            sent_ref[dest, :SHARE, 3 * HEAD_DIM :] = image_dvt_ref[:, at].T.astype(BF16)
            if dest % 4 == 3:
                group = slice(dest - 3, dest + 1)
                store = pltpu.make_async_copy(
                    sent_ref.at[group], sent_hbm.at[group], stored.at[dest // 4]
                )
                store.start()
                stores.append(store)
        for store in stores:
            store.wait()


def grid_call(kernel, steps, in_specs, out_shape, out_specs, scratch, products, limit):
    return pl.pallas_call(
        kernel,
        grid=(steps,),
        out_shape=out_shape,
        in_specs=in_specs,
        out_specs=out_specs,
        scratch_shapes=scratch,
        compiler_params=pltpu.CompilerParams(vmem_limit_bytes=limit),
        cost_estimate=pl.CostEstimate(
            flops=60 * products * HEAD_DIM, bytes_accessed=2**29, transcendentals=0
        ),
    )


IN_SMEM = pl.BlockSpec(memory_space=pltpu.SMEM)


def fixed(*shape):
    return pl.BlockSpec(shape, lambda step: (0,) * len(shape))


def per_block(rows, columns, skip=0):
    return pl.BlockSpec((rows, columns), lambda step: (jnp.maximum(step - skip, 0), 0))


def image_forward(order, packed):
    floats = jax.ShapeDtypeStruct((IMAGE, HEAD_DIM), F32)
    block = per_block(FORWARD_ROWS, HEAD_DIM)
    return grid_call(
        image_forward_kernel,
        IMAGE // FORWARD_ROWS,
        [IN_SMEM, fixed(HEADS, PACK_ROWS, PACK_COLS)],
        [rows_of(IMAGE, IMAGE), rows_of(IMAGE, PACK_COLS)] + [floats] * 3
        + [rows_of(PROMPT, HEAD_DIM)],
        [per_block(FORWARD_ROWS, IMAGE), per_block(FORWARD_ROWS, PACK_COLS)] + [block] * 3
        + [fixed(PROMPT, HEAD_DIM)],
        [pltpu.VMEM((IMAGE, HEAD_DIM), BF16), pltpu.VMEM((IMAGE, 2 * HEAD_DIM), BF16)],
        2 * IMAGE * IMAGE,
        WHOLE_VMEM,
    )(order, packed)


def attention(length, order, text_rows, text_do, rows, weights, output, maximum, total):
    block = per_block(FORWARD_ROWS, HEAD_DIM, 1)
    text_sum = pltpu.VMEM((HEAD_DIM, PROMPT), F32)
    image_sum = pltpu.VMEM((HEAD_DIM, IMAGE), F32)
    return grid_call(
        attention_kernel,
        1 + IMAGE // FORWARD_ROWS,
        [IN_SMEM, IN_SMEM, fixed(PROMPT, 3 * HEAD_DIM), fixed(PROMPT, HEAD_DIM)]
        + [fixed(IMAGE, PACK_COLS), per_block(FORWARD_ROWS, IMAGE, 1)] + [block] * 3,
        [rows_of(HEADS, PACK_ROWS, PACK_COLS), rows_of(PROMPT, 3 * HEAD_DIM)],
        [pl.BlockSpec(memory_space=pltpu.HBM), fixed(PROMPT, 3 * HEAD_DIM)],
        [pltpu.VMEM((HEADS, PACK_ROWS, PACK_COLS), BF16), text_sum, text_sum, image_sum, image_sum]
        + [pltpu.VMEM((PROMPT, 2 * HEAD_DIM), BF16), pltpu.SemaphoreType.DMA((4,))],
        6 * TOTAL * TOTAL - 2 * IMAGE * IMAGE,
        WHOLE_VMEM,
    )(length, order, text_rows, text_do, rows, weights, output, maximum, total)


def shift(rows, axis, step):
    size = 2 if axis in ("z_lo", "core") else 4
    return lax.ppermute(rows, axis, [(i, (i + step) % size) for i in range(size)])


def add(*rows):
    return sum(part.astype(F32) for part in rows)


def encode(place, context, residual, weight, gain, packed, order):
    other_weight = shift(weight, "core", 1)
    other = shift(context, "core", 1)
    packed = lax.all_to_all(packed, SEQ, split_axis=0, concat_axis=0, tiled=True)
    chunks = whole_call(
        partial_kernel,
        [rows_of(TEXT_SHARE, WIDTH)] * 8,
        1,
        4,
        [pltpu.VMEM((8 * TEXT_SHARE, 2 * FEATURES), BF16)],
        2 * 8 * TEXT_SHARE * 2 * FEATURES * WIDTH,
        2**23,
    )(place, context, other, weight, other_weight)
    part = dict(zip(CHIPS, chunks))
    from_across = shift(part[2, 1], "z_lo", 1)
    from_below = shift(part[1, 1], "y", 1)
    from_above = shift(part[3, 1], "y", -1)
    below = shift(part[1, 0], "y", 1)
    above = shift(part[3, 0], "y", -1)
    opposite = add(part[2, 0], from_across).astype(BF16)
    across = add(part[0, 1], from_below, from_above).astype(BF16)
    packed, opposite, across = lax.optimization_barrier((packed, opposite, across))
    forward = image_forward(order, packed)
    opposite = shift(opposite, "y", 2)
    across = shift(across, "z_lo", 1)
    forward, opposite, across = lax.optimization_barrier((forward, opposite, across))
    stream = add(residual, part[0, 0], below, above, opposite, across)
    inv_norm = lax.rsqrt(jnp.mean(stream * stream, axis=-1, keepdims=True) + 1e-06)
    encoded = (stream * inv_norm * gain).astype(BF16)
    held = {(0, 0): encoded}
    held[0, 1] = shift(encoded, "z_lo", 1)
    held[3, 0] = shift(encoded, "y", 1)
    held[1, 0] = shift(encoded, "y", -1)
    held[2, 0] = shift(encoded, "y", 2)
    held[3, 1] = shift(held[0, 1], "y", 1)
    held[1, 1] = shift(held[0, 1], "y", -1)
    held[2, 1] = shift(held[2, 0], "z_lo", 1)
    early = [held[chip] for chip in CHIPS[:5] + CHIPS[6:7]]
    early = lax.optimization_barrier(early)
    held.update(zip(CHIPS[:5] + CHIPS[6:7], early))
    own = [held[chip] for chip in CHIPS]
    return own + [shift(rows, "core", 1) for rows in own], forward


def project(place, blocks, weight):
    columns = weight.shape[1]
    quarter = 4 * FEATURES
    in_vmem = pl.BlockSpec(memory_space=pltpu.VMEM)
    in_hbm = pl.BlockSpec(memory_space=pltpu.HBM)
    return pl.pallas_call(
        text_kernel,
        out_shape=[rows_of(PROMPT, columns), rows_of(PROMPT, quarter)]
        + [rows_of(HALF_PROMPT, quarter)] * 3,
        in_specs=[IN_SMEM] + [in_vmem] * 17,
        out_specs=[in_vmem] + [in_hbm] * 4,
        scratch_shapes=[
            pltpu.VMEM((PROMPT, WIDTH), BF16),
            pltpu.VMEM((PROMPT, columns), F32),
            pltpu.SemaphoreType.DMA((16,)),
        ],
        compiler_params=pltpu.CompilerParams(vmem_limit_bytes=VMEM_LIMIT),
        cost_estimate=pl.CostEstimate(
            flops=2 * PROMPT * WIDTH * columns, bytes_accessed=2**23, transcendentals=0
        ),
    )(place, *blocks, weight)


def weight_sums(place, kept, near, far, grads):
    columns = grads[0].shape[1]
    half = 4 * PROMPT * 4 * FEATURES * columns
    totals = jax.ShapeDtypeStruct((4, columns, FEATURES), F32)
    early = whole_call(early_weight_kernel, totals, 1, 5, [], half, 2**22, WHOLE_VMEM)(
        place, kept, near[0], far[0], grads[0], grads[1]
    )
    kept_sum, *sent = whole_call(
        late_weight_kernel,
        [jax.ShapeDtypeStruct((columns, FEATURES), F32)] + [rows_of(columns, FEATURES)] * 3,
        1,
        7,
        [pltpu.VMEM((4, columns, FEATURES), F32)],
        LATE_COST * half,
        2**22,
        WHOLE_VMEM,
    )(place, early, *near[1:], *far[1:], *grads[2:])
    parts = [None] * 3
    for step in (2, 1, 3):
        parts[step - 1] = shift(sent[step - 1], "z_hi", step)
    return [kept_sum] + parts


def weight_total(kept_sum, *parts):
    shape = jax.ShapeDtypeStruct(kept_sum.shape[::-1], F32)
    return whole_call(total_kernel, shape, 0, 4, [], 0, 2**20)(kept_sum, *parts)


def on_device(
    t5_context,
    t5_resid,
    t5_out_weight,
    t5_gain,
    text_weight,
    prompt_len,
    text_order,
    img_qkv,
    d_img_out,
    d_txt_out,
):
    packed = pack(img_qkv[0], d_img_out[0], d_txt_out[0])
    place = jnp.stack([lax.axis_index(axis) for axis in SEQ + GRP])
    blocks, forward = encode(
        place, t5_context[0], t5_resid[0], t5_out_weight, t5_gain, packed, text_order[0]
    )
    weights, rows, *stats, text_do = forward
    text_rows, kept, *slices = project(place, blocks, text_weight)
    near = [shift(rows, "x", step + 1) for step, rows in enumerate(slices)]
    sent, text_grad = attention(
        prompt_len, text_order[0], text_rows, text_do, rows, weights, *stats
    )
    *near, sent = lax.optimization_barrier((*near, sent))
    grads = [text_grad] + [shift(text_grad, "x", step) for step in (1, 2)] + [None]
    far = [shift(rows, "core", 1) for rows in near]
    last, far = lax.optimization_barrier((text_grad, far))
    grads[3] = shift(last, "x", 3)
    sums = weight_sums(place, kept, near, far, grads)
    received = lax.all_to_all(sent, SEQ, split_axis=0, concat_axis=0, tiled=True)
    outputs = unpack(received)
    sums, outputs = lax.optimization_barrier((sums, outputs))
    image_out, text_out, image_qkv_grad = outputs
    text_weight_grad = weight_total(*sums)
    return (image_out[None], text_out[None], image_qkv_grad[None], text_weight_grad)


def solution(mesh):
    fine = Mesh(mesh.devices.reshape(4, 4, 4, 2, 2), GRP + SEQ)
    in_specs = (
        P(GRP, None, SEQ),
        P(GRP, SEQ, None),
        P(SEQ, None),
        P(),
        P(None, SEQ),
        P(GRP),
        P(GRP, None),
        P(GRP, SEQ, None),
        P(GRP, SEQ, None),
        P(GRP, SEQ, None),
    )
    out_specs = (
        P(GRP, SEQ, None),
        P(GRP, SEQ, None),
        P(GRP, SEQ, None),
        P(GRP, SEQ),
    )
    return jax.shard_map(
        on_device, mesh=fine, in_specs=in_specs, out_specs=out_specs, check_vma=False
    )
```

```python
import jax
import jax.numpy as jnp
from jax import lax
from jax.experimental import pallas as pl
from jax.experimental.pallas import tpu as pltpu
from jax.sharding import Mesh
from jax.sharding import PartitionSpec as P

HEAD_DIM = 128
HEADS = 16
PROMPT = 512
IMAGE = 2048
TOTAL = PROMPT + IMAGE
BLOCK_ROWS = 16
TEXT_BLOCKS = 32
SHARE = IMAGE // HEADS
PACK_ROWS = SHARE + BLOCK_ROWS
PACK_COLS = 4 * HEAD_DIM
QUERY_BLOCK = 256
EXPONENT = HEAD_DIM**-0.5 * 1.4426950408889634
FORWARD_ROWS = 512
PACK_HEADS = 4
CHAINS = 2
WIDTH = 4096
FEATURES = WIDTH // HEADS
TEXT_SHARE = PROMPT // HEADS
HALF_PROMPT = PROMPT // 2
TEXT_DEPTH = 1024
CHIPS = [(ahead, across) for ahead in range(4) for across in range(2)]

BF16 = jnp.bfloat16
F32 = jnp.float32
SEQ = ("y", "z_lo", "core")
GRP = ("z_hi", "x")
CONTRACT_LAST = (((1,), (1,)), ((), ()))
CONTRACT_FIRST = (((0,), (0,)), ((), ()))
VMEM_LIMIT = 48 * 2**20
WHOLE_VMEM = 60 * 2**20


def matmul(a, b, dims=(((1,), (0,)), ((), ()))):
    return lax.dot_general(a, b, dims, preferred_element_type=F32)


def pack_kernel(qkv_hbm, grad_hbm, text_hbm, packed_hbm, *refs):
    qkv_ref, grad_ref, text_ref, packed_ref, loaded, stored = refs
    loads = []
    for source, target in ((grad_hbm, grad_ref), (text_hbm, text_ref)):
        loads.append(pltpu.make_async_copy(source, target, loaded.at[len(loads)]))
    width = 3 * HEAD_DIM * PACK_HEADS
    for group in range(HEADS // PACK_HEADS):
        columns = slice(group * width, (group + 1) * width)
        source, target = qkv_hbm.at[:, columns], qkv_ref.at[:, columns]
        loads.append(pltpu.make_async_copy(source, target, loaded.at[len(loads)]))
    for load in loads:
        load.start()
    loads[0].wait()
    loads[1].wait()
    stores = []
    for group in range(HEADS // PACK_HEADS):
        loads[2 + group].wait()
        heads = slice(group * PACK_HEADS, (group + 1) * PACK_HEADS)
        for head in range(heads.start, heads.stop):
            columns = slice(head * HEAD_DIM, (head + 1) * HEAD_DIM)
            wide = slice(3 * head * HEAD_DIM, 3 * (head + 1) * HEAD_DIM)
            packed_ref[head, :SHARE, : 3 * HEAD_DIM] = qkv_ref[:, wide]
            packed_ref[head, :SHARE, 3 * HEAD_DIM :] = grad_ref[:, columns]
            packed_ref[head, SHARE:, :HEAD_DIM] = text_ref[:BLOCK_ROWS, columns]
            packed_ref[head, SHARE:, HEAD_DIM : 2 * HEAD_DIM] = text_ref[BLOCK_ROWS:, columns]
            packed_ref[head, SHARE:, 2 * HEAD_DIM :] = jnp.zeros(
                (BLOCK_ROWS, 2 * HEAD_DIM), BF16
            )
        store = pltpu.make_async_copy(
            packed_ref.at[heads], packed_hbm.at[heads], stored.at[group]
        )
        store.start()
        stores.append(store)
    for store in stores:
        store.wait()


def unpack_kernel(packed_ref, out_ref, text_ref, qkv_ref):
    for head in range(HEADS):
        columns = slice(head * HEAD_DIM, (head + 1) * HEAD_DIM)
        wide = slice(3 * head * HEAD_DIM, 3 * (head + 1) * HEAD_DIM)
        out_ref[:, columns] = packed_ref[head, :SHARE, :HEAD_DIM]
        qkv_ref[:, wide] = packed_ref[head, :SHARE, HEAD_DIM:]
        text_ref[:BLOCK_ROWS, columns] = packed_ref[head, SHARE:, :HEAD_DIM]
        text_ref[BLOCK_ROWS:, columns] = packed_ref[head, SHARE:, HEAD_DIM : 2 * HEAD_DIM]


def whole_call(kernel, out_shape, smem_inputs, vmem_inputs, scratch, flops, moved, limit=None):
    in_vmem = pl.BlockSpec(memory_space=pltpu.VMEM)
    in_smem = pl.BlockSpec(memory_space=pltpu.SMEM)
    return pl.pallas_call(
        kernel,
        out_shape=out_shape,
        in_specs=[in_smem] * smem_inputs + [in_vmem] * vmem_inputs,
        out_specs=jax.tree.map(lambda _: in_vmem, out_shape),
        scratch_shapes=scratch,
        compiler_params=pltpu.CompilerParams(vmem_limit_bytes=limit or VMEM_LIMIT),
        cost_estimate=pl.CostEstimate(flops=flops, bytes_accessed=moved, transcendentals=0),
    )


def rows_of(*shape):
    return jax.ShapeDtypeStruct(shape, BF16)


def pack(qkv, grad, text):
    anywhere = pl.BlockSpec(memory_space=pltpu.HBM)
    groups = HEADS // PACK_HEADS
    return pl.pallas_call(
        pack_kernel,
        out_shape=rows_of(HEADS, PACK_ROWS, PACK_COLS),
        in_specs=[anywhere] * 3,
        out_specs=anywhere,
        scratch_shapes=[
            pltpu.VMEM(qkv.shape, BF16),
            pltpu.VMEM(grad.shape, BF16),
            pltpu.VMEM(text.shape, BF16),
            pltpu.VMEM((HEADS, PACK_ROWS, PACK_COLS), BF16),
            pltpu.SemaphoreType.DMA((2 + groups,)),
            pltpu.SemaphoreType.DMA((groups,)),
        ],
        compiler_params=pltpu.CompilerParams(vmem_limit_bytes=WHOLE_VMEM),
        cost_estimate=pl.CostEstimate(flops=0, bytes_accessed=2**22, transcendentals=0),
    )(qkv, grad, text)


def unpack(packed):
    shapes = [
        rows_of(SHARE, HEADS * HEAD_DIM),
        rows_of(2 * BLOCK_ROWS, HEADS * HEAD_DIM),
        rows_of(SHARE, HEADS * 3 * HEAD_DIM),
    ]
    return whole_call(unpack_kernel, shapes, 0, 1, [], 0, 2**22)(packed)


def row_block(place_ref, ahead, across, other_core):
    y = lax.rem(place_ref[0] + ahead, 4)
    z = 1 - place_ref[1] if across else place_ref[1]
    core = 1 - place_ref[2] if other_core else place_ref[2]
    return (y * 2 + z) * 2 + core


def partial_kernel(place_ref, own_ref, other_ref, own_weight_ref, other_weight_ref, *refs):
    chunk_refs, rows_ref = refs[:8], refs[8]
    for index, (ahead, across) in enumerate(CHIPS):
        block = row_block(place_ref, ahead, across, False)
        rows = pl.ds(pl.multiple_of(block * TEXT_SHARE, TEXT_SHARE), TEXT_SHARE)
        to = slice(index * TEXT_SHARE, (index + 1) * TEXT_SHARE)
        rows_ref[to, :FEATURES] = own_ref[rows, :]
        rows_ref[to, FEATURES:] = other_ref[rows, :]

    def body(step, carry):
        columns = pl.ds(pl.multiple_of(step * 512, 512), 512)
        sums = matmul(rows_ref[:, :FEATURES], own_weight_ref[:, columns])
        sums += matmul(rows_ref[:, FEATURES:], other_weight_ref[:, columns])
        for index, chunk_ref in enumerate(chunk_refs):
            rows = slice(index * TEXT_SHARE, (index + 1) * TEXT_SHARE)
            chunk_ref[:, columns] = sums[rows].astype(BF16)
        return carry

    lax.fori_loop(0, WIDTH // 512, body, 0)


def text_kernel(place_ref, *refs):
    block_refs, weight_ref, text_ref = refs[:16], refs[16], refs[17]
    kept_hbm, sent_hbms, encoded_ref, total_ref, stored = refs[18], refs[19:22], *refs[22:]
    for index, block_ref in enumerate(block_refs):
        ahead, across = CHIPS[index % 8]
        block = row_block(place_ref, ahead, across, index >= 8)
        rows = pl.ds(pl.multiple_of(block * TEXT_SHARE, TEXT_SHARE), TEXT_SHARE)
        encoded_ref[rows, :] = block_ref[...]
    half = pl.ds(pl.multiple_of(place_ref[2] * HALF_PROMPT, HALF_PROMPT), HALF_PROMPT)
    stores = []
    for ahead in range(4):
        x = lax.rem(place_ref[4] + ahead, 4)
        for z_hi in range(4):
            at = pl.ds(pl.multiple_of((z_hi * 4 + x) * FEATURES, FEATURES), FEATURES)
            to = slice(z_hi * FEATURES, (z_hi + 1) * FEATURES)
            if ahead:
                source, target = encoded_ref.at[half, at], sent_hbms[ahead - 1].at[:, to]
            else:
                source, target = encoded_ref.at[:, at], kept_hbm.at[:, to]
            store = pltpu.make_async_copy(source, target, stored.at[len(stores)])
            store.start()
            stores.append(store)
    total_ref[...] = jnp.zeros_like(total_ref)

    def body(step, carry):
        depth = pl.ds(pl.multiple_of(step * TEXT_DEPTH, TEXT_DEPTH), TEXT_DEPTH)
        total_ref[...] += matmul(encoded_ref[:, depth], weight_ref[depth, :])
        return carry

    lax.fori_loop(0, WIDTH // TEXT_DEPTH, body, 0)
    text_ref[...] = total_ref[...].astype(BF16)
    for store in stores:
        store.wait()


def weight_kernel(place_ref, kept_ref, *refs):
    near_refs, far_refs, grad_refs = refs[:3], refs[3:6], refs[6:10]
    kept_sum_ref, sent_refs, totals_ref = refs[10], refs[11:14], refs[14]
    near = pl.ds(pl.multiple_of(place_ref[2] * HALF_PROMPT, HALF_PROMPT), HALF_PROMPT)
    far = pl.ds(pl.multiple_of((1 - place_ref[2]) * HALF_PROMPT, HALF_PROMPT), HALF_PROMPT)

    def body(ahead, carry):
        z_hi = lax.rem(place_ref[3] + ahead, 4)
        at = pl.ds(pl.multiple_of(z_hi * FEATURES, FEATURES), FEATURES)
        total = matmul(grad_refs[0][...], kept_ref[:, at], CONTRACT_FIRST)
        for grad_ref, near_ref, far_ref in zip(grad_refs[1:], near_refs, far_refs):
            total += matmul(grad_ref[near, :], near_ref[:, at], CONTRACT_FIRST)
            total += matmul(grad_ref[far, :], far_ref[:, at], CONTRACT_FIRST)
        totals_ref[ahead] = total
        return carry

    lax.fori_loop(0, 4, body, 0)
    kept_sum_ref[...] = totals_ref[0]
    for step, sent_ref in enumerate(sent_refs):
        sent_ref[...] = totals_ref[step + 1].astype(BF16)


def total_kernel(kept_ref, *refs):
    total = kept_ref[...]
    for part_ref in refs[:3]:
        total += part_ref[...].astype(F32)
    refs[3][...] = total.T


def exp_rows(scores, maximum):
    return jnp.exp2((scores - maximum) * EXPONENT).astype(BF16)


def spread(rows, columns):
    return jnp.concatenate([rows] * (columns // HEAD_DIM), axis=1)


def row_sums(out_grad, output):
    total = jnp.sum(out_grad.astype(F32) * output, axis=-1, keepdims=True)
    return jnp.broadcast_to(total, output.shape)


def score_gradient(weights, prob_grad, row_delta):
    wide = spread(row_delta, weights.shape[1])
    return (weights.astype(F32) * (prob_grad - wide)).astype(BF16)


def chains(count, first, then):
    ahead = first(0)
    for chain in range(count):
        current = ahead
        if chain + 1 < count:
            ahead = first(chain + 1)
        then(chain, current)


def chain_rows(chain):
    return slice(chain * QUERY_BLOCK, (chain + 1) * QUERY_BLOCK)


def image_forward_kernel(
    order_ref,
    packed_ref,
    weights_ref,
    rows_ref,
    output_ref,
    maximum_ref,
    total_ref,
    text_do_ref,
    k_ref,
    v_ref,
):
    step = pl.program_id(0)

    @pl.when(step == 0)
    def _():
        v_ref[:, HEAD_DIM:] = jnp.ones((IMAGE, HEAD_DIM), BF16)
        for src in range(HEADS):
            at = slice(src * SHARE, (src + 1) * SHARE)
            k_ref[at, :] = packed_ref[src, :SHARE, HEAD_DIM : 2 * HEAD_DIM]
            v_ref[at, :HEAD_DIM] = packed_ref[src, :SHARE, 2 * HEAD_DIM : 3 * HEAD_DIM]
        for block in range(TEXT_BLOCKS):
            slot = order_ref[block]
            columns = pl.ds(pl.multiple_of((slot % 2) * HEAD_DIM, HEAD_DIM), HEAD_DIM)
            text_do_ref[block * BLOCK_ROWS : (block + 1) * BLOCK_ROWS, :] = packed_ref[
                slot // 2, SHARE:, columns
            ]

    parts = FORWARD_ROWS // SHARE
    for part in range(parts):
        at = slice(part * SHARE, (part + 1) * SHARE)
        rows_ref[at, :] = packed_ref[step * parts + part, :SHARE, :]

    def first(chain):
        return matmul(rows_ref[chain_rows(chain), :HEAD_DIM], k_ref[...], CONTRACT_LAST)

    def then(chain, scores):
        at = chain_rows(chain)
        maximum = jnp.max(scores, axis=-1, keepdims=True)
        weights = exp_rows(scores, maximum)
        weights_ref[at, :] = weights
        both = matmul(weights, v_ref[...])
        output_ref[at, :] = both[:, :HEAD_DIM]
        total_ref[at, :] = both[:, HEAD_DIM:]
        maximum_ref[at, :] = jnp.broadcast_to(maximum, (QUERY_BLOCK, HEAD_DIM))

    chains(FORWARD_ROWS // QUERY_BLOCK, first, then)


def attention_kernel(
    length_ref,
    order_ref,
    text_ref,
    text_do_ref,
    rows_ref,
    weights_ref,
    output_ref,
    maximum_ref,
    total_ref,
    sent_hbm,
    text_grad_ref,
    sent_ref,
    dkt_ref,
    dvt_ref,
    image_dkt_ref,
    image_dvt_ref,
    tv_ref,
    stored,
):
    step = pl.program_id(0)
    factor = HEAD_DIM**-0.5
    text_keys = text_ref[:, HEAD_DIM : 2 * HEAD_DIM]
    text_values = text_ref[:, 2 * HEAD_DIM :]
    keys = rows_ref[:, HEAD_DIM : 2 * HEAD_DIM]
    values = rows_ref[:, 2 * HEAD_DIM : 3 * HEAD_DIM]
    live = lax.broadcasted_iota(jnp.int32, (1, PROMPT), 1) < length_ref[0]
    sums = (dkt_ref, dvt_ref, image_dkt_ref, image_dvt_ref)

    def text_scores(queries):
        return jnp.where(live, matmul(queries, text_keys, CONTRACT_LAST), -1e30)

    @pl.when(step == 0)
    def _():
        tv_ref[:, :HEAD_DIM] = text_values
        tv_ref[:, HEAD_DIM:] = jnp.ones((PROMPT, HEAD_DIM), BF16)
        sent_ref[:, SHARE:, 2 * HEAD_DIM :] = jnp.zeros((HEADS, BLOCK_ROWS, 2 * HEAD_DIM), BF16)
        for sum_ref in sums:
            sum_ref[...] = jnp.zeros_like(sum_ref)

        def body(chain, carry):
            rows = pl.ds(pl.multiple_of(chain * QUERY_BLOCK, QUERY_BLOCK), QUERY_BLOCK)
            queries = text_ref[rows, :HEAD_DIM]
            to_text = text_scores(queries)
            to_image = matmul(queries, keys, CONTRACT_LAST)
            maximum = jnp.maximum(
                jnp.max(to_text, axis=-1, keepdims=True), jnp.max(to_image, axis=-1, keepdims=True)
            )
            text_weights, image_weights = exp_rows(to_text, maximum), exp_rows(to_image, maximum)
            total = jnp.sum(image_weights.astype(F32), axis=-1, keepdims=True)
            both = matmul(text_weights, tv_ref[...])
            inverse = 1.0 / (both[:, HEAD_DIM:] + total)
            output = (both[:, :HEAD_DIM] + matmul(image_weights, values)) * inverse
            out_grad = (text_do_ref[rows, :].astype(F32) * inverse).astype(BF16)
            row_delta = row_sums(out_grad, output)
            prob_grads = [matmul(out_grad, part, CONTRACT_LAST) for part in (text_values, values)]
            text_scored = score_gradient(text_weights, prob_grads[0], row_delta)
            image_scored = score_gradient(image_weights, prob_grads[1], row_delta)
            query_grad = matmul(text_scored, text_keys) + matmul(image_scored, keys)
            text_grad_ref[rows, :HEAD_DIM] = (query_grad * factor).astype(BF16)
            dkt_ref[...] += matmul(queries, text_scored, CONTRACT_FIRST)
            dvt_ref[...] += matmul(out_grad, text_weights, CONTRACT_FIRST)
            image_dkt_ref[...] += matmul(queries, image_scored, CONTRACT_FIRST)
            image_dvt_ref[...] += matmul(out_grad, image_weights, CONTRACT_FIRST)
            output = output.astype(BF16)
            blocks = QUERY_BLOCK // BLOCK_ROWS
            for block in range(blocks):
                slot = order_ref[chain * blocks + block]
                columns = pl.ds(pl.multiple_of((slot % 2) * HEAD_DIM, HEAD_DIM), HEAD_DIM)
                sent_ref[slot // 2, SHARE:, columns] = output[
                    block * BLOCK_ROWS : (block + 1) * BLOCK_ROWS
                ]
            return carry

        lax.fori_loop(0, PROMPT // QUERY_BLOCK, body, 0)

    @pl.when(step > 0)
    def _():
        def place(chain):
            start = (step - 1) * FORWARD_ROWS + chain * QUERY_BLOCK
            return pl.ds(pl.multiple_of(start, QUERY_BLOCK), QUERY_BLOCK)

        places = [chain_rows(chain) for chain in range(CHAINS)]
        scores = [text_scores(rows_ref[place(chain), :HEAD_DIM]) for chain in range(CHAINS)]
        weights = []
        for at, to_text in zip(places, scores):
            image_maximum = maximum_ref[at, :]
            maximum = jnp.maximum(image_maximum, jnp.max(to_text, axis=-1, keepdims=True))
            scale = jnp.exp2((image_maximum - maximum) * EXPONENT)
            weights.append((exp_rows(to_text, spread(maximum, PROMPT)), scale))
        middle = []
        for chain, (at, (text_weights, scale)) in enumerate(zip(places, weights)):
            both = matmul(text_weights, tv_ref[...])
            inverse = 1.0 / (both[:, HEAD_DIM:] + scale * total_ref[at, :])
            output = (scale * output_ref[at, :] + both[:, :HEAD_DIM]) * inverse
            cotangent = rows_ref[place(chain), 3 * HEAD_DIM :].astype(F32)
            out_grad = (cotangent * inverse).astype(BF16)
            image_out_grad = (cotangent * (scale * inverse)).astype(BF16)
            prob_grad = matmul(out_grad, text_values, CONTRACT_LAST)
            image_prob_grad = matmul(image_out_grad, values, CONTRACT_LAST)
            middle.append(
                (
                    (out_grad, row_sums(out_grad, output), prob_grad),
                    (image_out_grad, row_sums(image_out_grad, output), image_prob_grad),
                )
            )
            output = output.astype(BF16)
            for part in range(QUERY_BLOCK // SHARE):
                dest = ((step - 1) * FORWARD_ROWS + chain * QUERY_BLOCK) // SHARE + part
                sent_ref[dest, :SHARE, :HEAD_DIM] = output[part * SHARE : (part + 1) * SHARE]
        for chain, at in enumerate(places):
            queries = rows_ref[place(chain), :HEAD_DIM]
            (out_grad, row_delta, prob_grad), image_parts = middle[chain]
            image_out_grad, image_delta, image_prob_grad = image_parts
            text_weights, image_weights = weights[chain][0], weights_ref[at, :]
            text_scored = score_gradient(text_weights, prob_grad, row_delta)
            image_scored = score_gradient(image_weights, image_prob_grad, image_delta)
            query_grad = matmul(text_scored, text_keys) + matmul(image_scored, keys)
            query_grad = (query_grad * factor).astype(BF16)
            for part in range(QUERY_BLOCK // SHARE):
                dest = ((step - 1) * FORWARD_ROWS + chain * QUERY_BLOCK) // SHARE + part
                sent_ref[dest, :SHARE, HEAD_DIM : 2 * HEAD_DIM] = query_grad[
                    part * SHARE : (part + 1) * SHARE
                ]
            dkt_ref[...] += matmul(queries, text_scored, CONTRACT_FIRST)
            dvt_ref[...] += matmul(out_grad, text_weights, CONTRACT_FIRST)
            image_dkt_ref[...] += matmul(queries, image_scored, CONTRACT_FIRST)
            image_dvt_ref[...] += matmul(image_out_grad, image_weights, CONTRACT_FIRST)

    @pl.when(step == IMAGE // FORWARD_ROWS)
    def _():
        text_grad_ref[:, HEAD_DIM : 2 * HEAD_DIM] = (dkt_ref[...] * factor).T.astype(BF16)
        text_grad_ref[:, 2 * HEAD_DIM :] = dvt_ref[...].T.astype(BF16)
        stores = []
        for dest in range(HEADS):
            at = slice(dest * SHARE, (dest + 1) * SHARE)
            sent_ref[dest, :SHARE, 2 * HEAD_DIM : 3 * HEAD_DIM] = (
                (image_dkt_ref[:, at] * factor).T.astype(BF16)
            )
            sent_ref[dest, :SHARE, 3 * HEAD_DIM :] = image_dvt_ref[:, at].T.astype(BF16)
            if dest % 4 == 3:
                group = slice(dest - 3, dest + 1)
                store = pltpu.make_async_copy(
                    sent_ref.at[group], sent_hbm.at[group], stored.at[dest // 4]
                )
                store.start()
                stores.append(store)
        for store in stores:
            store.wait()


def grid_call(kernel, steps, in_specs, out_shape, out_specs, scratch, products):
    return pl.pallas_call(
        kernel,
        grid=(steps,),
        out_shape=out_shape,
        in_specs=in_specs,
        out_specs=out_specs,
        scratch_shapes=scratch,
        compiler_params=pltpu.CompilerParams(vmem_limit_bytes=WHOLE_VMEM),
        cost_estimate=pl.CostEstimate(
            flops=60 * products * HEAD_DIM, bytes_accessed=2**29, transcendentals=0
        ),
    )


IN_SMEM = pl.BlockSpec(memory_space=pltpu.SMEM)


def fixed(*shape):
    return pl.BlockSpec(shape, lambda step: (0,) * len(shape))


def per_block(rows, columns, skip=0):
    return pl.BlockSpec((rows, columns), lambda step: (jnp.maximum(step - skip, 0), 0))


def image_forward(order, packed):
    floats = jax.ShapeDtypeStruct((IMAGE, HEAD_DIM), F32)
    block = per_block(FORWARD_ROWS, HEAD_DIM)
    return grid_call(
        image_forward_kernel,
        IMAGE // FORWARD_ROWS,
        [IN_SMEM, fixed(HEADS, PACK_ROWS, PACK_COLS)],
        [rows_of(IMAGE, IMAGE), rows_of(IMAGE, PACK_COLS)] + [floats] * 3
        + [rows_of(PROMPT, HEAD_DIM)],
        [per_block(FORWARD_ROWS, IMAGE), per_block(FORWARD_ROWS, PACK_COLS)] + [block] * 3
        + [fixed(PROMPT, HEAD_DIM)],
        [pltpu.VMEM((IMAGE, HEAD_DIM), BF16), pltpu.VMEM((IMAGE, 2 * HEAD_DIM), BF16)],
        2 * IMAGE * IMAGE,
    )(order, packed)


def attention(length, order, text_rows, text_do, rows, weights, output, maximum, total):
    block = per_block(FORWARD_ROWS, HEAD_DIM, 1)
    text_sum = pltpu.VMEM((HEAD_DIM, PROMPT), F32)
    image_sum = pltpu.VMEM((HEAD_DIM, IMAGE), F32)
    return grid_call(
        attention_kernel,
        1 + IMAGE // FORWARD_ROWS,
        [IN_SMEM, IN_SMEM, fixed(PROMPT, 3 * HEAD_DIM), fixed(PROMPT, HEAD_DIM)]
        + [fixed(IMAGE, PACK_COLS), per_block(FORWARD_ROWS, IMAGE, 1)] + [block] * 3,
        [rows_of(HEADS, PACK_ROWS, PACK_COLS), rows_of(PROMPT, 3 * HEAD_DIM)],
        [pl.BlockSpec(memory_space=pltpu.HBM), fixed(PROMPT, 3 * HEAD_DIM)],
        [pltpu.VMEM((HEADS, PACK_ROWS, PACK_COLS), BF16), text_sum, text_sum, image_sum, image_sum]
        + [pltpu.VMEM((PROMPT, 2 * HEAD_DIM), BF16), pltpu.SemaphoreType.DMA((4,))],
        6 * TOTAL * TOTAL - 2 * IMAGE * IMAGE,
    )(length, order, text_rows, text_do, rows, weights, output, maximum, total)


def shift(rows, axis, step):
    size = 2 if axis in ("z_lo", "core") else 4
    return lax.ppermute(rows, axis, [(i, (i + step) % size) for i in range(size)])


def add(*rows):
    return sum(part.astype(F32) for part in rows)


def encode(place, context, residual, weight, gain, packed, order):
    other_weight = shift(weight, "core", 1)
    other = shift(context, "core", 1)
    packed = lax.all_to_all(packed, SEQ, split_axis=0, concat_axis=0, tiled=True)
    chunks = whole_call(
        partial_kernel,
        [rows_of(TEXT_SHARE, WIDTH)] * 8,
        1,
        4,
        [pltpu.VMEM((8 * TEXT_SHARE, 2 * FEATURES), BF16)],
        2 * 8 * TEXT_SHARE * 2 * FEATURES * WIDTH,
        2**23,
    )(place, context, other, weight, other_weight)
    part = dict(zip(CHIPS, chunks))
    from_across = shift(part[2, 1], "z_lo", 1)
    from_below = shift(part[1, 1], "y", 1)
    from_above = shift(part[3, 1], "y", -1)
    below = shift(part[1, 0], "y", 1)
    above = shift(part[3, 0], "y", -1)
    opposite = add(part[2, 0], from_across).astype(BF16)
    across = add(part[0, 1], from_below, from_above).astype(BF16)
    packed, opposite, across = lax.optimization_barrier((packed, opposite, across))
    forward = image_forward(order, packed)
    opposite = shift(opposite, "y", 2)
    across = shift(across, "z_lo", 1)
    forward, opposite, across = lax.optimization_barrier((forward, opposite, across))
    stream = add(residual, part[0, 0], below, above, opposite, across)
    inv_norm = lax.rsqrt(jnp.mean(stream * stream, axis=-1, keepdims=True) + 1e-06)
    encoded = (stream * inv_norm * gain).astype(BF16)
    held = {(0, 0): encoded}
    held[0, 1] = shift(encoded, "z_lo", 1)
    held[3, 0] = shift(encoded, "y", 1)
    held[1, 0] = shift(encoded, "y", -1)
    held[2, 0] = shift(encoded, "y", 2)
    held[3, 1] = shift(held[0, 1], "y", 1)
    held[1, 1] = shift(held[0, 1], "y", -1)
    held[2, 1] = shift(held[2, 0], "z_lo", 1)
    early = [held[chip] for chip in CHIPS[:5] + CHIPS[6:7]]
    early = lax.optimization_barrier(early)
    held.update(zip(CHIPS[:5] + CHIPS[6:7], early))
    own = [held[chip] for chip in CHIPS]
    return own + [shift(rows, "core", 1) for rows in own], forward


def project(place, blocks, weight):
    columns = weight.shape[1]
    quarter = 4 * FEATURES
    in_vmem = pl.BlockSpec(memory_space=pltpu.VMEM)
    in_hbm = pl.BlockSpec(memory_space=pltpu.HBM)
    return pl.pallas_call(
        text_kernel,
        out_shape=[rows_of(PROMPT, columns), rows_of(PROMPT, quarter)]
        + [rows_of(HALF_PROMPT, quarter)] * 3,
        in_specs=[IN_SMEM] + [in_vmem] * 17,
        out_specs=[in_vmem] + [in_hbm] * 4,
        scratch_shapes=[
            pltpu.VMEM((PROMPT, WIDTH), BF16),
            pltpu.VMEM((PROMPT, columns), F32),
            pltpu.SemaphoreType.DMA((16,)),
        ],
        compiler_params=pltpu.CompilerParams(vmem_limit_bytes=VMEM_LIMIT),
        cost_estimate=pl.CostEstimate(
            flops=2 * PROMPT * WIDTH * columns, bytes_accessed=2**23, transcendentals=0
        ),
    )(place, *blocks, weight)


def weight_sums(place, kept, near, far, grads):
    columns = grads[0].shape[1]
    total = jax.ShapeDtypeStruct((columns, FEATURES), F32)
    kept_sum, *sent = whole_call(
        weight_kernel,
        [total] + [rows_of(columns, FEATURES)] * 3,
        1,
        11,
        [pltpu.VMEM((4, columns, FEATURES), F32)],
        12 * 2 * 4 * PROMPT * 4 * FEATURES * columns,
        2**23,
        WHOLE_VMEM,
    )(place, kept, *near, *far, *grads)
    return [kept_sum] + [shift(rows, "z_hi", step + 1) for step, rows in enumerate(sent)]


def weight_total(kept_sum, *parts):
    shape = jax.ShapeDtypeStruct(kept_sum.shape[::-1], F32)
    return whole_call(total_kernel, shape, 0, 4, [], 0, 2**20)(kept_sum, *parts)


def on_device(
    t5_context,
    t5_resid,
    t5_out_weight,
    t5_gain,
    text_weight,
    prompt_len,
    text_order,
    img_qkv,
    d_img_out,
    d_txt_out,
):
    packed = pack(img_qkv[0], d_img_out[0], d_txt_out[0])
    place = jnp.stack([lax.axis_index(axis) for axis in SEQ + GRP])
    blocks, forward = encode(
        place, t5_context[0], t5_resid[0], t5_out_weight, t5_gain, packed, text_order[0]
    )
    weights, rows, *stats, text_do = forward
    text_rows, kept, *slices = project(place, blocks, text_weight)
    near = [shift(rows, "x", step + 1) for step, rows in enumerate(slices)]
    sent, text_grad = attention(
        prompt_len, text_order[0], text_rows, text_do, rows, weights, *stats
    )
    *near, sent = lax.optimization_barrier((*near, sent))
    grads = [text_grad] + [shift(text_grad, "x", step) for step in (1, 2)] + [None]
    far = [shift(rows, "core", 1) for rows in near]
    last, far = lax.optimization_barrier((text_grad, far))
    grads[3] = shift(last, "x", 3)
    sums = weight_sums(place, kept, near, far, grads)
    received = lax.all_to_all(sent, SEQ, split_axis=0, concat_axis=0, tiled=True)
    outputs = unpack(received)
    sums, outputs = lax.optimization_barrier((sums, outputs))
    image_out, text_out, image_qkv_grad = outputs
    text_weight_grad = weight_total(*sums)
    return (image_out[None], text_out[None], image_qkv_grad[None], text_weight_grad)


def solution(mesh):
    fine = Mesh(mesh.devices.reshape(4, 4, 4, 2, 2), GRP + SEQ)
    in_specs = (
        P(GRP, None, SEQ),
        P(GRP, SEQ, None),
        P(SEQ, None),
        P(),
        P(None, SEQ),
        P(GRP),
        P(GRP, None),
        P(GRP, SEQ, None),
        P(GRP, SEQ, None),
        P(GRP, SEQ, None),
    )
    out_specs = (
        P(GRP, SEQ, None),
        P(GRP, SEQ, None),
        P(GRP, SEQ, None),
        P(GRP, SEQ),
    )
    return jax.shard_map(
        on_device, mesh=fine, in_specs=in_specs, out_specs=out_specs, check_vma=False
    )
```

```python
import jax
import jax.numpy as jnp
from jax import lax
from jax.experimental import pallas as pl
from jax.experimental.pallas import tpu as pltpu
from jax.sharding import Mesh
from jax.sharding import PartitionSpec as P

HEAD_DIM = 128
HEADS = 16
PROMPT = 512
IMAGE = 2048
TOTAL = PROMPT + IMAGE
BLOCK_ROWS = 16
TEXT_BLOCKS = 32
SHARE = IMAGE // HEADS
PACK_ROWS = SHARE + BLOCK_ROWS
PACK_COLS = 4 * HEAD_DIM
QUERY_BLOCK = 256
EXPONENT = HEAD_DIM**-0.5 * 1.4426950408889634
FORWARD_ROWS = 512
PACK_HEADS = 4
CHAINS = 2
WIDTH = 4096
FEATURES = WIDTH // HEADS
TEXT_SHARE = PROMPT // HEADS
HALF_PROMPT = PROMPT // 2
TEXT_DEPTH = 1024
CHIPS = [(ahead, across) for ahead in range(4) for across in range(2)]

BF16 = jnp.bfloat16
F32 = jnp.float32
SEQ = ("y", "z_lo", "core")
GRP = ("z_hi", "x")
CONTRACT_LAST = (((1,), (1,)), ((), ()))
CONTRACT_FIRST = (((0,), (0,)), ((), ()))
VMEM_LIMIT = 48 * 2**20
WHOLE_VMEM = 60 * 2**20


def matmul(a, b, dims=(((1,), (0,)), ((), ()))):
    return lax.dot_general(a, b, dims, preferred_element_type=F32)


def pack_kernel(qkv_hbm, grad_hbm, text_hbm, packed_hbm, *refs):
    qkv_ref, grad_ref, text_ref, packed_ref, loaded, stored = refs
    loads = []
    for source, target in ((grad_hbm, grad_ref), (text_hbm, text_ref)):
        loads.append(pltpu.make_async_copy(source, target, loaded.at[len(loads)]))
    width = 3 * HEAD_DIM * PACK_HEADS
    for group in range(HEADS // PACK_HEADS):
        columns = slice(group * width, (group + 1) * width)
        source, target = qkv_hbm.at[:, columns], qkv_ref.at[:, columns]
        loads.append(pltpu.make_async_copy(source, target, loaded.at[len(loads)]))
    for load in loads:
        load.start()
    loads[0].wait()
    loads[1].wait()
    stores = []
    for group in range(HEADS // PACK_HEADS):
        loads[2 + group].wait()
        heads = slice(group * PACK_HEADS, (group + 1) * PACK_HEADS)
        for head in range(heads.start, heads.stop):
            columns = slice(head * HEAD_DIM, (head + 1) * HEAD_DIM)
            wide = slice(3 * head * HEAD_DIM, 3 * (head + 1) * HEAD_DIM)
            packed_ref[head, :SHARE, : 3 * HEAD_DIM] = qkv_ref[:, wide]
            packed_ref[head, :SHARE, 3 * HEAD_DIM :] = grad_ref[:, columns]
            packed_ref[head, SHARE:, :HEAD_DIM] = text_ref[:BLOCK_ROWS, columns]
            packed_ref[head, SHARE:, HEAD_DIM : 2 * HEAD_DIM] = text_ref[BLOCK_ROWS:, columns]
            packed_ref[head, SHARE:, 2 * HEAD_DIM :] = jnp.zeros(
                (BLOCK_ROWS, 2 * HEAD_DIM), BF16
            )
        store = pltpu.make_async_copy(
            packed_ref.at[heads], packed_hbm.at[heads], stored.at[group]
        )
        store.start()
        stores.append(store)
    for store in stores:
        store.wait()


def unpack_kernel(packed_ref, out_ref, text_ref, qkv_ref):
    for head in range(HEADS):
        columns = slice(head * HEAD_DIM, (head + 1) * HEAD_DIM)
        wide = slice(3 * head * HEAD_DIM, 3 * (head + 1) * HEAD_DIM)
        out_ref[:, columns] = packed_ref[head, :SHARE, :HEAD_DIM]
        qkv_ref[:, wide] = packed_ref[head, :SHARE, HEAD_DIM:]
        text_ref[:BLOCK_ROWS, columns] = packed_ref[head, SHARE:, :HEAD_DIM]
        text_ref[BLOCK_ROWS:, columns] = packed_ref[head, SHARE:, HEAD_DIM : 2 * HEAD_DIM]


def whole_call(kernel, out_shape, smem_inputs, vmem_inputs, scratch, flops, moved, limit=None):
    in_vmem = pl.BlockSpec(memory_space=pltpu.VMEM)
    in_smem = pl.BlockSpec(memory_space=pltpu.SMEM)
    return pl.pallas_call(
        kernel,
        out_shape=out_shape,
        in_specs=[in_smem] * smem_inputs + [in_vmem] * vmem_inputs,
        out_specs=jax.tree.map(lambda _: in_vmem, out_shape),
        scratch_shapes=scratch,
        compiler_params=pltpu.CompilerParams(vmem_limit_bytes=limit or VMEM_LIMIT),
        cost_estimate=pl.CostEstimate(flops=flops, bytes_accessed=moved, transcendentals=0),
    )


def rows_of(*shape):
    return jax.ShapeDtypeStruct(shape, BF16)


def pack(qkv, grad, text):
    anywhere = pl.BlockSpec(memory_space=pltpu.HBM)
    groups = HEADS // PACK_HEADS
    return pl.pallas_call(
        pack_kernel,
        out_shape=rows_of(HEADS, PACK_ROWS, PACK_COLS),
        in_specs=[anywhere] * 3,
        out_specs=anywhere,
        scratch_shapes=[
            pltpu.VMEM(qkv.shape, BF16),
            pltpu.VMEM(grad.shape, BF16),
            pltpu.VMEM(text.shape, BF16),
            pltpu.VMEM((HEADS, PACK_ROWS, PACK_COLS), BF16),
            pltpu.SemaphoreType.DMA((2 + groups,)),
            pltpu.SemaphoreType.DMA((groups,)),
        ],
        compiler_params=pltpu.CompilerParams(vmem_limit_bytes=WHOLE_VMEM),
        cost_estimate=pl.CostEstimate(flops=0, bytes_accessed=2**22, transcendentals=0),
    )(qkv, grad, text)


def unpack(packed):
    shapes = [
        rows_of(SHARE, HEADS * HEAD_DIM),
        rows_of(2 * BLOCK_ROWS, HEADS * HEAD_DIM),
        rows_of(SHARE, HEADS * 3 * HEAD_DIM),
    ]
    return whole_call(unpack_kernel, shapes, 0, 1, [], 0, 2**22)(packed)


def row_block(place_ref, ahead, across, other_core):
    y = lax.rem(place_ref[0] + ahead, 4)
    z = 1 - place_ref[1] if across else place_ref[1]
    core = 1 - place_ref[2] if other_core else place_ref[2]
    return (y * 2 + z) * 2 + core


def partial_kernel(place_ref, own_ref, other_ref, own_weight_ref, other_weight_ref, *refs):
    chunk_refs, rows_ref = refs[:8], refs[8]
    for index, (ahead, across) in enumerate(CHIPS):
        block = row_block(place_ref, ahead, across, False)
        rows = pl.ds(pl.multiple_of(block * TEXT_SHARE, TEXT_SHARE), TEXT_SHARE)
        to = slice(index * TEXT_SHARE, (index + 1) * TEXT_SHARE)
        rows_ref[to, :FEATURES] = own_ref[rows, :]
        rows_ref[to, FEATURES:] = other_ref[rows, :]

    def body(step, carry):
        columns = pl.ds(pl.multiple_of(step * 512, 512), 512)
        sums = matmul(rows_ref[:, :FEATURES], own_weight_ref[:, columns])
        sums += matmul(rows_ref[:, FEATURES:], other_weight_ref[:, columns])
        for index, chunk_ref in enumerate(chunk_refs):
            rows = slice(index * TEXT_SHARE, (index + 1) * TEXT_SHARE)
            chunk_ref[:, columns] = sums[rows].astype(BF16)
        return carry

    lax.fori_loop(0, WIDTH // 512, body, 0)


def text_kernel(place_ref, *refs):
    block_refs, weight_ref, text_ref = refs[:16], refs[16], refs[17]
    kept_hbm, sent_hbms, encoded_ref, total_ref, stored = refs[18], refs[19:22], *refs[22:]
    for index, block_ref in enumerate(block_refs):
        ahead, across = CHIPS[index % 8]
        block = row_block(place_ref, ahead, across, index >= 8)
        rows = pl.ds(pl.multiple_of(block * TEXT_SHARE, TEXT_SHARE), TEXT_SHARE)
        encoded_ref[rows, :] = block_ref[...]
    half = pl.ds(pl.multiple_of(place_ref[2] * HALF_PROMPT, HALF_PROMPT), HALF_PROMPT)
    stores = []
    for ahead in range(4):
        x = lax.rem(place_ref[4] + ahead, 4)
        for z_hi in range(4):
            at = pl.ds(pl.multiple_of((z_hi * 4 + x) * FEATURES, FEATURES), FEATURES)
            to = slice(z_hi * FEATURES, (z_hi + 1) * FEATURES)
            if ahead:
                source, target = encoded_ref.at[half, at], sent_hbms[ahead - 1].at[:, to]
            else:
                source, target = encoded_ref.at[:, at], kept_hbm.at[:, to]
            store = pltpu.make_async_copy(source, target, stored.at[len(stores)])
            store.start()
            stores.append(store)
    total_ref[...] = jnp.zeros_like(total_ref)

    def body(step, carry):
        depth = pl.ds(pl.multiple_of(step * TEXT_DEPTH, TEXT_DEPTH), TEXT_DEPTH)
        total_ref[...] += matmul(encoded_ref[:, depth], weight_ref[depth, :])
        return carry

    lax.fori_loop(0, WIDTH // TEXT_DEPTH, body, 0)
    text_ref[...] = total_ref[...].astype(BF16)
    for store in stores:
        store.wait()


def weight_kernel(place_ref, kept_ref, *refs):
    near_refs, far_refs, grad_refs = refs[:3], refs[3:6], refs[6:10]
    kept_sum_ref, sent_refs, totals_ref = refs[10], refs[11:14], refs[14]
    near = pl.ds(pl.multiple_of(place_ref[2] * HALF_PROMPT, HALF_PROMPT), HALF_PROMPT)
    far = pl.ds(pl.multiple_of((1 - place_ref[2]) * HALF_PROMPT, HALF_PROMPT), HALF_PROMPT)

    def body(ahead, carry):
        z_hi = lax.rem(place_ref[3] + ahead, 4)
        at = pl.ds(pl.multiple_of(z_hi * FEATURES, FEATURES), FEATURES)
        total = matmul(grad_refs[0][...], kept_ref[:, at], CONTRACT_FIRST)
        for grad_ref, near_ref, far_ref in zip(grad_refs[1:], near_refs, far_refs):
            total += matmul(grad_ref[near, :], near_ref[:, at], CONTRACT_FIRST)
            total += matmul(grad_ref[far, :], far_ref[:, at], CONTRACT_FIRST)
        totals_ref[ahead] = total
        return carry

    lax.fori_loop(0, 4, body, 0, unroll=2)
    kept_sum_ref[...] = totals_ref[0]
    for step, sent_ref in enumerate(sent_refs):
        sent_ref[...] = totals_ref[step + 1].astype(BF16)


def total_kernel(kept_ref, *refs):
    total = kept_ref[...]
    for part_ref in refs[:3]:
        total += part_ref[...].astype(F32)
    refs[3][...] = total.T


def exp_rows(scores, maximum):
    return jnp.exp2((scores - maximum) * EXPONENT).astype(BF16)


def spread(rows, columns):
    return jnp.concatenate([rows] * (columns // HEAD_DIM), axis=1)


def row_sums(out_grad, output):
    total = jnp.sum(out_grad.astype(F32) * output, axis=-1, keepdims=True)
    return jnp.broadcast_to(total, output.shape)


def score_gradient(weights, prob_grad, row_delta):
    wide = spread(row_delta, weights.shape[1])
    return (weights.astype(F32) * (prob_grad - wide)).astype(BF16)


def chains(count, first, then):
    ahead = first(0)
    for chain in range(count):
        current = ahead
        if chain + 1 < count:
            ahead = first(chain + 1)
        then(chain, current)


def chain_rows(chain):
    return slice(chain * QUERY_BLOCK, (chain + 1) * QUERY_BLOCK)


def image_forward_kernel(
    order_ref,
    packed_ref,
    weights_ref,
    rows_ref,
    output_ref,
    maximum_ref,
    total_ref,
    text_do_ref,
    k_ref,
    v_ref,
):
    step = pl.program_id(0)

    @pl.when(step == 0)
    def _():
        v_ref[:, HEAD_DIM:] = jnp.ones((IMAGE, HEAD_DIM), BF16)
        for src in range(HEADS):
            at = slice(src * SHARE, (src + 1) * SHARE)
            k_ref[at, :] = packed_ref[src, :SHARE, HEAD_DIM : 2 * HEAD_DIM]
            v_ref[at, :HEAD_DIM] = packed_ref[src, :SHARE, 2 * HEAD_DIM : 3 * HEAD_DIM]
        for block in range(TEXT_BLOCKS):
            slot = order_ref[block]
            columns = pl.ds(pl.multiple_of((slot % 2) * HEAD_DIM, HEAD_DIM), HEAD_DIM)
            text_do_ref[block * BLOCK_ROWS : (block + 1) * BLOCK_ROWS, :] = packed_ref[
                slot // 2, SHARE:, columns
            ]

    parts = FORWARD_ROWS // SHARE
    for part in range(parts):
        at = slice(part * SHARE, (part + 1) * SHARE)
        rows_ref[at, :] = packed_ref[step * parts + part, :SHARE, :]

    def first(chain):
        return matmul(rows_ref[chain_rows(chain), :HEAD_DIM], k_ref[...], CONTRACT_LAST)

    def then(chain, scores):
        at = chain_rows(chain)
        maximum = jnp.max(scores, axis=-1, keepdims=True)
        weights = exp_rows(scores, maximum)
        weights_ref[at, :] = weights
        both = matmul(weights, v_ref[...])
        output_ref[at, :] = both[:, :HEAD_DIM]
        total_ref[at, :] = both[:, HEAD_DIM:]
        maximum_ref[at, :] = jnp.broadcast_to(maximum, (QUERY_BLOCK, HEAD_DIM))

    chains(FORWARD_ROWS // QUERY_BLOCK, first, then)


def attention_kernel(
    length_ref,
    order_ref,
    text_ref,
    text_do_ref,
    rows_ref,
    weights_ref,
    output_ref,
    maximum_ref,
    total_ref,
    sent_hbm,
    text_grad_ref,
    sent_ref,
    dkt_ref,
    dvt_ref,
    image_dkt_ref,
    image_dvt_ref,
    tv_ref,
    stored,
):
    step = pl.program_id(0)
    factor = HEAD_DIM**-0.5
    text_keys = text_ref[:, HEAD_DIM : 2 * HEAD_DIM]
    text_values = text_ref[:, 2 * HEAD_DIM :]
    keys = rows_ref[:, HEAD_DIM : 2 * HEAD_DIM]
    values = rows_ref[:, 2 * HEAD_DIM : 3 * HEAD_DIM]
    live = lax.broadcasted_iota(jnp.int32, (1, PROMPT), 1) < length_ref[0]
    sums = (dkt_ref, dvt_ref, image_dkt_ref, image_dvt_ref)

    def text_scores(queries):
        return jnp.where(live, matmul(queries, text_keys, CONTRACT_LAST), -1e30)

    @pl.when(step == 0)
    def _():
        tv_ref[:, :HEAD_DIM] = text_values
        tv_ref[:, HEAD_DIM:] = jnp.ones((PROMPT, HEAD_DIM), BF16)
        sent_ref[:, SHARE:, 2 * HEAD_DIM :] = jnp.zeros((HEADS, BLOCK_ROWS, 2 * HEAD_DIM), BF16)
        for sum_ref in sums:
            sum_ref[...] = jnp.zeros_like(sum_ref)

        def body(chain, carry):
            rows = pl.ds(pl.multiple_of(chain * QUERY_BLOCK, QUERY_BLOCK), QUERY_BLOCK)
            queries = text_ref[rows, :HEAD_DIM]
            to_text = text_scores(queries)
            to_image = matmul(queries, keys, CONTRACT_LAST)
            maximum = jnp.maximum(
                jnp.max(to_text, axis=-1, keepdims=True), jnp.max(to_image, axis=-1, keepdims=True)
            )
            text_weights, image_weights = exp_rows(to_text, maximum), exp_rows(to_image, maximum)
            total = jnp.sum(image_weights.astype(F32), axis=-1, keepdims=True)
            both = matmul(text_weights, tv_ref[...])
            inverse = 1.0 / (both[:, HEAD_DIM:] + total)
            output = (both[:, :HEAD_DIM] + matmul(image_weights, values)) * inverse
            out_grad = (text_do_ref[rows, :].astype(F32) * inverse).astype(BF16)
            row_delta = row_sums(out_grad, output)
            prob_grads = [matmul(out_grad, part, CONTRACT_LAST) for part in (text_values, values)]
            text_scored = score_gradient(text_weights, prob_grads[0], row_delta)
            image_scored = score_gradient(image_weights, prob_grads[1], row_delta)
            query_grad = matmul(text_scored, text_keys) + matmul(image_scored, keys)
            text_grad_ref[rows, :HEAD_DIM] = (query_grad * factor).astype(BF16)
            dkt_ref[...] += matmul(queries, text_scored, CONTRACT_FIRST)
            dvt_ref[...] += matmul(out_grad, text_weights, CONTRACT_FIRST)
            image_dkt_ref[...] += matmul(queries, image_scored, CONTRACT_FIRST)
            image_dvt_ref[...] += matmul(out_grad, image_weights, CONTRACT_FIRST)
            output = output.astype(BF16)
            blocks = QUERY_BLOCK // BLOCK_ROWS
            for block in range(blocks):
                slot = order_ref[chain * blocks + block]
                columns = pl.ds(pl.multiple_of((slot % 2) * HEAD_DIM, HEAD_DIM), HEAD_DIM)
                sent_ref[slot // 2, SHARE:, columns] = output[
                    block * BLOCK_ROWS : (block + 1) * BLOCK_ROWS
                ]
            return carry

        lax.fori_loop(0, PROMPT // QUERY_BLOCK, body, 0)

    @pl.when(step > 0)
    def _():
        def place(chain):
            start = (step - 1) * FORWARD_ROWS + chain * QUERY_BLOCK
            return pl.ds(pl.multiple_of(start, QUERY_BLOCK), QUERY_BLOCK)

        places = [chain_rows(chain) for chain in range(CHAINS)]
        scores = [text_scores(rows_ref[place(chain), :HEAD_DIM]) for chain in range(CHAINS)]
        weights = []
        for at, to_text in zip(places, scores):
            image_maximum = maximum_ref[at, :]
            maximum = jnp.maximum(image_maximum, jnp.max(to_text, axis=-1, keepdims=True))
            scale = jnp.exp2((image_maximum - maximum) * EXPONENT)
            weights.append((exp_rows(to_text, spread(maximum, PROMPT)), scale))
        middle = []
        for chain, (at, (text_weights, scale)) in enumerate(zip(places, weights)):
            both = matmul(text_weights, tv_ref[...])
            inverse = 1.0 / (both[:, HEAD_DIM:] + scale * total_ref[at, :])
            output = (scale * output_ref[at, :] + both[:, :HEAD_DIM]) * inverse
            cotangent = rows_ref[place(chain), 3 * HEAD_DIM :].astype(F32)
            out_grad = (cotangent * inverse).astype(BF16)
            image_out_grad = (cotangent * (scale * inverse)).astype(BF16)
            prob_grad = matmul(out_grad, text_values, CONTRACT_LAST)
            image_prob_grad = matmul(image_out_grad, values, CONTRACT_LAST)
            middle.append(
                (
                    (out_grad, row_sums(out_grad, output), prob_grad),
                    (image_out_grad, row_sums(image_out_grad, output), image_prob_grad),
                )
            )
            output = output.astype(BF16)
            for part in range(QUERY_BLOCK // SHARE):
                dest = ((step - 1) * FORWARD_ROWS + chain * QUERY_BLOCK) // SHARE + part
                sent_ref[dest, :SHARE, :HEAD_DIM] = output[part * SHARE : (part + 1) * SHARE]
        for chain, at in enumerate(places):
            queries = rows_ref[place(chain), :HEAD_DIM]
            (out_grad, row_delta, prob_grad), image_parts = middle[chain]
            image_out_grad, image_delta, image_prob_grad = image_parts
            text_weights, image_weights = weights[chain][0], weights_ref[at, :]
            text_scored = score_gradient(text_weights, prob_grad, row_delta)
            image_scored = score_gradient(image_weights, image_prob_grad, image_delta)
            query_grad = matmul(text_scored, text_keys) + matmul(image_scored, keys)
            query_grad = (query_grad * factor).astype(BF16)
            for part in range(QUERY_BLOCK // SHARE):
                dest = ((step - 1) * FORWARD_ROWS + chain * QUERY_BLOCK) // SHARE + part
                sent_ref[dest, :SHARE, HEAD_DIM : 2 * HEAD_DIM] = query_grad[
                    part * SHARE : (part + 1) * SHARE
                ]
            dkt_ref[...] += matmul(queries, text_scored, CONTRACT_FIRST)
            dvt_ref[...] += matmul(out_grad, text_weights, CONTRACT_FIRST)
            image_dkt_ref[...] += matmul(queries, image_scored, CONTRACT_FIRST)
            image_dvt_ref[...] += matmul(image_out_grad, image_weights, CONTRACT_FIRST)

    @pl.when(step == IMAGE // FORWARD_ROWS)
    def _():
        text_grad_ref[:, HEAD_DIM : 2 * HEAD_DIM] = (dkt_ref[...] * factor).T.astype(BF16)
        text_grad_ref[:, 2 * HEAD_DIM :] = dvt_ref[...].T.astype(BF16)
        stores = []
        for dest in range(HEADS):
            at = slice(dest * SHARE, (dest + 1) * SHARE)
            sent_ref[dest, :SHARE, 2 * HEAD_DIM : 3 * HEAD_DIM] = (
                (image_dkt_ref[:, at] * factor).T.astype(BF16)
            )
            sent_ref[dest, :SHARE, 3 * HEAD_DIM :] = image_dvt_ref[:, at].T.astype(BF16)
            if dest % 4 == 3:
                group = slice(dest - 3, dest + 1)
                store = pltpu.make_async_copy(
                    sent_ref.at[group], sent_hbm.at[group], stored.at[dest // 4]
                )
                store.start()
                stores.append(store)
        for store in stores:
            store.wait()


def grid_call(kernel, steps, in_specs, out_shape, out_specs, scratch, products):
    return pl.pallas_call(
        kernel,
        grid=(steps,),
        out_shape=out_shape,
        in_specs=in_specs,
        out_specs=out_specs,
        scratch_shapes=scratch,
        compiler_params=pltpu.CompilerParams(vmem_limit_bytes=WHOLE_VMEM),
        cost_estimate=pl.CostEstimate(
            flops=60 * products * HEAD_DIM, bytes_accessed=2**29, transcendentals=0
        ),
    )


IN_SMEM = pl.BlockSpec(memory_space=pltpu.SMEM)


def fixed(*shape):
    return pl.BlockSpec(shape, lambda step: (0,) * len(shape))


def per_block(rows, columns, skip=0):
    return pl.BlockSpec((rows, columns), lambda step: (jnp.maximum(step - skip, 0), 0))


def image_forward(order, packed):
    floats = jax.ShapeDtypeStruct((IMAGE, HEAD_DIM), F32)
    block = per_block(FORWARD_ROWS, HEAD_DIM)
    return grid_call(
        image_forward_kernel,
        IMAGE // FORWARD_ROWS,
        [IN_SMEM, fixed(HEADS, PACK_ROWS, PACK_COLS)],
        [rows_of(IMAGE, IMAGE), rows_of(IMAGE, PACK_COLS)] + [floats] * 3
        + [rows_of(PROMPT, HEAD_DIM)],
        [per_block(FORWARD_ROWS, IMAGE), per_block(FORWARD_ROWS, PACK_COLS)] + [block] * 3
        + [fixed(PROMPT, HEAD_DIM)],
        [pltpu.VMEM((IMAGE, HEAD_DIM), BF16), pltpu.VMEM((IMAGE, 2 * HEAD_DIM), BF16)],
        2 * IMAGE * IMAGE,
    )(order, packed)


def attention(length, order, text_rows, text_do, rows, weights, output, maximum, total):
    block = per_block(FORWARD_ROWS, HEAD_DIM, 1)
    text_sum = pltpu.VMEM((HEAD_DIM, PROMPT), F32)
    image_sum = pltpu.VMEM((HEAD_DIM, IMAGE), F32)
    return grid_call(
        attention_kernel,
        1 + IMAGE // FORWARD_ROWS,
        [IN_SMEM, IN_SMEM, fixed(PROMPT, 3 * HEAD_DIM), fixed(PROMPT, HEAD_DIM)]
        + [fixed(IMAGE, PACK_COLS), per_block(FORWARD_ROWS, IMAGE, 1)] + [block] * 3,
        [rows_of(HEADS, PACK_ROWS, PACK_COLS), rows_of(PROMPT, 3 * HEAD_DIM)],
        [pl.BlockSpec(memory_space=pltpu.HBM), fixed(PROMPT, 3 * HEAD_DIM)],
        [pltpu.VMEM((HEADS, PACK_ROWS, PACK_COLS), BF16), text_sum, text_sum, image_sum, image_sum]
        + [pltpu.VMEM((PROMPT, 2 * HEAD_DIM), BF16), pltpu.SemaphoreType.DMA((4,))],
        6 * TOTAL * TOTAL - 2 * IMAGE * IMAGE,
    )(length, order, text_rows, text_do, rows, weights, output, maximum, total)


def shift(rows, axis, step):
    size = 2 if axis in ("z_lo", "core") else 4
    return lax.ppermute(rows, axis, [(i, (i + step) % size) for i in range(size)])


def add(*rows):
    return sum(part.astype(F32) for part in rows)


def encode(place, context, residual, weight, gain, packed, order):
    other_weight = shift(weight, "core", 1)
    other = shift(context, "core", 1)
    packed = lax.all_to_all(packed, SEQ, split_axis=0, concat_axis=0, tiled=True)
    chunks = whole_call(
        partial_kernel,
        [rows_of(TEXT_SHARE, WIDTH)] * 8,
        1,
        4,
        [pltpu.VMEM((8 * TEXT_SHARE, 2 * FEATURES), BF16)],
        2 * 8 * TEXT_SHARE * 2 * FEATURES * WIDTH,
        2**23,
    )(place, context, other, weight, other_weight)
    part = dict(zip(CHIPS, chunks))
    from_across = shift(part[2, 1], "z_lo", 1)
    from_below = shift(part[1, 1], "y", 1)
    from_above = shift(part[3, 1], "y", -1)
    below = shift(part[1, 0], "y", 1)
    above = shift(part[3, 0], "y", -1)
    opposite = add(part[2, 0], from_across).astype(BF16)
    across = add(part[0, 1], from_below, from_above).astype(BF16)
    packed, opposite, across = lax.optimization_barrier((packed, opposite, across))
    forward = image_forward(order, packed)
    opposite = shift(opposite, "y", 2)
    across = shift(across, "z_lo", 1)
    forward, opposite, across = lax.optimization_barrier((forward, opposite, across))
    stream = add(residual, part[0, 0], below, above, opposite, across)
    inv_norm = lax.rsqrt(jnp.mean(stream * stream, axis=-1, keepdims=True) + 1e-06)
    encoded = (stream * inv_norm * gain).astype(BF16)
    held = {(0, 0): encoded}
    held[0, 1] = shift(encoded, "z_lo", 1)
    held[3, 0] = shift(encoded, "y", 1)
    held[1, 0] = shift(encoded, "y", -1)
    held[2, 0] = shift(encoded, "y", 2)
    held[3, 1] = shift(held[0, 1], "y", 1)
    held[1, 1] = shift(held[0, 1], "y", -1)
    held[2, 1] = shift(held[2, 0], "z_lo", 1)
    early = [held[chip] for chip in CHIPS[:5] + CHIPS[6:7]]
    early = lax.optimization_barrier(early)
    held.update(zip(CHIPS[:5] + CHIPS[6:7], early))
    own = [held[chip] for chip in CHIPS]
    return own + [shift(rows, "core", 1) for rows in own], forward


def project(place, blocks, weight):
    columns = weight.shape[1]
    quarter = 4 * FEATURES
    in_vmem = pl.BlockSpec(memory_space=pltpu.VMEM)
    in_hbm = pl.BlockSpec(memory_space=pltpu.HBM)
    return pl.pallas_call(
        text_kernel,
        out_shape=[rows_of(PROMPT, columns), rows_of(PROMPT, quarter)]
        + [rows_of(HALF_PROMPT, quarter)] * 3,
        in_specs=[IN_SMEM] + [in_vmem] * 17,
        out_specs=[in_vmem] + [in_hbm] * 4,
        scratch_shapes=[
            pltpu.VMEM((PROMPT, WIDTH), BF16),
            pltpu.VMEM((PROMPT, columns), F32),
            pltpu.SemaphoreType.DMA((16,)),
        ],
        compiler_params=pltpu.CompilerParams(vmem_limit_bytes=VMEM_LIMIT),
        cost_estimate=pl.CostEstimate(
            flops=2 * PROMPT * WIDTH * columns, bytes_accessed=2**23, transcendentals=0
        ),
    )(place, *blocks, weight)


def weight_sums(place, kept, near, far, grads):
    columns = grads[0].shape[1]
    total = jax.ShapeDtypeStruct((columns, FEATURES), F32)
    kept_sum, *sent = whole_call(
        weight_kernel,
        [total] + [rows_of(columns, FEATURES)] * 3,
        1,
        11,
        [pltpu.VMEM((4, columns, FEATURES), F32)],
        12 * 2 * 4 * PROMPT * 4 * FEATURES * columns,
        2**23,
        WHOLE_VMEM,
    )(place, kept, *near, *far, *grads)
    return [kept_sum] + [shift(rows, "z_hi", step + 1) for step, rows in enumerate(sent)]


def weight_total(kept_sum, *parts):
    shape = jax.ShapeDtypeStruct(kept_sum.shape[::-1], F32)
    return whole_call(total_kernel, shape, 0, 4, [], 0, 2**20)(kept_sum, *parts)


def on_device(
    t5_context,
    t5_resid,
    t5_out_weight,
    t5_gain,
    text_weight,
    prompt_len,
    text_order,
    img_qkv,
    d_img_out,
    d_txt_out,
):
    packed = pack(img_qkv[0], d_img_out[0], d_txt_out[0])
    place = jnp.stack([lax.axis_index(axis) for axis in SEQ + GRP])
    blocks, forward = encode(
        place, t5_context[0], t5_resid[0], t5_out_weight, t5_gain, packed, text_order[0]
    )
    weights, rows, *stats, text_do = forward
    text_rows, kept, *slices = project(place, blocks, text_weight)
    near = [shift(rows, "x", step + 1) for step, rows in enumerate(slices)]
    sent, text_grad = attention(
        prompt_len, text_order[0], text_rows, text_do, rows, weights, *stats
    )
    *near, sent = lax.optimization_barrier((*near, sent))
    grads = [text_grad] + [shift(text_grad, "x", step) for step in (1, 2)] + [None]
    far = [shift(rows, "core", 1) for rows in near]
    last, far = lax.optimization_barrier((text_grad, far))
    grads[3] = shift(last, "x", 3)
    sums = weight_sums(place, kept, near, far, grads)
    received = lax.all_to_all(sent, SEQ, split_axis=0, concat_axis=0, tiled=True)
    outputs = unpack(received)
    sums, outputs = lax.optimization_barrier((sums, outputs))
    image_out, text_out, image_qkv_grad = outputs
    text_weight_grad = weight_total(*sums)
    return (image_out[None], text_out[None], image_qkv_grad[None], text_weight_grad)


def solution(mesh):
    fine = Mesh(mesh.devices.reshape(4, 4, 4, 2, 2), GRP + SEQ)
    in_specs = (
        P(GRP, None, SEQ),
        P(GRP, SEQ, None),
        P(SEQ, None),
        P(),
        P(None, SEQ),
        P(GRP),
        P(GRP, None),
        P(GRP, SEQ, None),
        P(GRP, SEQ, None),
        P(GRP, SEQ, None),
    )
    out_specs = (
        P(GRP, SEQ, None),
        P(GRP, SEQ, None),
        P(GRP, SEQ, None),
        P(GRP, SEQ),
    )
    return jax.shard_map(
        on_device, mesh=fine, in_specs=in_specs, out_specs=out_specs, check_vma=False
    )
```
